32 devices in a mesh: groups: 2 (over x), tp: 8 (over z, y), rep: 2 (over core).
Axes of the slice: x: 2, y: 2, z: 4, core: 2. Of those that a mesh axis runs over, the one named last changes fastest.
Arguments:
- queries: bfloat16 [512, 8192], P(('groups', 'rep'), 'tp'), parts along dimension 0
- key_cache: bfloat16 [8, 512, 32, 128], P('tp', ('groups', 'rep')), parts along dimension 1, as said below
- value_cache: bfloat16 [8, 512, 32, 128], P('tp', ('groups', 'rep')), parts along dimension 1, as said below
- new_keys: bfloat16 [8, 512, 128], P('tp', ('groups', 'rep')), parts along dimension 1, as said below
- new_values: bfloat16 [8, 512, 128], P('tp', ('groups', 'rep')), parts along dimension 1, as said below
- lengths: int32 [512], P(('groups', 'rep')), parts along dimension 0, may hold values from 2 to 32, as said below
- request_variant: int32 [512], P(('groups', 'rep')), parts along dimension 0, may hold values from 0 to 31
- holder_slot: int32 [32], replicated, may hold values from 0 to 31, each once
- out_weight: bfloat16 [8192, 8192], P('tp'), may hold values from -0.375 to 0.375
- factor_in: bfloat16 [32, 8192, 64], P('tp'), may hold values from -0.25 to 0.25
- second_factor: bfloat16 [32, 64, 8192], P('tp'), may hold values from -0.75 to 0.75
- block_values: bfloat16 [32, 16, 128, 128], P('tp'), may hold values from -0.5 to 0.5
- block_scale: float32 [32, 16], P('tp'), may hold values from 1 to 16
- block_owner: int32 [32, 16, 1], P('tp'), may hold values from 0 to 7; in each aligned block of 16 rows (0 to 15, 16 to 31, ..., all dimensions but the last counted through in order) at most 2 rows name the same one
- block_cell: int32 [32, 16], P('tp'), may hold values from 0 to 511
Outputs:
- mixed: bfloat16 [512, 8192], P(('groups', 'rep'), 'tp'), parts along dimension 0
The draws below stay inside these ranges and needn't reach their ends.
There are 2 independent parts, one for each index of `groups`. The reference program is written for one: setup_inputs(seed, part) draws one part's arguments, and reference() takes and returns one part's arrays. A program takes and returns all parts, laid end to end along the dimension named above; an argument that names none is the same for every part. Nothing has to cross between parts.
Inputs may be any that keep to these rules, and one draw needn't show every extreme that they name: `lengths`: within the rows of each rep index some row has 32 live positions. `block_owner`: in each slot at most 2 blocks lie on one tensor shard's rows; some slot reaches 2. `key_cache`: entries s and s' along the first dimension are equal when floor(s * 8 / number of tensor shards) equals floor(s' * 8 / number of tensor shards). `value_cache`: equal along the first dimension within a key-value head, as key_cache. `new_keys`: equal along the first dimension within a key-value head, as key_cache. `new_values`: equal along the first dimension within a key-value head, as key_cache.
All inputs are finite; a program needn't handle non-finite values.
Results may differ from the reference program's by a relative error of at most 0.015.
Values may be sent and summed in bfloat16 or wider, within the bound.
No kernel may reach another device: no remote copies, remote signals or barrier semaphores. Data moves between devices by JAX's collectives and lax.ppermute only.
A program may use at most 128 MiB of HBM per device.

```python
import math
import jax
import jax.numpy as jnp
import numpy as np
from jax import lax

D = 8192
HEADS = 64
KV = 8
HD = 128
RANK = 64
VARIANTS = 32
BS = 128
NBLK = 16
CAP = 2
ROWS_DEV = 128
CACHE = 32
ROWS = 256
N_TP = 8


def spread_heads(values):
    return jnp.repeat(values, N_TP // KV, axis=0)


def lead_keys(key):
    return jnp.clip(jax.random.normal(jax.random.fold_in(key, 11), (KV, ROWS, 1, HD), jnp.float32), -6.0, 6.0)


def draw_key_cache(key, part):
    lead_key = lead_keys(key)
    key = jax.random.fold_in(key, 3)
    tail_keys = jnp.clip(jax.random.normal(key, (KV, ROWS, CACHE - 1, HD), jnp.float32), -6.0, 6.0)
    return spread_heads(jnp.concatenate([lead_key, tail_keys], axis=2)).astype(jnp.bfloat16)


def draw_value_cache(key, part):
    key = jax.random.fold_in(key, 13)
    drawn = jnp.clip(jax.random.normal(key, (KV, ROWS, CACHE, HD), jnp.float32), -6.0, 6.0)
    return spread_heads(drawn).astype(jnp.bfloat16)


def draw_new_keys(key, part):
    key = jax.random.fold_in(key, 17)
    drawn = jnp.clip(jax.random.normal(key, (KV, ROWS, HD), jnp.float32), -6.0, 6.0)
    return spread_heads(drawn).astype(jnp.bfloat16)


def draw_new_values(key, part):
    key = jax.random.fold_in(key, 19)
    drawn = jnp.clip(jax.random.normal(key, (KV, ROWS, HD), jnp.float32), -6.0, 6.0)
    return spread_heads(drawn).astype(jnp.bfloat16)


def draw_queries(key, part):
    key = jax.random.fold_in(key, 5)
    drawn_queries = jnp.clip(jax.random.normal(key, (ROWS, HEADS, HD), jnp.float32), -6.0, 6.0)
    return drawn_queries.reshape(ROWS, HEADS * HD).astype(jnp.bfloat16)


def draw_lengths(key, part):
    key = jax.random.fold_in(key, 7)
    drawn_len = jax.random.randint(key, (ROWS,), 2, CACHE + 1)
    full_spot = jax.random.randint(jax.random.fold_in(key, 1), (ROWS // ROWS_DEV,), 0, ROWS_DEV)
    row_ids = jnp.arange(ROWS)
    target = row_ids // ROWS_DEV * ROWS_DEV + full_spot[row_ids // ROWS_DEV]
    return jnp.where(row_ids == target, CACHE, drawn_len).astype(jnp.int32)


def touch_ends(array, own_key, low, largest):
    longest = array.shape.index(max(array.shape))
    spots = []
    for shift in (0, 1):
        where = [jax.random.randint(jax.random.fold_in(own_key, axis), (), 0, length) for axis, length in enumerate(array.shape)]
        where[longest] = (where[longest] + shift) % array.shape[longest]
        spots.append(tuple(where))
    return array.at[spots[0]].set(low).at[spots[1]].set(largest)


def raised(result, key, source, target, parts, factor):
    owner, partner = [(jnp.arange(result.shape[axis_at]) // (result.shape[axis_at] // parts)).reshape([-1 if axis == axis_at else 1 for axis in range(result.ndim)]) for axis_at in (source, target)]
    chosen = jax.random.permutation(key, parts)[partner]
    strong = (owner == chosen) | (owner == (partner + parts // 2) % parts)
    return jnp.where(strong, factor * result, result)


def steps_of(stream_key, extent, cuts, smallest, high):
    def one(position, shards_of):
        draws = jax.random.uniform(jax.random.fold_in(jax.random.fold_in(stream_key, 6), position), (shards_of,), jnp.float32, smallest / len(cuts), high / len(cuts))
        return jnp.repeat(jnp.exp(draws), extent[position] // shards_of).reshape((-1,) + (1,) * (len(extent) - position - 1))

    level = one(*cuts[0])
    for cut in cuts[1:]:
        level = level * one(*cut)
    return level


def rank_bounds(count, skew):
    loads = [(1 << 20) // math.isqrt(rank ** skew) + 1 for rank in range(1, count + 1)]
    width = 1 + sum(loads) // (1 << 30)
    return np.cumsum(np.array([max(1, weight // width) for weight in loads]))


def skewed_ids(key, dims, count, skew):
    listing = rank_bounds(count, skew)
    pick = jax.random.randint(jax.random.fold_in(key, 1), dims, 0, int(listing[count - 1]))
    rank = jnp.searchsorted(jnp.asarray(listing, jnp.int32), pick, side="right")
    return jax.random.permutation(jax.random.fold_in(key, 2), count)[rank].astype(jnp.int32)


def assign_block(key, own, number, rows, amount, top, limit, skew):
    order = jax.random.permutation(key, amount)
    crowded, common = load_shares(amount, rows * top, limit, skew, True), load_shares(amount, rows * top, limit, skew, False)
    places = jnp.arange(amount)

    def named(sizes, rotation):
        used = int((sizes > 0).sum())
        fixed = max(1, used // 4)
        moved = fixed + (places - fixed + rotation * (used - fixed)) % max(1, amount - fixed)
        return jnp.zeros((amount,), jnp.int32).at[order[jnp.where(places < fixed, places, moved)]].set(jnp.asarray(sizes, jnp.int32))

    sizes = jnp.where(number % 4 == 0, named(crowded, number // 4), named(common, number - number // 4 - 1))
    mixed = jax.random.permutation(jax.random.fold_in(own, 3), amount)
    donor, receiver = mixed[0:amount // 2 * 2:2], mixed[1:amount // 2 * 2:2]
    slack = jnp.minimum(sizes[donor] - 1, limit - sizes[receiver]) // 2
    slack = jnp.where((donor == order[0]) | (receiver == order[0]) | (sizes[receiver] == 0), 0, jnp.maximum(slack, 0))
    moved = jax.random.randint(jax.random.fold_in(own, 4), (amount // 2,), 0, 1 << 20) % (slack + 1)
    sizes = sizes.at[donor].add(-moved).at[receiver].add(moved)
    labels = jnp.searchsorted(jnp.cumsum(sizes), jnp.arange(rows * top), side="right").astype(jnp.int32)
    table = labels.reshape(top, rows).T
    table = table[jax.random.permutation(jax.random.fold_in(own, 1), rows)]
    rotation = jax.random.randint(jax.random.fold_in(own, 2), (rows, 1), 0, top)
    return jnp.take_along_axis(table, (jnp.arange(top)[None, :] + rotation) % top, axis=1)


def load_shares(amount, total, limit, skew, full):
    portions = [(1 << 20) // math.isqrt(standing ** skew) + 1 for standing in range(1, amount + 1)]
    largest = limit if full else min(limit, max(-(-total // amount), total * portions[0] // sum(portions)))
    least = 1 if total - largest >= amount - 1 else 0
    holding, spare = [largest] + [least] * (amount - 1), total - largest - least * (amount - 1)
    while spare > 0:
        free = [i for i in range(1, amount) if holding[i] < largest] or [i for i in range(1, amount) if holding[i] < limit]
        mass, left = sum([portions[i] for i in free]), spare
        for i in free:
            addition = min(limit - holding[i], max(1, left * portions[i] // mass), spare)
            holding[i] = holding[i] + addition
            spare = spare - addition
    return np.array(holding)


def scatter_about(rng, shape, width, reach, split=(), kind=jnp.bfloat16):
    level = steps_of(rng, shape, split, -0.22, 0.18) if split else 1.0
    values = jax.random.normal(rng, shape, jnp.float32) * width * level
    return jnp.minimum(jnp.maximum(values, -reach), reach).astype(kind)


def bell_draw_with(key, shape, width, bound, cuts, heavy, kind=jnp.bfloat16):
    values = width * jax.random.normal(key, shape, jnp.float32)
    if cuts:
        values = values * steps_of(key, shape, cuts, -0.22, 0.18)
    return jnp.clip(raised(values, jax.random.fold_in(key, 3), *heavy), -bound, bound).astype(kind)


def setup_inputs(seed: int = 0, part: int = 0) -> dict:
    keys = jax.random.split(jax.random.key(seed), 16)
    part_splits = jax.random.split(jax.random.fold_in(keys[15], part), 16)
    queries = draw_queries(jax.random.fold_in(jax.random.fold_in(keys[15], part), 71), part)
    key_cache = draw_key_cache(jax.random.fold_in(jax.random.fold_in(keys[15], part), 71), part)
    value_cache = draw_value_cache(jax.random.fold_in(jax.random.fold_in(keys[15], part), 71), part)
    new_keys = draw_new_keys(jax.random.fold_in(jax.random.fold_in(keys[15], part), 71), part)
    new_values = draw_new_values(jax.random.fold_in(jax.random.fold_in(keys[15], part), 71), part)
    lengths = draw_lengths(jax.random.fold_in(jax.random.fold_in(keys[15], part), 71), part)
    request_variant = touch_ends(skewed_ids(part_splits[6], (ROWS,), VARIANTS, 2), jax.random.fold_in(part_splits[6], 3), 0, VARIANTS - 1).astype(jnp.int32)
    holder_slot = jax.random.permutation(keys[7], VARIANTS).astype(jnp.int32)
    out_weight = bell_draw_with(keys[8], (D, D), (D // 16) ** -0.5, 0.375, ((0, 8),), (0, 1, 8, 2.0))
    factor_in = scatter_about(keys[9], (VARIANTS, D, RANK), (D // 16) ** -0.5, 0.25, ((0, 8),))
    second_factor = scatter_about(keys[10], (VARIANTS, RANK, D), RANK ** -0.5, 0.75, ((0, 8),))
    block_values = scatter_about(keys[11], (VARIANTS, NBLK, BS, BS), BS ** -0.5, 0.5, ((0, 8),))
    block_scale = jnp.clip(jnp.exp(math.log(16.0) - 2.7725887 * jax.random.uniform(keys[12], (VARIANTS, NBLK), jnp.float32) ** steps_of(keys[12], (VARIANTS, NBLK), ((0, 8),), -0.2, 0.2)), 1.0, 16.0)
    block_owner_keys = jax.random.split(jax.random.fold_in(keys[13], 1), VARIANTS * NBLK // NBLK)
    block_owner_turns = jax.random.permutation(jax.random.fold_in(keys[13], 3), VARIANTS * NBLK // NBLK)
    block_owner = jax.vmap(lambda own, number: assign_block(jax.random.fold_in(keys[13], 2), own, number, NBLK, N_TP, 1, CAP, 2))(block_owner_keys, block_owner_turns).reshape((VARIANTS, NBLK, 1))
    block_cell = touch_ends(jax.random.randint(keys[14], (VARIANTS, NBLK), 0, (D // (N_TP * BS)) * (D // BS)), jax.random.fold_in(keys[14], 1), 0, ((D // (N_TP * BS)) * (D // BS)) - 1).astype(jnp.int32)
    return {"queries": queries, "key_cache": key_cache, "value_cache": value_cache, "new_keys": new_keys, "new_values": new_values, "lengths": lengths, "request_variant": request_variant, "holder_slot": holder_slot, "out_weight": out_weight, "factor_in": factor_in, "second_factor": second_factor, "block_values": block_values, "block_scale": block_scale, "block_owner": block_owner, "block_cell": block_cell}


def attend(queries, key_cache, value_cache, new_keys, new_values, lengths):
    shards, row_count, cache_len, head_dim = key_cache.shape
    query_heads = queries.astype(jnp.float32).reshape(row_count, shards, -1, head_dim)
    inv_scale = 1.0 / math.sqrt(head_dim)
    scores = jnp.einsum('rshd,srpd->rshp', query_heads, key_cache.astype(jnp.float32)) * inv_scale
    fresh_score = jnp.einsum('rshd,srd->rsh', query_heads, new_keys.astype(jnp.float32)) * inv_scale
    in_cache = (jnp.arange(cache_len, dtype=jnp.int32)[None, :] < lengths[:, None])[:, None, None, :]
    masked = jnp.where(in_cache, scores, -1e+30)
    top_score = jnp.maximum(lax.optimization_barrier(jnp.max(masked, axis=-1)), fresh_score)
    raw_weights = jnp.where(in_cache, jnp.exp(masked - top_score[..., None]), 0.0)
    fresh_raw = jnp.exp(fresh_score - top_score)
    denominator = lax.optimization_barrier(jnp.sum(raw_weights, axis=-1)) + fresh_raw
    weights = (raw_weights / denominator[..., None]).astype(jnp.bfloat16)
    fresh_weight = (fresh_raw / denominator).astype(jnp.bfloat16)
    fresh_values = jnp.transpose(new_values.astype(jnp.float32), (1, 0, 2))[:, :, None, :]
    attended_f = jnp.einsum('rshp,srpd->rshd', weights.astype(jnp.float32), value_cache.astype(jnp.float32))
    attended_f = attended_f + fresh_weight.astype(jnp.float32)[..., None] * fresh_values
    return attended_f.astype(jnp.bfloat16).reshape(row_count, -1)

def apply_blocks(features, slot_row, slot_of, row_block, col_block, rebuilt, complete_width):
    row_count = features.shape[0]
    block_size = rebuilt.shape[1]
    feature_tiles = features.reshape(row_count, -1, block_size)
    picked = jnp.take(feature_tiles, row_block, axis=1)
    row_match = slot_row[:, None] == slot_of[None, :]
    picked = jnp.where(row_match[:, :, None], picked, jnp.zeros((), features.dtype))
    contrib = jnp.einsum('reb,ebc->rec', picked.astype(jnp.float32), rebuilt.astype(jnp.float32))
    placed = jnp.zeros((row_count, complete_width // block_size, block_size), jnp.float32)
    return placed.at[:, col_block].add(contrib).reshape(row_count, complete_width)

def reference(queries, key_cache, value_cache, new_keys, new_values, lengths, request_variant, holder_slot, out_weight, factor_in, second_factor, block_values, block_scale, block_owner, block_cell):
    attended = attend(queries, key_cache, value_cache, new_keys, new_values, lengths)
    row_count, complete_width = attended.shape
    variants, block_count, block_size, _ = block_values.shape
    slot_row = jnp.take(holder_slot, request_variant).astype(jnp.int32)
    dense_product = jnp.dot(attended, out_weight, preferred_element_type=jnp.float32)
    low_all = jnp.einsum('rd,jdk->rjk', attended.astype(jnp.float32), factor_in.astype(jnp.float32))
    low_rank = jnp.take_along_axis(low_all, slot_row[:, None, None], axis=1)[:, 0, :].astype(jnp.bfloat16)
    slot_pick = slot_row[:, None] == jnp.arange(variants, dtype=jnp.int32)[None, :]
    broadcast_rows = jnp.where(slot_pick[:, :, None], low_rank[:, None, :], jnp.zeros((), jnp.bfloat16)).reshape(row_count, -1)
    adapter_product = jnp.dot(broadcast_rows, second_factor.reshape(-1, complete_width), preferred_element_type=jnp.float32)
    rebuilt = (block_values.astype(jnp.float32) * block_scale[:, :, None, None]).astype(jnp.bfloat16).reshape(-1, block_size, block_size)
    col_blocks = complete_width // block_size
    per_owner = complete_width // N_TP // block_size
    row_block = (block_owner[:, :, 0] * per_owner + block_cell // col_blocks).reshape(-1).astype(jnp.int32)
    col_block = (block_cell % col_blocks).reshape(-1).astype(jnp.int32)
    slot_of = (jnp.arange(variants * block_count, dtype=jnp.int32) // block_count).astype(jnp.int32)
    residual_block_product = apply_blocks(attended, slot_row, slot_of, row_block, col_block, rebuilt, complete_width)
    return (dense_product + residual_block_product + adapter_product).astype(jnp.bfloat16)
```

```python
import functools
import math

import jax
import jax.numpy as jnp
from jax import lax
from jax.experimental import pallas as pl
from jax.experimental.pallas import tpu as pltpu
from jax.sharding import PartitionSpec as P

BF16 = jnp.bfloat16
F32 = jnp.float32


def attend_local(queries, key_cache, value_cache, new_keys, new_values, lengths):
    row_count = queries.shape[0]
    cache_len = key_cache.shape[2]
    head_dim = key_cache.shape[3]
    query_heads = queries.reshape(row_count, -1, head_dim)
    inv_scale = 1.0 / math.sqrt(head_dim)
    scores = (
        jnp.einsum("rhd,rpd->rhp", query_heads, key_cache[0], preferred_element_type=F32) * inv_scale
    )
    fresh_score = (
        jnp.einsum("rhd,rd->rh", query_heads, new_keys[0], preferred_element_type=F32) * inv_scale
    )
    in_cache = (jnp.arange(cache_len, dtype=jnp.int32)[None, :] < lengths[:, None])[:, None, :]
    masked = jnp.where(in_cache, scores, -1e30)
    top_score = jnp.maximum(jnp.max(masked, axis=-1), fresh_score)
    raw_weights = jnp.where(in_cache, jnp.exp(masked - top_score[..., None]), 0.0)
    fresh_raw = jnp.exp(fresh_score - top_score)
    denominator = jnp.sum(raw_weights, axis=-1) + fresh_raw
    weights = (raw_weights / denominator[..., None]).astype(BF16)
    fresh_weight = (fresh_raw / denominator).astype(BF16)
    attended = jnp.einsum("rhp,rpd->rhd", weights, value_cache[0], preferred_element_type=F32)
    attended = (
        attended + fresh_weight.astype(F32)[..., None] * new_values[0].astype(F32)[:, None, :]
    )
    return jnp.transpose(attended.astype(BF16), (1, 0, 2))


def delta_kernel(
    per_owner, tiles_ref, slot_ref, factor_ref, second_ref, base_ref, values_ref,
    scale_ref, owner_ref, cell_ref, out_ref, total,
):
    tiles, rows, side = tiles_ref.shape
    slots, block_count = values_ref.shape[:2]
    rank = factor_ref.shape[0] // slots
    low = jnp.zeros((rows, slots * rank), F32)
    for t in range(0, tiles, 2):
        pair = jnp.concatenate([tiles_ref[t], tiles_ref[t + 1]], axis=1)
        low = low + lax.dot_general(
            pair,
            factor_ref[:, t * side : (t + 2) * side],
            (((1,), (1,)), ((), ())),
            preferred_element_type=F32,
        )
    slot_row = slot_ref[...]
    held = lax.broadcasted_iota(jnp.int32, (rows, slots * rank), 1) // rank
    low = jnp.where(slot_row == held, low, 0.0).astype(BF16)
    for c in range(0, tiles, 2):
        part = base_ref[:, c * side : (c + 2) * side] + jnp.dot(
            low, second_ref[:, c * side : (c + 2) * side], preferred_element_type=F32
        )
        total[c] = part[:, :side]
        total[c + 1] = part[:, side:]
    group = 4
    for j in range(slots):
        mine = jnp.broadcast_to(slot_row == j, (rows, side))

        def step(i, carry, j=j, mine=mine):
            added = []
            for k in range(group):
                b = i * group + k
                cell = cell_ref[j, b]
                row_block = owner_ref[j, b] * per_owner + lax.div(cell, tiles)
                rebuilt = (values_ref[j, b].astype(F32) * scale_ref[j, b]).astype(BF16)
                product = jnp.dot(tiles_ref[row_block], rebuilt, preferred_element_type=F32)
                added.append((lax.rem(cell, tiles), jnp.where(mine, product, 0.0)))
            for column, product in added:
                total[column] += product
            return carry

        lax.fori_loop(0, block_count // group, step, 0)
    for c in range(tiles):
        out_ref[:, c * side : (c + 1) * side] = total[c].astype(BF16)


def add_delta(tiles, slot_local, factor_t, second, base, block_values, scale, owner, cell, per_owner):
    count, rows, side = tiles.shape
    vmem = pl.BlockSpec(memory_space=pltpu.VMEM)
    smem = pl.BlockSpec(memory_space=pltpu.SMEM)
    return pl.pallas_call(
        functools.partial(delta_kernel, per_owner),
        out_shape=jax.ShapeDtypeStruct((rows, count * side), BF16),
        in_specs=[vmem] * 6 + [smem] * 3,
        out_specs=vmem,
        scratch_shapes=[pltpu.VMEM((count, rows, side), F32)],
        compiler_params=pltpu.CompilerParams(vmem_limit_bytes=40 * 1024 * 1024),
        name="delta",
    )(tiles, slot_local, factor_t, second, base, block_values, scale, owner, cell)


def body(
    queries, key_cache, value_cache, new_keys, new_values, lengths, request_variant, holder_slot,
    out_weight, factor_in, second_factor, block_values, block_scale, block_owner, block_cell,
):
    attended = attend_local(queries, key_cache, value_cache, new_keys, new_values, lengths)
    heads, rows, side = attended.shape
    variants = holder_slot.shape[0]
    slots_here = block_values.shape[0]
    width = out_weight.shape[1]
    slot_row = jnp.sum(
        jnp.where(
            request_variant[:, None] == jnp.arange(variants, dtype=jnp.int32)[None, :],
            holder_slot[None, :],
            0,
        ),
        axis=1,
    )
    slot_local = (slot_row - lax.axis_index("tp") * slots_here)[:, None]
    tiles = lax.all_gather(attended, "tp", axis=0, tiled=True)
    base = lax.dot_general(
        attended,
        out_weight.reshape(heads, side, width),
        (((0, 2), (0, 1)), ((), ())),
        preferred_element_type=F32,
    )
    factor_t = jnp.swapaxes(factor_in, 1, 2).reshape(-1, factor_in.shape[1])
    partial = add_delta(
        tiles,
        slot_local,
        factor_t,
        second_factor.reshape(-1, width),
        base,
        block_values,
        block_scale,
        block_owner[:, :, 0],
        block_cell,
        heads,
    )
    return lax.psum_scatter(partial, "tp", scatter_dimension=1, tiled=True)


def solution(mesh):
    return jax.shard_map(
        body,
        mesh=mesh,
        in_specs=(
            P(("groups", "rep"), "tp"),
            P("tp", ("groups", "rep"), None, None),
            P("tp", ("groups", "rep"), None, None),
            P("tp", ("groups", "rep"), None),
            P("tp", ("groups", "rep"), None),
            P(("groups", "rep")),
            P(("groups", "rep")),
            P(),
            P("tp", None),
            P("tp", None, None),
            P("tp", None, None),
            P("tp", None, None, None),
            P("tp", None),
            P("tp", None, None),
            P("tp", None),
        ),
        out_specs=P(("groups", "rep"), "tp"),
        check_vma=False,
    )
```

```python
import functools
import math

import jax
import jax.numpy as jnp
from jax import lax
from jax.experimental import pallas as pl
from jax.experimental.pallas import tpu as pltpu
from jax.sharding import PartitionSpec as P

BF16 = jnp.bfloat16
F32 = jnp.float32


def attend_local(queries, key_cache, value_cache, new_keys, new_values, lengths):
    row_count = queries.shape[0]
    cache_len = key_cache.shape[2]
    head_dim = key_cache.shape[3]
    query_heads = queries.reshape(row_count, -1, head_dim)
    inv_scale = 1.0 / math.sqrt(head_dim)
    scores = (
        jnp.einsum("rhd,rpd->rhp", query_heads, key_cache[0], preferred_element_type=F32) * inv_scale
    )
    fresh_score = (
        jnp.einsum("rhd,rd->rh", query_heads, new_keys[0], preferred_element_type=F32) * inv_scale
    )
    in_cache = (jnp.arange(cache_len, dtype=jnp.int32)[None, :] < lengths[:, None])[:, None, :]
    masked = jnp.where(in_cache, scores, -1e30)
    top_score = jnp.maximum(jnp.max(masked, axis=-1), fresh_score)
    raw_weights = jnp.where(in_cache, jnp.exp(masked - top_score[..., None]), 0.0)
    fresh_raw = jnp.exp(fresh_score - top_score)
    denominator = jnp.sum(raw_weights, axis=-1) + fresh_raw
    weights = (raw_weights / denominator[..., None]).astype(BF16)
    fresh_weight = (fresh_raw / denominator).astype(BF16)
    attended = jnp.einsum("rhp,rpd->rhd", weights, value_cache[0], preferred_element_type=F32)
    attended = (
        attended + fresh_weight.astype(F32)[..., None] * new_values[0].astype(F32)[:, None, :]
    )
    return jnp.transpose(attended.astype(BF16), (1, 0, 2))


def ring_order(count):
    if count == 8:
        return [0, 2, 4, 6, 7, 5, 3, 1]
    return list(range(count))


def gather_ring(first, second, to_left, to_right, count):
    got = [[None, None] for _ in range(count)]
    got[0] = [first, second]
    half = count // 2
    right, left = [first, second], [first, second]
    for step in range(1, half + 1):
        for part in (0, 1):
            if step < half or part == 0:
                right[part] = lax.ppermute(right[part], "tp", to_left)
                got[step][part] = right[part]
            if step < half or part == 1:
                left[part] = lax.ppermute(left[part], "tp", to_right)
                got[count - step][part] = left[part]
    return got


def scatter_ring(parts, to_left, to_right, count):
    half = count // 2
    sums = [None, None]
    for part in (0, 1):
        reach_left, reach_right = (half, half - 1) if part == 0 else (half - 1, half)
        left = right = None
        for distance in range(reach_left, 0, -1):
            mine = parts[count - distance][part]
            left = mine if left is None else (mine.astype(F32) + left.astype(F32)).astype(BF16)
            left = lax.ppermute(left, "tp", to_left)
        for distance in range(reach_right, 0, -1):
            mine = parts[distance][part]
            right = mine if right is None else (mine.astype(F32) + right.astype(F32)).astype(BF16)
            right = lax.ppermute(right, "tp", to_right)
        sums[part] = parts[0][part] + left.astype(F32) + right.astype(F32)
    return jnp.concatenate(sums, axis=0).astype(BF16)


def delta_kernel(count, *refs):
    chunk_refs, refs = refs[: 2 * count], refs[2 * count :]
    slot_ref, factor_ref, second_ref, base_ref, values_ref = refs[:5]
    scale_ref, owner_ref, cell_ref, order_ref, place_ref = refs[5:10]
    out_refs, (tiles, total) = refs[10:-2], refs[-2:]
    half, rows, side = chunk_refs[0].shape
    heads = 2 * half
    width = heads * side
    slots, block_count = values_ref.shape[:2]
    rank = factor_ref.shape[0] // slots
    low = jnp.zeros((rows, slots * rank), F32)
    for k in range(count):
        for i in range(0, heads, 2):
            one = chunk_refs[2 * k + i // half][i % half]
            two = chunk_refs[2 * k + (i + 1) // half][(i + 1) % half]
            tiles[k * heads + i] = one
            tiles[k * heads + i + 1] = two
            start = pl.multiple_of(order_ref[k] * width + i * side, 2 * side)
            low = low + lax.dot_general(
                jnp.concatenate([one, two], axis=1),
                factor_ref[:, pl.ds(start, 2 * side)],
                (((1,), (1,)), ((), ())),
                preferred_element_type=F32,
            )
    slot_row = slot_ref[...]
    held = lax.broadcasted_iota(jnp.int32, (rows, slots * rank), 1) // rank
    low = jnp.where(slot_row == held, low, 0.0).astype(BF16)
    for k in range(count):
        for i in range(0, heads, 2):
            start = pl.multiple_of(order_ref[k] * width + i * side, 2 * side)
            part = base_ref[:, pl.ds(start, 2 * side)] + jnp.dot(
                low, second_ref[:, pl.ds(start, 2 * side)], preferred_element_type=F32
            )
            total[k * heads + i] = part[:, :side]
            total[k * heads + i + 1] = part[:, side:]
    group = 4
    for j in range(slots):
        mine = jnp.broadcast_to(slot_row == j, (rows, side))

        def step(i, carry, j=j, mine=mine):
            added = []
            for g in range(group):
                b = i * group + g
                cell = cell_ref[j, b]
                row_cell, column = lax.div(cell, count * heads), lax.rem(cell, count * heads)
                source = place_ref[owner_ref[j, b]] * heads + row_cell
                target = place_ref[lax.div(column, heads)] * heads + lax.rem(column, heads)
                rebuilt = (values_ref[j, b].astype(F32) * scale_ref[j, b]).astype(BF16)
                product = jnp.dot(tiles[source], rebuilt, preferred_element_type=F32)
                added.append((target, jnp.where(mine, product, 0.0)))
            for target, product in added:
                total[target] += product
            return carry

        lax.fori_loop(0, block_count // group, step, 0)
    for i in range(heads):
        out_refs[0][:, i * side : (i + 1) * side] = total[i]
    for k in range(1, count):
        for part in (0, 1):
            out = out_refs[2 * k - 1 + part]
            for i in range(heads):
                out[:, i * side : (i + 1) * side] = total[
                    k * heads + i, part * (rows // 2) : (part + 1) * (rows // 2)
                ].astype(BF16)


def add_delta(chunks, slot_local, factor_t, second, base, block_values, scale, owner, cell, order, place):
    count = len(chunks)
    half, rows, side = chunks[0][0].shape
    heads = 2 * half
    width = heads * side
    vmem = pl.BlockSpec(memory_space=pltpu.VMEM)
    smem = pl.BlockSpec(memory_space=pltpu.SMEM)
    outs = [jax.ShapeDtypeStruct((rows, width), F32)]
    outs += [jax.ShapeDtypeStruct((rows // 2, width), BF16)] * (2 * (count - 1))
    got = pl.pallas_call(
        functools.partial(delta_kernel, count),
        out_shape=outs,
        in_specs=[vmem] * (2 * count + 5) + [smem] * 5,
        out_specs=[vmem] * len(outs),
        scratch_shapes=[
            pltpu.VMEM((count * heads, rows, side), BF16),
            pltpu.VMEM((count * heads, rows, side), F32),
        ],
        compiler_params=pltpu.CompilerParams(vmem_limit_bytes=40 * 1024 * 1024),
        name="delta",
    )(
        *[part for chunk in chunks for part in chunk],
        slot_local, factor_t, second, base, block_values, scale, owner, cell, order, place,
    )
    own = [got[0][: rows // 2], got[0][rows // 2 :]]
    return [own] + [[got[2 * k - 1], got[2 * k]] for k in range(1, count)]


def body(
    queries, key_cache, value_cache, new_keys, new_values, lengths, request_variant, holder_slot,
    out_weight, factor_in, second_factor, block_values, block_scale, block_owner, block_cell,
):
    count = lax.axis_size("tp")
    ring = ring_order(count)
    to_right = [(ring[i], ring[(i + 1) % count]) for i in range(count)]
    to_left = [(ring[(i + 1) % count], ring[i]) for i in range(count)]
    spots = jnp.asarray([ring.index(i) for i in range(count)], jnp.int32)
    spot = spots[lax.axis_index("tp")]
    order = jnp.asarray(ring, jnp.int32)[(spot + jnp.arange(count, dtype=jnp.int32)) % count]
    place = (spots - spot) % count

    attended = attend_local(queries, key_cache, value_cache, new_keys, new_values, lengths)
    heads, rows, side = attended.shape
    variants = holder_slot.shape[0]
    slots_here = block_values.shape[0]
    width = out_weight.shape[1]
    slot_row = jnp.sum(
        jnp.where(
            request_variant[:, None] == jnp.arange(variants, dtype=jnp.int32)[None, :],
            holder_slot[None, :],
            0,
        ),
        axis=1,
    )
    slot_local = (slot_row - lax.axis_index("tp") * slots_here)[:, None]
    chunks = gather_ring(attended[: heads // 2], attended[heads // 2 :], to_left, to_right, count)
    base = lax.dot_general(
        attended,
        out_weight.reshape(heads, side, width),
        (((0, 2), (0, 1)), ((), ())),
        preferred_element_type=F32,
    )
    factor_t = jnp.swapaxes(factor_in, 1, 2).reshape(-1, factor_in.shape[1])
    parts = add_delta(
        chunks,
        slot_local,
        factor_t,
        second_factor.reshape(-1, width),
        base,
        block_values,
        block_scale,
        block_owner[:, :, 0],
        block_cell,
        order,
        place,
    )
    return scatter_ring(parts, to_left, to_right, count)


def solution(mesh):
    return jax.shard_map(
        body,
        mesh=mesh,
        in_specs=(
            P(("groups", "rep"), "tp"),
            P("tp", ("groups", "rep"), None, None),
            P("tp", ("groups", "rep"), None, None),
            P("tp", ("groups", "rep"), None),
            P("tp", ("groups", "rep"), None),
            P(("groups", "rep")),
            P(("groups", "rep")),
            P(),
            P("tp", None),
            P("tp", None, None),
            P("tp", None, None),
            P("tp", None, None, None),
            P("tp", None),
            P("tp", None, None),
            P("tp", None),
        ),
        out_specs=P(("groups", "rep"), "tp"),
        check_vma=False,
    )
```

```python
import functools
import math

import jax
import jax.numpy as jnp
from jax import lax
from jax.experimental import pallas as pl
from jax.experimental.pallas import tpu as pltpu
from jax.sharding import PartitionSpec as P

BF16 = jnp.bfloat16
F32 = jnp.float32
CAP = 2
ROW_BLOCK = 16
MIB = 1024 * 1024
NT = (((1,), (1,)), ((), ()))
VMEM = pl.BlockSpec(memory_space=pltpu.VMEM)
SMEM = pl.BlockSpec(memory_space=pltpu.SMEM)
ANY = pl.BlockSpec(memory_space=pl.ANY)


def ring_order(count):
    if count == 8:
        return [0, 2, 4, 6, 7, 5, 3, 1]
    return list(range(count))


def owner_at(distance, count):
    me = lax.axis_index("tp")
    if count != 8:
        return lax.rem(me + distance, count)
    spot = jnp.where((me & 1) == 0, me >> 1, count - 1 - (me >> 1))
    spot = lax.rem(spot + distance, count)
    return jnp.where(spot < count // 2, 2 * spot, 2 * (count - 1 - spot) + 1)


def call(kernel, name, outs, ins, specs, out_specs, scratch=(), limit=16, flops=0, moved=0):
    return pl.pallas_call(
        kernel,
        out_shape=outs,
        in_specs=specs,
        out_specs=out_specs,
        scratch_shapes=list(scratch),
        compiler_params=pltpu.CompilerParams(vmem_limit_bytes=limit * MIB),
        cost_estimate=pl.CostEstimate(flops=flops, bytes_accessed=moved, transcendentals=0),
        name=name,
    )(*ins)


def attend_kernel(q_ref, key_ref, value_ref, new_key_ref, new_value_ref, length_ref, out_ref):
    heads, rows, side = out_ref.shape
    cache = key_ref.shape[0] // rows
    tall, wide = heads * ROW_BLOCK, cache * ROW_BLOCK
    scale = 1.0 / math.sqrt(side)
    lengths = jnp.transpose(jnp.broadcast_to(length_ref[...].astype(F32), (rows, rows)))[:, :1]
    row_in = lax.broadcasted_iota(jnp.int32, (tall, wide), 0) % ROW_BLOCK
    place = (lax.broadcasted_iota(jnp.int32, (tall, wide), 1) - cache * row_in).astype(F32)
    place = jnp.where(place < 0, 1e9, place)
    for r in range(0, rows, ROW_BLOCK):
        here = slice(r, r + ROW_BLOCK)
        cached = slice(r * cache, (r + ROW_BLOCK) * cache)
        query = jnp.concatenate(
            [q_ref[here, h * side : (h + 1) * side] for h in range(heads)], axis=0
        )
        new_key = jnp.concatenate([new_key_ref[here].astype(F32)] * heads, axis=0)
        new_value = jnp.concatenate([new_value_ref[here].astype(F32)] * heads, axis=0)
        live = place < jnp.concatenate([lengths[here]] * heads, axis=0)
        scores = lax.dot_general(query, key_ref[cached], NT, preferred_element_type=F32) * scale
        fresh = jnp.sum(query.astype(F32) * new_key, axis=1, keepdims=True) * scale
        scores = jnp.where(live, scores, -1e30)
        top = jnp.maximum(jnp.max(scores, axis=1, keepdims=True), fresh)
        raw = jnp.where(live, jnp.exp(scores - top), 0.0)
        fresh_raw = jnp.exp(fresh - top)
        inverse = 1.0 / (jnp.sum(raw, axis=1, keepdims=True) + fresh_raw)
        weights = (raw * inverse).astype(BF16)
        fresh_weight = (fresh_raw * inverse).astype(BF16).astype(F32)
        attended = jnp.dot(weights, value_ref[cached], preferred_element_type=F32)
        attended = (attended + fresh_weight * new_value).astype(BF16)
        for h in range(heads):
            out_ref[h, here, :] = attended[h * ROW_BLOCK : (h + 1) * ROW_BLOCK]


def dense_kernel(distances, count, first, *refs):
    x_ref, weight_ref = refs[:2]
    if first:
        variant_ref, holder_ref, owner_ref = refs[2:5]
        outs, slot_ref, table_ref = refs[5 : 5 + len(distances)], refs[-4], refs[-3]
    else:
        outs = refs[3 : 3 + len(distances)]
    buffers, sems = refs[-2:]
    heads, rows, side = x_ref.shape
    width = heads * side
    depth = buffers.shape[0]
    cuts = 2 if width >= 512 else 1
    piece = width // cuts

    def fetch(i):
        start = pl.multiple_of(owner_at(distances[i // cuts], count) * width, width) + i % cuts * piece
        return pltpu.make_async_copy(
            weight_ref.at[:, pl.ds(pl.multiple_of(start, piece), piece)],
            buffers.at[i % depth],
            sems.at[i % depth],
        )

    total = len(distances) * cuts
    for i in range(min(depth, total)):
        fetch(i).start()
    if first:
        slots = owner_ref.shape[0]
        variant = variant_ref[...]
        slot_row = jnp.zeros(variant.shape, jnp.int32)
        for v in range(holder_ref.shape[0]):
            slot_row = jnp.where(variant == v, holder_ref[v], slot_row)
        slot_row = (slot_row - lax.axis_index("tp") * slots).astype(F32)
        slot_ref[...] = jnp.transpose(jnp.broadcast_to(slot_row, (rows, rows))).astype(jnp.int32)
        for e in range(table_ref.shape[0]):
            table_ref[e] = -1
        for j in range(slots):

            def note(b, carry, j=j):
                e = (owner_ref[j, b] * slots + j) * CAP
                table_ref[e + jnp.where(table_ref[e] >= 0, 1, 0)] = b
                return carry

            lax.fori_loop(0, owner_ref.shape[1], note, 0)
    x = jnp.concatenate([x_ref[h] for h in range(heads)], axis=1)
    for i in range(total):
        fetch(i).wait()
        outs[i // cuts][:, i % cuts * piece : (i % cuts + 1) * piece] = jnp.dot(
            x, buffers[i % depth], preferred_element_type=F32
        )
        if i + depth < total:
            fetch(i + depth).start()


def held_blocks(distance, count, slots, heads, scale_ref, cell_ref, table_ref):
    tiles = count * heads
    owner = owner_at(distance, count)
    listed = []
    for j in range(slots):
        for c in range(CAP):
            b = table_ref[(owner * slots + j) * CAP + c]
            found = jnp.maximum(b, 0)
            cell = cell_ref[j, found]
            scale = jnp.where(b >= 0, scale_ref[j, found], 0.0)
            listed.append((j, found, scale, lax.div(cell, tiles), lax.rem(cell, tiles)))
    return listed


def fold_chunk(distance, count, chunk_ref, slot, factor_ref, values_ref, scale_ref, cell_ref,
               table_ref, low_ref):
    heads, rows, side = chunk_ref.shape
    width = heads * side
    features = jnp.concatenate([chunk_ref[h] for h in range(heads)], axis=1)
    start = pl.multiple_of(owner_at(distance, count) * width, width)
    low_ref[...] += lax.dot_general(
        features, factor_ref[:, pl.ds(start, width)], NT, preferred_element_type=F32
    )
    added = []
    for j, b, scale, row_block, column in held_blocks(
        distance, count, values_ref.shape[0], heads, scale_ref, cell_ref, table_ref
    ):
        mine = jnp.where(slot == j, 1.0, 0.0)
        product = jnp.dot(chunk_ref[row_block], values_ref[j, b], preferred_element_type=F32)
        added.append((column, product * (mine * scale)))
    return added


def fold_kernel(distances, count, first, *refs):
    chunks, refs = refs[: len(distances)], refs[len(distances) :]
    slot_ref, factor_ref, values_ref, scale_ref, cell_ref, table_ref = refs[:6]
    low_ref, block_ref = refs[-2:]
    if first:
        low_ref[...] = jnp.zeros_like(low_ref)
        block_ref[...] = jnp.zeros_like(block_ref)
    else:
        low_ref[...] = refs[6][...]
        block_ref[...] = refs[7][...]
    slot = slot_ref[...]
    for distance, chunk in zip(distances, chunks):
        for column, product in fold_chunk(distance, count, chunk, slot, factor_ref, values_ref,
                                          scale_ref, cell_ref, table_ref, low_ref):
            block_ref[column] += product


def part_for(distance, count, low, second_ref, dense_ref, block_ref, extra_ref, columns, out_ref):
    rows, width = dense_ref.shape
    side = block_ref.shape[2]
    heads = width // side
    owner = owner_at(distance, count)
    start = pl.multiple_of(owner * width, width)
    blocks = jnp.concatenate([block_ref[owner * heads + i] for i in range(heads)], axis=1)
    out_ref[...] = (
        jnp.dot(low, second_ref[:, pl.ds(start, width)], preferred_element_type=F32)
        + dense_ref[...]
        + blocks
    )
    for e, column in enumerate(columns):

        @pl.when(lax.div(column, heads) == owner)
        def _(e=e, column=column):
            place = pl.ds(pl.multiple_of(lax.rem(column, heads) * side, side), side)
            out_ref[:, place] += extra_ref[e]


def finish_kernel(distances, count, *refs):
    front_ref, back_ref, slot_ref, factor_ref, values_ref, scale_ref, cell_ref, table_ref = refs[:8]
    second_ref, low_in, block_ref = refs[8:11]
    dense_refs = refs[11 : 11 + len(distances)]
    low_out, extra_out, top_out, bottom_out = refs[11 + len(distances) : 15 + len(distances)]
    outs = refs[15 + len(distances) : -3]
    chunk, low_sum, farthest = refs[-3:]
    half, rows, side = front_ref.shape
    chunk[:half] = front_ref[...]
    chunk[half:] = back_ref[...]
    low_sum[...] = low_in[...]
    slot = slot_ref[...]
    added = fold_chunk(distances[0], count, chunk, slot, factor_ref, values_ref, scale_ref, cell_ref,
                       table_ref, low_sum)
    for e, (_, product) in enumerate(added):
        extra_out[e] = product
    columns = [column for column, _ in added]
    low_width = low_sum.shape[1]
    rank = low_width // values_ref.shape[0]
    held = lax.broadcasted_iota(jnp.int32, (rows, low_width), 1) // rank
    slots_wide = jnp.concatenate([slot] * -(-low_width // side), axis=1)[:, :low_width]
    low = jnp.where(slots_wide == held, low_sum[...], 0.0).astype(BF16)
    low_out[...] = low
    for distance, dense_ref, out in zip(distances, dense_refs, (farthest, *outs)):
        part_for(distance, count, low, second_ref, dense_ref, block_ref, extra_out, columns, out)
    top_out[...] = farthest[: rows // 2].astype(BF16)
    bottom_out[...] = farthest[rows // 2 :].astype(BF16)


def part_kernel(distances, count, slots, *refs):
    low_ref, second_ref, block_ref, extra_ref, scale_ref, cell_ref, table_ref = refs[:7]
    dense_refs = refs[7 : 7 + len(distances)]
    outs = refs[7 + len(distances) :]
    heads = dense_refs[0].shape[1] // block_ref.shape[2]
    listed = held_blocks(count // 2, count, slots, heads, scale_ref, cell_ref, table_ref)
    columns = [entry[-1] for entry in listed]
    for distance, dense_ref, out in zip(distances, dense_refs, outs):
        part_for(distance, count, low_ref[...], second_ref, dense_ref, block_ref, extra_ref, columns, out)


def after(value, *others):
    return lax.optimization_barrier((value, *others))[0]


def body(
    queries, key_cache, value_cache, new_keys, new_values, lengths, request_variant, holder_slot,
    out_weight, factor_in, second_factor, block_values, block_scale, block_owner, block_cell,
):
    count = lax.axis_size("tp")
    half = count // 2
    ring = ring_order(count)
    to_right = [(ring[i], ring[(i + 1) % count]) for i in range(count)]
    to_left = [(ring[(i + 1) % count], ring[i]) for i in range(count)]
    rows, width = queries.shape
    side = key_cache.shape[3]
    cache = key_cache.shape[2]
    heads = width // side
    slots = block_values.shape[0]
    complete = out_weight.shape[1]
    low_width = slots * factor_in.shape[2]
    shape = jax.ShapeDtypeStruct

    attended = call(
        attend_kernel,
        "attend",
        shape((heads, rows, side), BF16),
        (queries, key_cache.reshape(-1, side), value_cache.reshape(-1, side), new_keys[0],
         new_values[0], lengths[None, :]),
        [VMEM] * 6,
        VMEM,
    )

    chunks = {0: attended}
    right = left = attended
    for step in range(1, half):
        right = chunks[step] = lax.ppermute(right, "tp", to_left)
        left = chunks[count - step] = lax.ppermute(left, "tp", to_right)
    front = lax.ppermute(right[: heads // 2], "tp", to_left)
    back = lax.ppermute(left[heads // 2 :], "tp", to_right)

    wanted = [half]
    for distance in range(half - 1, 0, -1):
        wanted += [distance, count - distance]
    wanted += [0]
    piece = width // 2 if width >= 512 else width
    streams = [pltpu.VMEM((4, width, piece), BF16), pltpu.SemaphoreType.DMA((4,))]
    dense_cost = dict(flops=rows * width * complete, moved=width * complete)
    dense = {}
    *sums, slot, table = call(
        functools.partial(dense_kernel, wanted[:half], count, True),
        "dense_first",
        [shape((rows, width), F32)] * half
        + [shape((rows, rows), jnp.int32), shape((count * slots * CAP,), jnp.int32)],
        (attended, out_weight, request_variant[None, :], holder_slot, block_owner[:, :, 0]),
        [VMEM, ANY, VMEM, SMEM, SMEM],
        [VMEM] * half + [VMEM, SMEM],
        streams,
        **dense_cost,
    )
    dense.update(zip(wanted[:half], sums))
    sums = call(
        functools.partial(dense_kernel, wanted[half:], count, False),
        "dense_second",
        [shape((rows, width), F32)] * half,
        (attended, out_weight, chunks[1]),
        [VMEM, ANY, ANY],
        [VMEM] * half,
        streams,
        **dense_cost,
    )
    dense.update(zip(wanted[half:], sums))

    factor_t = jnp.swapaxes(factor_in, 1, 2).reshape(low_width, -1)
    second = second_factor.reshape(low_width, complete)
    state = [shape((rows, low_width), F32), shape((complete // side, rows, side), F32)]
    early = [0]
    for distance in range(1, half - 1):
        early += [distance, count - distance]
    late = [half - 1, count - half + 1]
    tables = (slot, factor_t, block_values, block_scale, block_cell, table)
    table_specs = [VMEM, VMEM, VMEM, SMEM, SMEM, SMEM]
    low, blocks = call(
        functools.partial(fold_kernel, early, count, True),
        "fold_early",
        state,
        (*[chunks[d] for d in early], *tables),
        [VMEM] * len(early) + table_specs,
        [VMEM] * 2,
        flops=rows * low_width * complete,
        moved=4 * MIB,
    )
    low, blocks = call(
        functools.partial(fold_kernel, late, count, False),
        "fold_late",
        state,
        (*[chunks[d] for d in late], *tables, low, blocks),
        [VMEM] * len(late) + table_specs + [VMEM] * 2,
        [VMEM] * 2,
        flops=rows * low_width * width * 4,
        moved=MIB,
    )
    first = wanted[:3]
    extras = shape((slots * CAP, rows, side), F32)
    low, extra, top, bottom, one, two = call(
        functools.partial(finish_kernel, first, count),
        "finish",
        [shape((rows, low_width), BF16), extras]
        + [shape((rows // 2, width), BF16)] * 2
        + [shape((rows, width), F32)] * 2,
        (front, back, *tables, second, low, blocks, *[dense[d] for d in first]),
        [VMEM] * 2 + table_specs + [VMEM] * (3 + len(first)),
        [VMEM] * 6,
        [pltpu.VMEM((heads, rows, side), BF16), pltpu.VMEM((rows, low_width), F32),
         pltpu.VMEM((rows, width), F32)],
        flops=rows * low_width * width * 8,
        moved=2 * MIB,
    )
    parts = {first[1]: one, first[2]: two}
    for distance in range(half - 2, -1, -1):
        pair = [distance, count - distance] if distance else [0]
        sums = call(
            functools.partial(part_kernel, pair, count, slots),
            "part",
            [shape((rows, width), F32)] * len(pair),
            (low, second, blocks, extra, block_scale, block_cell, table, *[dense[d] for d in pair]),
            [VMEM] * 4 + [SMEM] * 3 + [VMEM] * len(pair),
            [VMEM] * len(pair),
            flops=rows * low_width * width * 4,
            moved=2 * MIB,
        )
        parts.update(zip(pair, sums))

    left = lax.ppermute(top, "tp", to_left)
    right = lax.ppermute(bottom, "tp", to_right)
    for distance in range(half - 1, 0, -1):
        mine, other = parts[count - distance], parts[distance]
        if distance == half - 1:
            none = jnp.zeros_like(left)
            left = jnp.concatenate([left, none], axis=0)
            right = jnp.concatenate([none, right], axis=0)
        left = lax.ppermute((mine + left.astype(F32)).astype(BF16), "tp", to_left)
        right = lax.ppermute((other + right.astype(F32)).astype(BF16), "tp", to_right)
    return (parts[0] + left.astype(F32) + right.astype(F32)).astype(BF16)


def solution(mesh):
    return jax.shard_map(
        body,
        mesh=mesh,
        in_specs=(
            P(("groups", "rep"), "tp"),
            P("tp", ("groups", "rep"), None, None),
            P("tp", ("groups", "rep"), None, None),
            P("tp", ("groups", "rep"), None),
            P("tp", ("groups", "rep"), None),
            P(("groups", "rep")),
            P(("groups", "rep")),
            P(),
            P("tp", None),
            P("tp", None, None),
            P("tp", None, None),
            P("tp", None, None, None),
            P("tp", None),
            P("tp", None, None),
            P("tp", None),
        ),
        out_specs=P(("groups", "rep"), "tp"),
        check_vma=False,
    )
```

```python
import functools
import math

import jax
import jax.numpy as jnp
from jax import lax
from jax.experimental import pallas as pl
from jax.experimental.pallas import tpu as pltpu
from jax.sharding import PartitionSpec as P

BF16 = jnp.bfloat16
F32 = jnp.float32
CAP = 2
ROW_BLOCK = 16
PIECES = 4
MIB = 1024 * 1024
NT = (((1,), (1,)), ((), ()))
VMEM = pl.BlockSpec(memory_space=pltpu.VMEM)
SMEM = pl.BlockSpec(memory_space=pltpu.SMEM)
ANY = pl.BlockSpec(memory_space=pl.ANY)


def ring_order(count):
    if count == 8:
        return [0, 2, 4, 6, 7, 5, 3, 1]
    return list(range(count))


def owner_at(distance, count):
    me = lax.axis_index("tp")
    if count != 8:
        return lax.rem(me + distance, count)
    spot = jnp.where((me & 1) == 0, me >> 1, count - 1 - (me >> 1))
    spot = lax.rem(spot + distance, count)
    return jnp.where(spot < count // 2, 2 * spot, 2 * (count - 1 - spot) + 1)


def call(kernel, name, outs, ins, specs, out_specs, scratch=(), limit=16, flops=0, moved=0):
    return pl.pallas_call(
        kernel,
        out_shape=outs,
        in_specs=specs,
        out_specs=out_specs,
        scratch_shapes=list(scratch),
        compiler_params=pltpu.CompilerParams(vmem_limit_bytes=limit * MIB),
        cost_estimate=pl.CostEstimate(flops=flops, bytes_accessed=moved, transcendentals=0),
        name=name,
    )(*ins)


def attend_kernel(
    query_hbm, key_hbm, value_hbm, new_key_hbm, new_value_hbm, length_hbm, out_ref,
    q_ref, key_ref, value_ref, new_key_ref, new_value_ref, length_ref, sems,
):
    heads, rows, side = out_ref.shape
    cache = key_ref.shape[0] // rows
    small = [
        pltpu.make_async_copy(source, target, sems.at[i])
        for i, (source, target) in enumerate(
            ((length_hbm, length_ref), (query_hbm, q_ref), (new_key_hbm, new_key_ref),
             (new_value_hbm, new_value_ref))
        )
    ]
    tall_piece = key_ref.shape[0] // PIECES
    pieces = []
    for i in range(PIECES):
        for n, (source, target) in enumerate(((key_hbm, key_ref), (value_hbm, value_ref))):
            part = pl.ds(i * tall_piece, tall_piece)
            pieces.append(
                pltpu.make_async_copy(source.at[part], target.at[part], sems.at[4 + 2 * i + n])
            )
    for copy in small + pieces:
        copy.start()
    for copy in small:
        copy.wait()
    tall, wide = heads * ROW_BLOCK, cache * ROW_BLOCK
    scale = 1.0 / math.sqrt(side)
    lengths = jnp.transpose(jnp.broadcast_to(length_ref[...].astype(F32), (rows, rows)))[:, :1]
    row_in = lax.broadcasted_iota(jnp.int32, (tall, wide), 0) % ROW_BLOCK
    place = (lax.broadcasted_iota(jnp.int32, (tall, wide), 1) - cache * row_in).astype(F32)
    place = jnp.where(place < 0, 1e9, place)
    for r in range(0, rows, ROW_BLOCK):
        if r % (rows // PIECES) == 0:
            for copy in pieces[2 * (r * PIECES // rows) :][:2]:
                copy.wait()
        here = slice(r, r + ROW_BLOCK)
        cached = slice(r * cache, (r + ROW_BLOCK) * cache)
        query = jnp.concatenate(
            [q_ref[here, h * side : (h + 1) * side] for h in range(heads)], axis=0
        )
        new_key = jnp.concatenate([new_key_ref[here].astype(F32)] * heads, axis=0)
        new_value = jnp.concatenate([new_value_ref[here].astype(F32)] * heads, axis=0)
        live = place < jnp.concatenate([lengths[here]] * heads, axis=0)
        scores = lax.dot_general(query, key_ref[cached], NT, preferred_element_type=F32) * scale
        fresh = jnp.sum(query.astype(F32) * new_key, axis=1, keepdims=True) * scale
        scores = jnp.where(live, scores, -1e30)
        top = jnp.maximum(jnp.max(scores, axis=1, keepdims=True), fresh)
        raw = jnp.where(live, jnp.exp(scores - top), 0.0)
        fresh_raw = jnp.exp(fresh - top)
        inverse = 1.0 / (jnp.sum(raw, axis=1, keepdims=True) + fresh_raw)
        weights = (raw * inverse).astype(BF16)
        fresh_weight = (fresh_raw * inverse).astype(BF16).astype(F32)
        attended = jnp.dot(weights, value_ref[cached], preferred_element_type=F32)
        attended = (attended + fresh_weight * new_value).astype(BF16)
        for h in range(heads):
            out_ref[h, here, :] = attended[h * ROW_BLOCK : (h + 1) * ROW_BLOCK]


def dense_kernel(distances, count, first, *refs):
    x_ref, weight_ref = refs[:2]
    if first:
        variant_ref, holder_ref, owner_ref = refs[2:5]
        outs, slot_ref, table_ref = refs[5 : 5 + len(distances)], refs[-4], refs[-3]
    else:
        outs = refs[2 : 2 + len(distances)]
    buffers, sems = refs[-2:]
    heads, rows, side = x_ref.shape
    width = heads * side
    depth = buffers.shape[0]
    cuts = 2 if width >= 512 else 1
    piece = width // cuts

    def fetch(i):
        start = pl.multiple_of(owner_at(distances[i // cuts], count) * width, width) + i % cuts * piece
        return pltpu.make_async_copy(
            weight_ref.at[:, pl.ds(pl.multiple_of(start, piece), piece)],
            buffers.at[i % depth],
            sems.at[i % depth],
        )

    total = len(distances) * cuts
    for i in range(min(depth, total)):
        fetch(i).start()
    if first:
        slots = owner_ref.shape[0]
        variant = variant_ref[...]
        slot_row = jnp.zeros(variant.shape, jnp.int32)
        for v in range(holder_ref.shape[0]):
            slot_row = jnp.where(variant == v, holder_ref[v], slot_row)
        slot_row = (slot_row - lax.axis_index("tp") * slots).astype(F32)
        slot_ref[...] = jnp.transpose(jnp.broadcast_to(slot_row, (rows, rows))).astype(jnp.int32)
        for e in range(table_ref.shape[0]):
            table_ref[e] = -1
        for j in range(slots):

            def note(b, carry, j=j):
                e = (owner_ref[j, b] * slots + j) * CAP
                table_ref[e + jnp.where(table_ref[e] >= 0, 1, 0)] = b
                return carry

            lax.fori_loop(0, owner_ref.shape[1], note, 0)
    x = jnp.concatenate([x_ref[h] for h in range(heads)], axis=1)
    for i in range(total):
        fetch(i).wait()
        outs[i // cuts][:, i % cuts * piece : (i % cuts + 1) * piece] = jnp.dot(
            x, buffers[i % depth], preferred_element_type=F32
        )
        if i + depth < total:
            fetch(i + depth).start()


def held_blocks(distance, count, slots, heads, scale_ref, cell_ref, table_ref):
    tiles = count * heads
    owner = owner_at(distance, count)
    listed = []
    for j in range(slots):
        for c in range(CAP):
            b = table_ref[(owner * slots + j) * CAP + c]
            found = jnp.maximum(b, 0)
            cell = cell_ref[j, found]
            scale = jnp.where(b >= 0, scale_ref[j, found], 0.0)
            listed.append((j, found, scale, lax.div(cell, tiles), lax.rem(cell, tiles)))
    return listed


def fold_chunk(distance, count, chunk_ref, slot, factor_ref, values_ref, scale_ref, cell_ref,
               table_ref, low_ref):
    heads, rows, side = chunk_ref.shape
    width = heads * side
    features = jnp.concatenate([chunk_ref[h] for h in range(heads)], axis=1)
    start = pl.multiple_of(owner_at(distance, count) * width, width)
    low_ref[...] += lax.dot_general(
        features, factor_ref[:, pl.ds(start, width)], NT, preferred_element_type=F32
    )
    added = []
    for j, b, scale, row_block, column in held_blocks(
        distance, count, values_ref.shape[0], heads, scale_ref, cell_ref, table_ref
    ):
        mine = jnp.where(slot == j, 1.0, 0.0)
        product = jnp.dot(chunk_ref[row_block], values_ref[j, b], preferred_element_type=F32)
        added.append((column, product * (mine * scale)))
    return added


def fold_kernel(distances, count, first, *refs):
    chunks, refs = refs[: len(distances)], refs[len(distances) :]
    slot_ref, factor_ref, values_ref, scale_ref, cell_ref, table_ref = refs[:6]
    low_ref, block_ref = refs[-2:]
    if first:
        low_ref[...] = jnp.zeros_like(low_ref)
        block_ref[...] = jnp.zeros_like(block_ref)
    else:
        low_ref[...] = refs[6][...]
        block_ref[...] = refs[7][...]
    slot = slot_ref[...]
    for distance, chunk in zip(distances, chunks):
        for column, product in fold_chunk(distance, count, chunk, slot, factor_ref, values_ref,
                                          scale_ref, cell_ref, table_ref, low_ref):
            block_ref[column] += product


def part_for(distance, count, low, second_ref, dense_ref, block_ref, extra_ref, columns, out_ref):
    rows, width = dense_ref.shape
    side = block_ref.shape[2]
    heads = width // side
    owner = owner_at(distance, count)
    start = pl.multiple_of(owner * width, width)
    blocks = jnp.concatenate([block_ref[owner * heads + i] for i in range(heads)], axis=1)
    out_ref[...] = (
        jnp.dot(low, second_ref[:, pl.ds(start, width)], preferred_element_type=F32)
        + dense_ref[...]
        + blocks
    )
    for e, column in enumerate(columns):

        @pl.when(lax.div(column, heads) == owner)
        def _(e=e, column=column):
            place = pl.ds(pl.multiple_of(lax.rem(column, heads) * side, side), side)
            out_ref[:, place] += extra_ref[e]


def finish_kernel(distance, count, *refs):
    front_ref, back_ref, slot_ref, factor_ref, values_ref, scale_ref, cell_ref, table_ref = refs[:8]
    second_ref, low_in, block_ref = refs[8:11]
    dense_ref, low_out, extra_out, top_out, bottom_out = refs[11:16]
    chunk, low_sum, farthest = refs[-3:]
    half, rows, side = front_ref.shape
    chunk[:half] = front_ref[...]
    chunk[half:] = back_ref[...]
    low_sum[...] = low_in[...]
    slot = slot_ref[...]
    added = fold_chunk(distance, count, chunk, slot, factor_ref, values_ref, scale_ref, cell_ref,
                       table_ref, low_sum)
    for e, (_, product) in enumerate(added):
        extra_out[e] = product
    columns = [column for column, _ in added]
    low_width = low_sum.shape[1]
    rank = low_width // values_ref.shape[0]
    held = lax.broadcasted_iota(jnp.int32, (rows, low_width), 1) // rank
    slots_wide = jnp.concatenate([slot] * -(-low_width // side), axis=1)[:, :low_width]
    low = jnp.where(slots_wide == held, low_sum[...], 0.0).astype(BF16)
    low_out[...] = low
    part_for(distance, count, low, second_ref, dense_ref, block_ref, extra_out, columns, farthest)
    top_out[...] = farthest[: rows // 2].astype(BF16)
    bottom_out[...] = farthest[rows // 2 :].astype(BF16)


def part_kernel(distances, count, slots, *refs):
    low_ref, second_ref, block_ref, extra_ref, scale_ref, cell_ref, table_ref = refs[:7]
    dense_refs = refs[7 : 7 + len(distances)]
    outs = refs[7 + len(distances) :]
    heads = dense_refs[0].shape[1] // block_ref.shape[2]
    listed = held_blocks(count // 2, count, slots, heads, scale_ref, cell_ref, table_ref)
    columns = [entry[-1] for entry in listed]
    for distance, dense_ref, out in zip(distances, dense_refs, outs):
        part_for(distance, count, low_ref[...], second_ref, dense_ref, block_ref, extra_ref, columns, out)


def after(value, *others):
    return lax.optimization_barrier((value, *others))[0]


def body(
    queries, key_cache, value_cache, new_keys, new_values, lengths, request_variant, holder_slot,
    out_weight, factor_in, second_factor, block_values, block_scale, block_owner, block_cell,
):
    count = lax.axis_size("tp")
    half = count // 2
    ring = ring_order(count)
    to_right = [(ring[i], ring[(i + 1) % count]) for i in range(count)]
    to_left = [(ring[(i + 1) % count], ring[i]) for i in range(count)]
    rows, width = queries.shape
    side = key_cache.shape[3]
    cache = key_cache.shape[2]
    heads = width // side
    slots = block_values.shape[0]
    complete = out_weight.shape[1]
    low_width = slots * factor_in.shape[2]
    shape = jax.ShapeDtypeStruct

    attended = call(
        attend_kernel,
        "attend",
        shape((heads, rows, side), BF16),
        (queries, key_cache.reshape(-1, side), value_cache.reshape(-1, side), new_keys[0],
         new_values[0], lengths[None, :]),
        [ANY] * 6,
        VMEM,
        [pltpu.VMEM((rows, width), BF16), pltpu.VMEM((rows * cache, side), BF16),
         pltpu.VMEM((rows * cache, side), BF16), pltpu.VMEM((rows, side), BF16),
         pltpu.VMEM((rows, side), BF16), pltpu.VMEM((1, rows), jnp.int32),
         pltpu.SemaphoreType.DMA((4 + 2 * PIECES,))],
        limit=60,
    )

    wanted = [half]
    for distance in range(half - 1, 0, -1):
        wanted += [distance, count - distance]
    wanted += [0]
    cut = max(half - 1, 1)
    piece = width // 2 if width >= 512 else width
    streams = [pltpu.VMEM((4, width, piece), BF16), pltpu.SemaphoreType.DMA((4,))]
    dense_cost = dict(flops=rows * width * complete, moved=width * complete)
    dense = {}
    chunks = {0: attended}

    def pass_on(step, *done):
        right, left = chunks[step - 1], chunks[(count - step + 1) % count]
        if done:
            right, left = after(right, *done), after(left, *done)
        chunks[step] = lax.ppermute(right, "tp", to_left)
        chunks[count - step] = lax.ppermute(left, "tp", to_right)

    pass_on(1)
    *sums, slot, table = call(
        functools.partial(dense_kernel, wanted[:cut], count, True),
        "dense_first",
        [shape((rows, width), F32)] * cut
        + [shape((rows, rows), jnp.int32), shape((count * slots * CAP,), jnp.int32)],
        (attended, out_weight, request_variant[None, :], holder_slot, block_owner[:, :, 0]),
        [VMEM, ANY, VMEM, SMEM, SMEM],
        [VMEM] * cut + [VMEM, SMEM],
        streams,
        limit=40,
        **dense_cost,
    )
    dense.update(zip(wanted[:cut], sums))
    pass_on(2, slot)
    sums = call(
        functools.partial(dense_kernel, wanted[cut:], count, False),
        "dense_second",
        [shape((rows, width), F32)] * (count - cut),
        (after(attended, slot), out_weight),
        [VMEM, ANY],
        [VMEM] * (count - cut),
        streams,
        limit=40,
        **dense_cost,
    )
    dense.update(zip(wanted[cut:], sums))
    for step in range(3, half):
        pass_on(step, sums[0])

    factor_t = jnp.swapaxes(factor_in, 1, 2).reshape(low_width, -1)
    second = second_factor.reshape(low_width, complete)
    state = [shape((rows, low_width), F32), shape((complete // side, rows, side), F32)]
    early = [0]
    for distance in range(1, half - 1):
        early += [distance, count - distance]
    late = [half - 1, count - half + 1]
    tables = (slot, factor_t, block_values, block_scale, block_cell, table)
    table_specs = [VMEM, VMEM, VMEM, SMEM, SMEM, SMEM]
    low, blocks = call(
        functools.partial(fold_kernel, early, count, True),
        "fold_early",
        state,
        (*[chunks[d] for d in early], *tables),
        [VMEM] * len(early) + table_specs,
        [VMEM] * 2,
        flops=rows * low_width * complete,
        moved=4 * MIB,
    )
    front = lax.ppermute(after(chunks[half - 1], low)[: heads // 2], "tp", to_left)
    back = lax.ppermute(after(chunks[count - half + 1], low)[heads // 2 :], "tp", to_right)
    low, blocks = call(
        functools.partial(fold_kernel, late, count, False),
        "fold_late",
        state,
        (*[chunks[d] for d in late], *tables, low, blocks),
        [VMEM] * len(late) + table_specs + [VMEM] * 2,
        [VMEM] * 2,
        flops=rows * low_width * width * 4,
        moved=MIB,
    )
    extras = shape((slots * CAP, rows, side), F32)
    low, extra, top, bottom = call(
        functools.partial(finish_kernel, half, count),
        "finish",
        [shape((rows, low_width), BF16), extras]
        + [shape((rows // 2, width), BF16)] * 2,
        (front, back, *tables, second, low, blocks, dense[half]),
        [VMEM] * 2 + table_specs + [VMEM] * 4,
        [VMEM] * 4,
        [pltpu.VMEM((heads, rows, side), BF16), pltpu.VMEM((rows, low_width), F32),
         pltpu.VMEM((rows, width), F32)],
        flops=rows * low_width * width * 8,
        moved=2 * MIB,
    )

    def parts_for(pair, low):
        sums = call(
            functools.partial(part_kernel, pair, count, slots),
            "part",
            [shape((rows, width), F32)] * len(pair),
            (low, second, blocks, extra, block_scale, block_cell, table, *[dense[d] for d in pair]),
            [VMEM] * 4 + [SMEM] * 3 + [VMEM] * len(pair),
            [VMEM] * len(pair),
            flops=rows * low_width * width * 4,
            moved=2 * MIB,
        )
        return sums

    left = lax.ppermute(top, "tp", to_left)
    right = lax.ppermute(bottom, "tp", to_right)
    if half > 1:
        other, mine = parts_for([half - 1, count - half + 1], low)
    for distance in range(half - 1, 0, -1):
        if distance == half - 1:
            none = jnp.zeros_like(left)
            left = jnp.concatenate([left, none], axis=0)
            right = jnp.concatenate([none, right], axis=0)
        sent_left = (mine + left.astype(F32)).astype(BF16)
        sent_right = (other + right.astype(F32)).astype(BF16)
        if distance > 1:
            other, mine = parts_for([distance - 1, count - distance + 1], after(low, sent_right))
        else:
            (own,) = parts_for([0], after(low, sent_right))
        left = lax.ppermute(sent_left, "tp", to_left)
        right = lax.ppermute(sent_right, "tp", to_right)
    return (own + left.astype(F32) + right.astype(F32)).astype(BF16)


def solution(mesh):
    return jax.shard_map(
        body,
        mesh=mesh,
        in_specs=(
            P(("groups", "rep"), "tp"),
            P("tp", ("groups", "rep"), None, None),
            P("tp", ("groups", "rep"), None, None),
            P("tp", ("groups", "rep"), None),
            P("tp", ("groups", "rep"), None),
            P(("groups", "rep")),
            P(("groups", "rep")),
            P(),
            P("tp", None),
            P("tp", None, None),
            P("tp", None, None),
            P("tp", None, None, None),
            P("tp", None),
            P("tp", None, None),
            P("tp", None),
        ),
        out_specs=P(("groups", "rep"), "tp"),
        check_vma=False,
    )
```

```python
import functools
import math

import jax
import jax.numpy as jnp
from jax import lax
from jax.experimental import pallas as pl
from jax.experimental.pallas import tpu as pltpu
from jax.sharding import PartitionSpec as P

BF16 = jnp.bfloat16
F32 = jnp.float32
CAP = 2
ROW_BLOCK = 16
PIECES = 4
MIB = 1024 * 1024
NT = (((1,), (1,)), ((), ()))
VMEM = pl.BlockSpec(memory_space=pltpu.VMEM)
SMEM = pl.BlockSpec(memory_space=pltpu.SMEM)
ANY = pl.BlockSpec(memory_space=pl.ANY)


def ring_order(count):
    if count == 8:
        return [0, 2, 4, 6, 7, 5, 3, 1]
    return list(range(count))


def owner_at(distance, count):
    me = lax.axis_index("tp")
    if count != 8:
        return lax.rem(me + distance, count)
    spot = jnp.where((me & 1) == 0, me >> 1, count - 1 - (me >> 1))
    spot = lax.rem(spot + distance, count)
    return jnp.where(spot < count // 2, 2 * spot, 2 * (count - 1 - spot) + 1)


def call(kernel, name, outs, ins, specs, out_specs, scratch=(), limit=16, flops=0, moved=0):
    return pl.pallas_call(
        kernel,
        out_shape=outs,
        in_specs=specs,
        out_specs=out_specs,
        scratch_shapes=list(scratch),
        compiler_params=pltpu.CompilerParams(vmem_limit_bytes=limit * MIB),
        cost_estimate=pl.CostEstimate(flops=flops, bytes_accessed=moved, transcendentals=0),
        name=name,
    )(*ins)


def attend_kernel(
    query_hbm, key_hbm, value_hbm, new_key_hbm, new_value_hbm, length_hbm, out_ref,
    q_ref, key_ref, value_ref, new_key_ref, new_value_ref, length_ref, sems,
):
    heads, rows, side = out_ref.shape
    cache = key_ref.shape[0] // rows
    small = [
        pltpu.make_async_copy(source, target, sems.at[i])
        for i, (source, target) in enumerate(
            ((length_hbm, length_ref), (query_hbm, q_ref), (new_key_hbm, new_key_ref),
             (new_value_hbm, new_value_ref))
        )
    ]
    tall_piece = key_ref.shape[0] // PIECES
    pieces = []
    for i in range(PIECES):
        for n, (source, target) in enumerate(((key_hbm, key_ref), (value_hbm, value_ref))):
            part = pl.ds(i * tall_piece, tall_piece)
            pieces.append(
                pltpu.make_async_copy(source.at[part], target.at[part], sems.at[4 + 2 * i + n])
            )
    for copy in small + pieces:
        copy.start()
    for copy in small:
        copy.wait()
    tall, wide = heads * ROW_BLOCK, cache * ROW_BLOCK
    scale = math.log2(math.e) / math.sqrt(side)
    lengths = jnp.transpose(jnp.broadcast_to(length_ref[...].astype(F32), (rows, rows)))[:, :1]
    row_in = lax.broadcasted_iota(jnp.int32, (tall, wide), 0) % ROW_BLOCK
    place = (lax.broadcasted_iota(jnp.int32, (tall, wide), 1) - cache * row_in).astype(F32)
    place = jnp.where(place < 0, 1e9, place)
    for r in range(0, rows, ROW_BLOCK):
        if r % (rows // PIECES) == 0:
            for copy in pieces[2 * (r * PIECES // rows) :][:2]:
                copy.wait()
        here = slice(r, r + ROW_BLOCK)
        cached = slice(r * cache, (r + ROW_BLOCK) * cache)
        query = jnp.concatenate(
            [q_ref[here, h * side : (h + 1) * side] for h in range(heads)], axis=0
        )
        new_key = jnp.concatenate([new_key_ref[here].astype(F32)] * heads, axis=0)
        new_value = jnp.concatenate([new_value_ref[here].astype(F32)] * heads, axis=0)
        live = place < jnp.concatenate([lengths[here]] * heads, axis=0)
        scores = lax.dot_general(query, key_ref[cached], NT, preferred_element_type=F32)
        fresh = jnp.sum(query.astype(F32) * new_key, axis=1, keepdims=True)
        scores = jnp.where(live, scores, -jnp.inf)
        top = jnp.maximum(jnp.max(scores, axis=1, keepdims=True), fresh)
        raw = jnp.exp2((scores - top) * scale)
        fresh_raw = jnp.exp2((fresh - top) * scale)
        inverse = 1.0 / (jnp.sum(raw, axis=1, keepdims=True) + fresh_raw)
        attended = jnp.dot(raw.astype(BF16), value_ref[cached], preferred_element_type=F32)
        attended = ((attended + fresh_raw * new_value) * inverse).astype(BF16)
        for h in range(heads):
            out_ref[h, here, :] = attended[h * ROW_BLOCK : (h + 1) * ROW_BLOCK]


def dense_kernel(distances, count, listing, *refs):
    x_hbm, weight_ref = refs[:2]
    if listing:
        variant_ref, holder_ref, owner_ref = refs[2:5]
        outs, slot_ref, table_ref = refs[5 : 5 + len(distances)], refs[-6], refs[-5]
    else:
        outs = refs[2 : 2 + len(distances)]
    x_ref, buffers, sems, x_sem = refs[-4:]
    heads, rows, side = x_hbm.shape
    width = heads * side
    depth = buffers.shape[0]
    piece = buffers.shape[2]
    cuts = width // piece

    def fetch(i):
        start = pl.multiple_of(owner_at(distances[i // cuts], count) * width, width) + i % cuts * piece
        return pltpu.make_async_copy(
            weight_ref.at[:, pl.ds(pl.multiple_of(start, piece), piece)],
            buffers.at[i % depth],
            sems.at[i % depth],
        )

    own = pltpu.make_async_copy(x_hbm, x_ref, x_sem)
    own.start()
    total = len(distances) * cuts
    for i in range(min(depth, total)):
        fetch(i).start()
    if listing:
        slots = owner_ref.shape[0]
        variant = variant_ref[...]
        slot_row = jnp.zeros(variant.shape, jnp.int32)
        for v in range(holder_ref.shape[0]):
            slot_row = jnp.where(variant == v, holder_ref[v], slot_row)
        slot_row = (slot_row - lax.axis_index("tp") * slots).astype(F32)
        slot_ref[...] = jnp.transpose(jnp.broadcast_to(slot_row, (rows, rows))).astype(jnp.int32)
        for e in range(table_ref.shape[0]):
            table_ref[e] = -1
        for j in range(slots):

            def note(b, carry, j=j):
                e = (owner_ref[j, b] * slots + j) * CAP
                table_ref[e + jnp.where(table_ref[e] >= 0, 1, 0)] = b
                return carry

            lax.fori_loop(0, owner_ref.shape[1], note, 0)
    own.wait()
    x = jnp.concatenate([x_ref[h] for h in range(heads)], axis=1)
    for i in range(total):
        fetch(i).wait()
        outs[i // cuts][:, i % cuts * piece : (i % cuts + 1) * piece] = jnp.dot(
            x, buffers[i % depth], preferred_element_type=F32
        )
        if i + depth < total:
            fetch(i + depth).start()


def held_blocks(distance, count, slots, heads, scale_ref, cell_ref, table_ref):
    tiles = count * heads
    owner = owner_at(distance, count)
    listed = []
    for j in range(slots):
        for c in range(CAP):
            b = table_ref[(owner * slots + j) * CAP + c]
            found = jnp.maximum(b, 0)
            cell = cell_ref[j, found]
            scale = jnp.where(b >= 0, scale_ref[j, found], 0.0)
            listed.append((j, found, scale, lax.div(cell, tiles), lax.rem(cell, tiles)))
    return listed


def fold_chunk(distance, count, chunk_ref, slot, factor_ref, values_ref, scale_ref, cell_ref,
               table_ref, low_ref):
    heads, rows, side = chunk_ref.shape
    width = heads * side
    features = jnp.concatenate([chunk_ref[h] for h in range(heads)], axis=1)
    start = pl.multiple_of(owner_at(distance, count) * width, width)
    low_ref[...] += lax.dot_general(
        features, factor_ref[:, pl.ds(start, width)], NT, preferred_element_type=F32
    )
    added = []
    for j, b, scale, row_block, column in held_blocks(
        distance, count, values_ref.shape[0], heads, scale_ref, cell_ref, table_ref
    ):
        mine = jnp.where(slot == j, 1.0, 0.0)
        product = jnp.dot(chunk_ref[row_block], values_ref[j, b], preferred_element_type=F32)
        added.append((column, product * (mine * scale)))
    return added


def fold_kernel(distances, count, first, *refs):
    chunks, refs = refs[: len(distances)], refs[len(distances) :]
    slot_ref, factor_ref, values_ref, scale_ref, cell_ref, table_ref = refs[:6]
    low_ref, block_ref = refs[-2:]
    if first:
        low_ref[...] = jnp.zeros_like(low_ref)
        block_ref[...] = jnp.zeros_like(block_ref)
    else:
        low_ref[...] = refs[6][...]
        block_ref[...] = refs[7][...]
    slot = slot_ref[...]
    for distance, chunk in zip(distances, chunks):
        for column, product in fold_chunk(distance, count, chunk, slot, factor_ref, values_ref,
                                          scale_ref, cell_ref, table_ref, low_ref):
            block_ref[column] += product


def part_for(distance, count, low_ref, second_ref, dense_ref, block_ref, extra_ref, columns, rows,
             out_ref):
    width = dense_ref.shape[1]
    side = block_ref.shape[2]
    heads = width // side
    owner = owner_at(distance, count)
    start = pl.multiple_of(owner * width, width)
    blocks = jnp.concatenate([block_ref[owner * heads + i, rows] for i in range(heads)], axis=1)
    out_ref[...] = (
        jnp.dot(low_ref[rows], second_ref[:, pl.ds(start, width)], preferred_element_type=F32)
        + dense_ref[rows]
        + blocks
    )
    for e, column in enumerate(columns):

        @pl.when(lax.div(column, heads) == owner)
        def _(e=e, column=column):
            place = pl.ds(pl.multiple_of(lax.rem(column, heads) * side, side), side)
            out_ref[:, place] += extra_ref[e, rows]


def finish_kernel(distance, count, *refs):
    front_ref, back_ref, slot_ref, factor_ref, values_ref, scale_ref, cell_ref, table_ref = refs[:8]
    second_ref, low_in, block_ref = refs[8:11]
    dense_ref, low_out, extra_out, top_out, bottom_out = refs[11:16]
    chunk, low_sum, farthest = refs[-3:]
    half, rows, side = front_ref.shape
    chunk[:half] = front_ref[...]
    chunk[half:] = back_ref[...]
    low_sum[...] = low_in[...]
    slot = slot_ref[...]
    added = fold_chunk(distance, count, chunk, slot, factor_ref, values_ref, scale_ref, cell_ref,
                       table_ref, low_sum)
    for e, (_, product) in enumerate(added):
        extra_out[e] = product
    columns = [column for column, _ in added]
    low_width = low_sum.shape[1]
    rank = low_width // values_ref.shape[0]
    held = lax.broadcasted_iota(jnp.int32, (rows, low_width), 1) // rank
    slots_wide = jnp.concatenate([slot] * -(-low_width // side), axis=1)[:, :low_width]
    low = jnp.where(slots_wide == held, low_sum[...], 0.0).astype(BF16)
    low_out[...] = low
    part_for(distance, count, low_out, second_ref, dense_ref, block_ref, extra_out, columns,
             slice(0, rows), farthest)
    top_out[...] = farthest[: rows // 2].astype(BF16)
    bottom_out[...] = farthest[rows // 2 :].astype(BF16)


def join_kernel(jobs, count, slots, *refs):
    low_ref, second_ref, block_ref, extra_ref, scale_ref, cell_ref, table_ref = refs[:7]
    dense_refs, refs = refs[7 : 7 + len(jobs)], refs[7 + len(jobs) :]
    came, outs, totals = refs[: -2 * len(jobs)], refs[-2 * len(jobs) : -len(jobs)], refs[-len(jobs) :]
    rows, width = dense_refs[0].shape
    heads = width // block_ref.shape[2]
    listed = held_blocks(count // 2, count, slots, heads, scale_ref, cell_ref, table_ref)
    columns = [entry[-1] for entry in listed]
    for n, (distance, half) in enumerate(jobs):
        here = slice(half * rows // 2, (half + 1) * rows // 2)
        part_for(distance, count, low_ref, second_ref, dense_refs[n], block_ref, extra_ref, columns,
                 here, totals[n])
        total = totals[n][...]
        if came:
            total = total + came[n][...].astype(F32)
        outs[n][...] = total.astype(outs[n].dtype)


def sum_kernel(upper_ref, lower_ref, *refs):
    out_ref = refs[-1]
    cut = upper_ref.shape[0]
    upper, lower = upper_ref[...], lower_ref[...]
    for n, ref in enumerate(refs[:-1]):
        if n in (0, 2):
            upper = upper + ref[...].astype(F32)
        else:
            lower = lower + ref[...].astype(F32)
    out_ref[:cut] = upper.astype(BF16)
    out_ref[cut:] = lower.astype(BF16)


def after(value, *others):
    return lax.optimization_barrier((value, *others))[0]


def body(
    queries, key_cache, value_cache, new_keys, new_values, lengths, request_variant, holder_slot,
    out_weight, factor_in, second_factor, block_values, block_scale, block_owner, block_cell,
):
    count = lax.axis_size("tp")
    half = count // 2
    ring = ring_order(count)
    to_right = [(ring[i], ring[(i + 1) % count]) for i in range(count)]
    to_left = [(ring[(i + 1) % count], ring[i]) for i in range(count)]
    rows, width = queries.shape
    side = key_cache.shape[3]
    cache = key_cache.shape[2]
    heads = width // side
    slots = block_values.shape[0]
    complete = out_weight.shape[1]
    low_width = slots * factor_in.shape[2]
    shape = jax.ShapeDtypeStruct

    attended = call(
        attend_kernel,
        "attend",
        shape((heads, rows, side), BF16),
        (queries, key_cache.reshape(-1, side), value_cache.reshape(-1, side), new_keys[0],
         new_values[0], lengths[None, :]),
        [ANY] * 6,
        VMEM,
        [pltpu.VMEM((rows, width), BF16), pltpu.VMEM((rows * cache, side), BF16),
         pltpu.VMEM((rows * cache, side), BF16), pltpu.VMEM((rows, side), BF16),
         pltpu.VMEM((rows, side), BF16), pltpu.VMEM((1, rows), jnp.int32),
         pltpu.SemaphoreType.DMA((4 + 2 * PIECES,))],
        limit=60,
    )

    wanted = [half]
    for distance in range(half - 1, 0, -1):
        wanted += [distance, count - distance]
    wanted += [0]
    piece = width // 2 if width >= 512 else width
    dense = {}

    def dense_for(distances, x, listing=False):
        extra_shapes = [shape((rows, rows), jnp.int32), shape((count * slots * CAP,), jnp.int32)]
        extra_ins = (request_variant[None, :], holder_slot, block_owner[:, :, 0])
        got = call(
            functools.partial(dense_kernel, distances, count, listing),
            "dense",
            [shape((rows, width), F32)] * len(distances) + extra_shapes * listing,
            (x, out_weight) + extra_ins * listing,
            [ANY, ANY] + [VMEM, SMEM, SMEM] * listing,
            [VMEM] * len(distances) + [VMEM, SMEM] * listing,
            [pltpu.VMEM((heads, rows, side), BF16), pltpu.VMEM((4, width, piece), BF16),
             pltpu.SemaphoreType.DMA((4,)), pltpu.SemaphoreType.DMA],
            limit=40,
            flops=2 * rows * width * width * len(distances),
            moved=2 * width * width * len(distances),
        )
        dense.update(zip(distances, got))
        return got[len(distances) :] if listing else got[0]

    chunks = {0: attended}

    def pass_on(step, *done):
        right, left = chunks[step - 1], chunks[(count - step + 1) % count]
        if done:
            right, left = after(right, *done), after(left, *done)
        chunks[step] = lax.ppermute(right, "tp", to_left)
        chunks[count - step] = lax.ppermute(left, "tp", to_right)

    third = -(-3 * count // 8)
    pass_on(1)
    token = dense_for(wanted[:third], attended)
    pass_on(2, token)
    slot, table = dense_for(wanted[third : 2 * third], after(attended, token), True)
    for step in range(3, half):
        pass_on(step, slot)
    token = dense_for(wanted[2 * third :], after(attended, slot))

    factor_t = jnp.swapaxes(factor_in, 1, 2).reshape(low_width, -1)
    second = second_factor.reshape(low_width, complete)
    state = [shape((rows, low_width), F32), shape((complete // side, rows, side), F32)]
    early = [0]
    for distance in range(1, half - 1):
        early += [distance, count - distance]
    late = [half - 1, count - half + 1]
    tables = (slot, factor_t, block_values, block_scale, block_cell, table)
    table_specs = [VMEM, VMEM, VMEM, SMEM, SMEM, SMEM]
    low, blocks = call(
        functools.partial(fold_kernel, early, count, True),
        "fold_early",
        state,
        (*[chunks[d] for d in early], *tables),
        [VMEM] * len(early) + table_specs,
        [VMEM] * 2,
        flops=rows * low_width * complete,
        moved=4 * MIB,
    )
    front = lax.ppermute(after(chunks[half - 1], low, token)[: heads // 2], "tp", to_left)
    back = lax.ppermute(after(chunks[count - half + 1], low, token)[heads // 2 :], "tp", to_right)
    low, blocks = call(
        functools.partial(fold_kernel, late, count, False),
        "fold_late",
        state,
        (*[chunks[d] for d in late], *tables, low, blocks),
        [VMEM] * len(late) + table_specs + [VMEM] * 2,
        [VMEM] * 2,
        flops=rows * low_width * width * 4,
        moved=MIB,
    )
    extras = shape((slots * CAP, rows, side), F32)
    low, extra, top, bottom = call(
        functools.partial(finish_kernel, half, count),
        "finish",
        [shape((rows, low_width), BF16), extras]
        + [shape((rows // 2, width), BF16)] * 2,
        (front, back, *tables, second, low, blocks, dense[half]),
        [VMEM] * 2 + table_specs + [VMEM] * 4,
        [VMEM] * 4,
        [pltpu.VMEM((heads, rows, side), BF16), pltpu.VMEM((rows, low_width), F32),
         pltpu.VMEM((rows, width), F32)],
        flops=rows * low_width * width * 8,
        moved=2 * MIB,
    )

    def join(jobs, came, low, kind=BF16):
        return call(
            functools.partial(join_kernel, jobs, count, slots),
            "join",
            [shape((rows // 2, width), kind)] * len(jobs),
            (low, second, blocks, extra, block_scale, block_cell, table,
             *[dense[distance] for distance, _ in jobs], *came),
            [VMEM] * 4 + [SMEM] * 3 + [VMEM] * (len(jobs) + len(came)),
            [VMEM] * len(jobs),
            [pltpu.VMEM((rows // 2, width), F32)] * len(jobs),
            flops=rows * low_width * width * 2,
            moved=MIB,
        )

    far, near = (top, bottom), ()
    for distance in range(half, 0, -1):
        if distance < half:
            far = join([(count - distance, 0), (distance, 1)], far, low)
        ready = far
        far = [lax.ppermute(far[0], "tp", to_left), lax.ppermute(far[1], "tp", to_right)]
        if distance > 1:
            near = join([(count - distance + 1, 1), (distance - 1, 0)], near, low)
            near = [lax.ppermute(near[0], "tp", to_left), lax.ppermute(near[1], "tp", to_right)]
    own = join([(0, 0), (0, 1)], (), after(low, *ready), F32)
    up_left, low_right = far
    if half > 1:
        low_left, up_right = near
    came = [up_left, low_right] if half == 1 else [up_left, low_right, up_right, low_left]
    return call(
        sum_kernel,
        "sum_up",
        shape((rows, width), BF16),
        (*own, *came),
        [VMEM] * (2 + len(came)),
        VMEM,
        flops=1,
        moved=1,
    )


def solution(mesh):
    return jax.shard_map(
        body,
        mesh=mesh,
        in_specs=(
            P(("groups", "rep"), "tp"),
            P("tp", ("groups", "rep"), None, None),
            P("tp", ("groups", "rep"), None, None),
            P("tp", ("groups", "rep"), None),
            P("tp", ("groups", "rep"), None),
            P(("groups", "rep")),
            P(("groups", "rep")),
            P(),
            P("tp", None),
            P("tp", None, None),
            P("tp", None, None),
            P("tp", None, None, None),
            P("tp", None),
            P("tp", None, None),
            P("tp", None),
        ),
        out_specs=P(("groups", "rep"), "tp"),
        check_vma=False,
    )
```

```python
import functools
import math

import jax
import jax.numpy as jnp
from jax import lax
from jax.experimental import pallas as pl
from jax.experimental.pallas import tpu as pltpu
from jax.sharding import PartitionSpec as P

BF16 = jnp.bfloat16
F32 = jnp.float32
CAP = 2
ROW_BLOCK = 16
PIECES = 4
MIB = 1024 * 1024
NT = (((1,), (1,)), ((), ()))
VMEM = pl.BlockSpec(memory_space=pltpu.VMEM)
SMEM = pl.BlockSpec(memory_space=pltpu.SMEM)
ANY = pl.BlockSpec(memory_space=pl.ANY)


def ring_order(count):
    if count == 8:
        return [0, 2, 4, 6, 7, 5, 3, 1]
    return list(range(count))


def owner_at(distance, count):
    me = lax.axis_index("tp")
    if count != 8:
        return lax.rem(me + distance, count)
    spot = jnp.where((me & 1) == 0, me >> 1, count - 1 - (me >> 1))
    spot = lax.rem(spot + distance, count)
    return jnp.where(spot < count // 2, 2 * spot, 2 * (count - 1 - spot) + 1)


def call(kernel, name, outs, ins, specs, out_specs, scratch=(), limit=16, flops=0, moved=0):
    return pl.pallas_call(
        kernel,
        out_shape=outs,
        in_specs=specs,
        out_specs=out_specs,
        scratch_shapes=list(scratch),
        compiler_params=pltpu.CompilerParams(vmem_limit_bytes=limit * MIB),
        cost_estimate=pl.CostEstimate(flops=flops, bytes_accessed=moved, transcendentals=0),
        name=name,
    )(*ins)


def attend_kernel(
    query_hbm, key_hbm, value_hbm, new_key_hbm, new_value_hbm, length_hbm, out_ref,
    q_ref, key_ref, value_ref, new_key_ref, new_value_ref, length_ref, sems,
):
    heads, rows, side = out_ref.shape
    cache = key_ref.shape[0] // rows
    small = [
        pltpu.make_async_copy(source, target, sems.at[i])
        for i, (source, target) in enumerate(
            ((length_hbm, length_ref), (query_hbm, q_ref), (new_key_hbm, new_key_ref),
             (new_value_hbm, new_value_ref))
        )
    ]
    tall_piece = key_ref.shape[0] // PIECES
    pieces = []
    for i in range(PIECES):
        for n, (source, target) in enumerate(((key_hbm, key_ref), (value_hbm, value_ref))):
            part = pl.ds(i * tall_piece, tall_piece)
            pieces.append(
                pltpu.make_async_copy(source.at[part], target.at[part], sems.at[4 + 2 * i + n])
            )
    for copy in small + pieces:
        copy.start()
    for copy in small:
        copy.wait()
    tall, wide = heads * ROW_BLOCK, cache * ROW_BLOCK
    scale = math.log2(math.e) / math.sqrt(side)
    lengths = jnp.transpose(jnp.broadcast_to(length_ref[...].astype(F32), (rows, rows)))[:, :1]
    row_in = lax.broadcasted_iota(jnp.int32, (tall, wide), 0) % ROW_BLOCK
    place = (lax.broadcasted_iota(jnp.int32, (tall, wide), 1) - cache * row_in).astype(F32)
    place = jnp.where(place < 0, 1e9, place)
    for r in range(0, rows, ROW_BLOCK):
        if r % (rows // PIECES) == 0:
            for copy in pieces[2 * (r * PIECES // rows) :][:2]:
                copy.wait()
        here = slice(r, r + ROW_BLOCK)
        cached = slice(r * cache, (r + ROW_BLOCK) * cache)
        query = jnp.concatenate(
            [q_ref[here, h * side : (h + 1) * side] for h in range(heads)], axis=0
        )
        new_key = jnp.concatenate([new_key_ref[here].astype(F32)] * heads, axis=0)
        new_value = jnp.concatenate([new_value_ref[here].astype(F32)] * heads, axis=0)
        live = place < jnp.concatenate([lengths[here]] * heads, axis=0)
        scores = lax.dot_general(query, key_ref[cached], NT, preferred_element_type=F32)
        fresh = jnp.sum(query.astype(F32) * new_key, axis=1, keepdims=True)
        scores = jnp.where(live, scores, -jnp.inf)
        top = jnp.maximum(jnp.max(scores, axis=1, keepdims=True), fresh)
        raw = jnp.exp2((scores - top) * scale)
        fresh_raw = jnp.exp2((fresh - top) * scale)
        inverse = 1.0 / (jnp.sum(raw, axis=1, keepdims=True) + fresh_raw)
        attended = jnp.dot(raw.astype(BF16), value_ref[cached], preferred_element_type=F32)
        attended = ((attended + fresh_raw * new_value) * inverse).astype(BF16)
        for h in range(heads):
            out_ref[h, here, :] = attended[h * ROW_BLOCK : (h + 1) * ROW_BLOCK]


def dense_kernel(distances, count, listing, *refs):
    x_ref, weight_ref = refs[:2]
    if listing:
        variant_ref, holder_ref, owner_ref = refs[2:5]
        outs, slot_ref, table_ref = refs[5 : 5 + len(distances)], refs[-4], refs[-3]
    else:
        outs = refs[2 : 2 + len(distances)]
    buffers, sems = refs[-2:]
    heads, rows, side = x_ref.shape
    width = heads * side
    depth = buffers.shape[0]
    piece = buffers.shape[2]
    cuts = width // piece

    def fetch(i):
        start = pl.multiple_of(owner_at(distances[i // cuts], count) * width, width) + i % cuts * piece
        return pltpu.make_async_copy(
            weight_ref.at[:, pl.ds(pl.multiple_of(start, piece), piece)],
            buffers.at[i % depth],
            sems.at[i % depth],
        )

    total = len(distances) * cuts
    for i in range(min(depth, total)):
        fetch(i).start()
    if listing:
        slots = owner_ref.shape[0]
        variant = variant_ref[...]
        slot_row = jnp.zeros(variant.shape, jnp.int32)
        for v in range(holder_ref.shape[0]):
            slot_row = jnp.where(variant == v, holder_ref[v], slot_row)
        slot_row = (slot_row - lax.axis_index("tp") * slots).astype(F32)
        slot_ref[...] = jnp.transpose(jnp.broadcast_to(slot_row, (rows, rows))).astype(jnp.int32)
        for e in range(table_ref.shape[0]):
            table_ref[e] = -1
        for j in range(slots):

            def note(b, carry, j=j):
                e = (owner_ref[j, b] * slots + j) * CAP
                table_ref[e + jnp.where(table_ref[e] >= 0, 1, 0)] = b
                return carry

            lax.fori_loop(0, owner_ref.shape[1], note, 0)
    x = jnp.concatenate([x_ref[h] for h in range(heads)], axis=1)
    for i in range(total):
        fetch(i).wait()
        outs[i // cuts][:, i % cuts * piece : (i % cuts + 1) * piece] = jnp.dot(
            x, buffers[i % depth], preferred_element_type=F32
        )
        if i + depth < total:
            fetch(i + depth).start()


def held_blocks(distance, count, slots, heads, scale_ref, cell_ref, table_ref):
    tiles = count * heads
    owner = owner_at(distance, count)
    listed = []
    for j in range(slots):
        for c in range(CAP):
            b = table_ref[(owner * slots + j) * CAP + c]
            found = jnp.maximum(b, 0)
            cell = cell_ref[j, found]
            scale = jnp.where(b >= 0, scale_ref[j, found], 0.0)
            listed.append((j, found, scale, lax.div(cell, tiles), lax.rem(cell, tiles)))
    return listed


def fold_chunk(distance, count, chunk_ref, slot, factor_ref, values_ref, scale_ref, cell_ref,
               table_ref, low_ref):
    heads, rows, side = chunk_ref.shape
    width = heads * side
    features = jnp.concatenate([chunk_ref[h] for h in range(heads)], axis=1)
    start = pl.multiple_of(owner_at(distance, count) * width, width)
    low_ref[...] += lax.dot_general(
        features, factor_ref[:, pl.ds(start, width)], NT, preferred_element_type=F32
    )
    added = []
    for j, b, scale, row_block, column in held_blocks(
        distance, count, values_ref.shape[0], heads, scale_ref, cell_ref, table_ref
    ):
        mine = jnp.where(slot == j, 1.0, 0.0)
        product = jnp.dot(chunk_ref[row_block], values_ref[j, b], preferred_element_type=F32)
        added.append((column, product * (mine * scale)))
    return added


def fold_kernel(distances, count, first, *refs):
    chunks, refs = refs[: len(distances)], refs[len(distances) :]
    slot_ref, factor_ref, values_ref, scale_ref, cell_ref, table_ref = refs[:6]
    low_ref, block_ref = refs[-2:]
    if first:
        low_ref[...] = jnp.zeros_like(low_ref)
        block_ref[...] = jnp.zeros_like(block_ref)
    else:
        low_ref[...] = refs[6][...]
        block_ref[...] = refs[7][...]
    slot = slot_ref[...]
    for distance, chunk in zip(distances, chunks):
        for column, product in fold_chunk(distance, count, chunk, slot, factor_ref, values_ref,
                                          scale_ref, cell_ref, table_ref, low_ref):
            block_ref[column] += product


def part_for(distance, count, low_ref, second_ref, dense_ref, block_ref, extra_ref, columns, rows,
             out_ref):
    width = dense_ref.shape[1]
    side = block_ref.shape[2]
    heads = width // side
    owner = owner_at(distance, count)
    start = pl.multiple_of(owner * width, width)
    blocks = jnp.concatenate([block_ref[owner * heads + i, rows] for i in range(heads)], axis=1)
    out_ref[...] = (
        jnp.dot(low_ref[rows], second_ref[:, pl.ds(start, width)], preferred_element_type=F32)
        + dense_ref[rows]
        + blocks
    )
    for e, column in enumerate(columns):

        @pl.when(lax.div(column, heads) == owner)
        def _(e=e, column=column):
            place = pl.ds(pl.multiple_of(lax.rem(column, heads) * side, side), side)
            out_ref[:, place] += extra_ref[e, rows]


def finish_kernel(distance, count, *refs):
    front_ref, back_ref, slot_ref, factor_ref, values_ref, scale_ref, cell_ref, table_ref = refs[:8]
    second_ref, low_in, block_ref = refs[8:11]
    dense_ref, low_out, extra_out, top_out, bottom_out = refs[11:16]
    chunk, low_sum, farthest = refs[-3:]
    half, rows, side = front_ref.shape
    chunk[:half] = front_ref[...]
    chunk[half:] = back_ref[...]
    low_sum[...] = low_in[...]
    slot = slot_ref[...]
    added = fold_chunk(distance, count, chunk, slot, factor_ref, values_ref, scale_ref, cell_ref,
                       table_ref, low_sum)
    for e, (_, product) in enumerate(added):
        extra_out[e] = product
    columns = [column for column, _ in added]
    low_width = low_sum.shape[1]
    rank = low_width // values_ref.shape[0]
    held = lax.broadcasted_iota(jnp.int32, (rows, low_width), 1) // rank
    slots_wide = jnp.concatenate([slot] * -(-low_width // side), axis=1)[:, :low_width]
    low = jnp.where(slots_wide == held, low_sum[...], 0.0).astype(BF16)
    low_out[...] = low
    part_for(distance, count, low_out, second_ref, dense_ref, block_ref, extra_out, columns,
             slice(0, rows), farthest)
    for i in range(2 * half):
        tile = farthest[:, i * side : (i + 1) * side].astype(BF16)
        top_out[i] = tile[: rows // 2]
        bottom_out[i] = tile[rows // 2 :]


def join_kernel(jobs, count, slots, *refs):
    low_ref, second_ref, block_ref, extra_ref, scale_ref, cell_ref, table_ref = refs[:7]
    dense_refs, refs = refs[7 : 7 + len(jobs)], refs[7 + len(jobs) :]
    came, outs, totals = refs[: -2 * len(jobs)], refs[-2 * len(jobs) : -len(jobs)], refs[-len(jobs) :]
    rows, width = dense_refs[0].shape
    heads = width // block_ref.shape[2]
    listed = held_blocks(count // 2, count, slots, heads, scale_ref, cell_ref, table_ref)
    columns = [entry[-1] for entry in listed]
    for n, (distance, half) in enumerate(jobs):
        here = slice(half * rows // 2, (half + 1) * rows // 2)
        part_for(distance, count, low_ref, second_ref, dense_refs[n], block_ref, extra_ref, columns,
                 here, totals[n])
        side = width // heads
        for i in range(heads):
            total = totals[n][:, i * side : (i + 1) * side]
            if came:
                total = total + came[n][i].astype(F32)
            outs[n][i] = total.astype(outs[n].dtype)


def sum_kernel(upper_ref, lower_ref, *refs):
    out_ref = refs[-1]
    heads, cut, side = upper_ref.shape
    for i in range(heads):
        upper, lower = upper_ref[i], lower_ref[i]
        for n, ref in enumerate(refs[:-1]):
            if n in (0, 2):
                upper = upper + ref[i].astype(F32)
            else:
                lower = lower + ref[i].astype(F32)
        out_ref[:cut, i * side : (i + 1) * side] = upper.astype(BF16)
        out_ref[cut:, i * side : (i + 1) * side] = lower.astype(BF16)


def after(value, *others):
    return lax.optimization_barrier((value, *others))[0]


def body(
    queries, key_cache, value_cache, new_keys, new_values, lengths, request_variant, holder_slot,
    out_weight, factor_in, second_factor, block_values, block_scale, block_owner, block_cell,
):
    count = lax.axis_size("tp")
    half = count // 2
    ring = ring_order(count)
    to_right = [(ring[i], ring[(i + 1) % count]) for i in range(count)]
    to_left = [(ring[(i + 1) % count], ring[i]) for i in range(count)]
    rows, width = queries.shape
    side = key_cache.shape[3]
    cache = key_cache.shape[2]
    heads = width // side
    slots = block_values.shape[0]
    complete = out_weight.shape[1]
    low_width = slots * factor_in.shape[2]
    shape = jax.ShapeDtypeStruct

    attended = call(
        attend_kernel,
        "attend",
        shape((heads, rows, side), BF16),
        (queries, key_cache.reshape(-1, side), value_cache.reshape(-1, side), new_keys[0],
         new_values[0], lengths[None, :]),
        [ANY] * 6,
        VMEM,
        [pltpu.VMEM((rows, width), BF16), pltpu.VMEM((rows * cache, side), BF16),
         pltpu.VMEM((rows * cache, side), BF16), pltpu.VMEM((rows, side), BF16),
         pltpu.VMEM((rows, side), BF16), pltpu.VMEM((1, rows), jnp.int32),
         pltpu.SemaphoreType.DMA((4 + 2 * PIECES,))],
        limit=60,
    )

    wanted = [half]
    for distance in range(half - 1, 0, -1):
        wanted += [distance, count - distance]
    wanted += [0]
    piece = width // 2 if width >= 512 else width
    dense = {}

    def dense_for(distances, x, listing=False):
        extra_shapes = [shape((rows, rows), jnp.int32), shape((count * slots * CAP,), jnp.int32)]
        extra_ins = (request_variant[None, :], holder_slot, block_owner[:, :, 0])
        got = call(
            functools.partial(dense_kernel, distances, count, listing),
            "dense",
            [shape((rows, width), F32)] * len(distances) + extra_shapes * listing,
            (x, out_weight) + extra_ins * listing,
            [VMEM, ANY] + [VMEM, SMEM, SMEM] * listing,
            [VMEM] * len(distances) + [VMEM, SMEM] * listing,
            [pltpu.VMEM((4, width, piece), BF16), pltpu.SemaphoreType.DMA((4,))],
            limit=40,
            flops=2 * rows * width * width * len(distances),
            moved=2 * width * width * len(distances),
        )
        dense.update(zip(distances, got))
        return got[len(distances) :] if listing else got[0]

    chunks = {0: attended}

    def pass_on(step, *done):
        right, left = chunks[step - 1], chunks[(count - step + 1) % count]
        if done:
            right, left = after(right, *done), after(left, *done)
        chunks[step] = lax.ppermute(right, "tp", to_left)
        chunks[count - step] = lax.ppermute(left, "tp", to_right)

    third = -(-3 * count // 8)
    pass_on(1)
    token = dense_for(wanted[:third], attended)
    pass_on(2, token)
    slot, table = dense_for(wanted[third : 2 * third], after(attended, token), True)
    for step in range(3, half):
        pass_on(step, slot)

    factor_t = jnp.swapaxes(factor_in, 1, 2).reshape(low_width, -1)
    second = second_factor.reshape(low_width, complete)
    state = [shape((rows, low_width), F32), shape((complete // side, rows, side), F32)]
    early = [0]
    for distance in range(1, half - 1):
        early += [distance, count - distance]
    late = [half - 1, count - half + 1]
    tables = (slot, factor_t, block_values, block_scale, block_cell, table)
    table_specs = [VMEM, VMEM, VMEM, SMEM, SMEM, SMEM]
    low, blocks = call(
        functools.partial(fold_kernel, early, count, True),
        "fold_early",
        state,
        (*[chunks[d] for d in early], *tables),
        [VMEM] * len(early) + table_specs,
        [VMEM] * 2,
        flops=rows * low_width * complete,
        moved=4 * MIB,
    )
    front = lax.ppermute(after(chunks[half - 1], low)[: heads // 2], "tp", to_left)
    back = lax.ppermute(after(chunks[count - half + 1], low)[heads // 2 :], "tp", to_right)
    if len(wanted) > 2 * third + 1:
        token = dense_for(wanted[2 * third : -1], after(attended, low))
    low, blocks = call(
        functools.partial(fold_kernel, late, count, False),
        "fold_late",
        state,
        (*[chunks[d] for d in late], *tables, low, blocks),
        [VMEM] * len(late) + table_specs + [VMEM] * 2,
        [VMEM] * 2,
        flops=rows * low_width * width * 4,
        moved=MIB,
    )
    low = after(low, token)
    extras = shape((slots * CAP, rows, side), F32)
    low, extra, top, bottom = call(
        functools.partial(finish_kernel, half, count),
        "finish",
        [shape((rows, low_width), BF16), extras]
        + [shape((heads, rows // 2, side), BF16)] * 2,
        (front, back, *tables, second, low, blocks, dense[half]),
        [VMEM] * 2 + table_specs + [VMEM] * 4,
        [VMEM] * 4,
        [pltpu.VMEM((heads, rows, side), BF16), pltpu.VMEM((rows, low_width), F32),
         pltpu.VMEM((rows, width), F32)],
        flops=rows * low_width * width * 8,
        moved=2 * MIB,
    )

    def join(jobs, came, low, kind=BF16):
        return call(
            functools.partial(join_kernel, jobs, count, slots),
            "join",
            [shape((heads, rows // 2, side), kind)] * len(jobs),
            (low, second, blocks, extra, block_scale, block_cell, table,
             *[dense[distance] for distance, _ in jobs], *came),
            [VMEM] * 4 + [SMEM] * 3 + [VMEM] * (len(jobs) + len(came)),
            [VMEM] * len(jobs),
            [pltpu.VMEM((rows // 2, width), F32)] * len(jobs),
            flops=rows * low_width * width * 2,
            moved=MIB,
        )

    far, near = (top, bottom), ()
    for distance in range(half, 0, -1):
        if distance < half:
            far = join([(count - distance, 0), (distance, 1)], far, low)
        ready = far
        far = [lax.ppermute(far[0], "tp", to_left), lax.ppermute(far[1], "tp", to_right)]
        if distance > 1:
            near = join([(count - distance + 1, 1), (distance - 1, 0)], near, low)
            near = [lax.ppermute(near[0], "tp", to_left), lax.ppermute(near[1], "tp", to_right)]
    dense_for([0], after(attended, *ready))
    own = join([(0, 0), (0, 1)], (), after(low, *ready), F32)
    up_left, low_right = far
    if half > 1:
        low_left, up_right = near
    came = [up_left, low_right] if half == 1 else [up_left, low_right, up_right, low_left]
    return call(
        sum_kernel,
        "sum_up",
        shape((rows, width), BF16),
        (*own, *came),
        [VMEM] * (2 + len(came)),
        VMEM,
        flops=1,
        moved=1,
    )


def solution(mesh):
    return jax.shard_map(
        body,
        mesh=mesh,
        in_specs=(
            P(("groups", "rep"), "tp"),
            P("tp", ("groups", "rep"), None, None),
            P("tp", ("groups", "rep"), None, None),
            P("tp", ("groups", "rep"), None),
            P("tp", ("groups", "rep"), None),
            P(("groups", "rep")),
            P(("groups", "rep")),
            P(),
            P("tp", None),
            P("tp", None, None),
            P("tp", None, None),
            P("tp", None, None, None),
            P("tp", None),
            P("tp", None, None),
            P("tp", None),
        ),
        out_specs=P(("groups", "rep"), "tp"),
        check_vma=False,
    )
```

```python
import functools
import math

import jax
import jax.numpy as jnp
from jax import lax
from jax.experimental import pallas as pl
from jax.experimental.pallas import tpu as pltpu
from jax.sharding import PartitionSpec as P

BF16 = jnp.bfloat16
F32 = jnp.float32
CAP = 2
ROW_BLOCK = 16
PIECES = 4
MIB = 1024 * 1024
NT = (((1,), (1,)), ((), ()))
VMEM = pl.BlockSpec(memory_space=pltpu.VMEM)
SMEM = pl.BlockSpec(memory_space=pltpu.SMEM)
ANY = pl.BlockSpec(memory_space=pl.ANY)


def ring_order(count):
    if count == 8:
        return [0, 2, 4, 6, 7, 5, 3, 1]
    return list(range(count))


def owner_at(distance, count):
    me = lax.axis_index("tp")
    if count != 8:
        return lax.rem(me + distance, count)
    spot = jnp.where((me & 1) == 0, me >> 1, count - 1 - (me >> 1))
    spot = lax.rem(spot + distance, count)
    return jnp.where(spot < count // 2, 2 * spot, 2 * (count - 1 - spot) + 1)


def call(kernel, name, outs, ins, specs, out_specs, scratch=(), limit=16, flops=0, moved=0):
    return pl.pallas_call(
        kernel,
        out_shape=outs,
        in_specs=specs,
        out_specs=out_specs,
        scratch_shapes=list(scratch),
        compiler_params=pltpu.CompilerParams(vmem_limit_bytes=limit * MIB),
        cost_estimate=pl.CostEstimate(flops=flops, bytes_accessed=moved, transcendentals=0),
        name=name,
    )(*ins)


def attend_kernel(
    query_hbm, key_hbm, value_hbm, new_key_hbm, new_value_hbm, length_hbm, out_ref,
    q_ref, key_ref, value_ref, new_key_ref, new_value_ref, length_ref, sems,
):
    heads, rows, side = out_ref.shape
    cache = key_ref.shape[0] // rows
    small = [
        pltpu.make_async_copy(source, target, sems.at[i])
        for i, (source, target) in enumerate(
            ((length_hbm, length_ref), (query_hbm, q_ref), (new_key_hbm, new_key_ref),
             (new_value_hbm, new_value_ref))
        )
    ]
    tall_piece = key_ref.shape[0] // PIECES
    pieces = []
    for i in range(PIECES):
        for n, (source, target) in enumerate(((key_hbm, key_ref), (value_hbm, value_ref))):
            part = pl.ds(i * tall_piece, tall_piece)
            pieces.append(
                pltpu.make_async_copy(source.at[part], target.at[part], sems.at[4 + 2 * i + n])
            )
    for copy in small + pieces:
        copy.start()
    for copy in small:
        copy.wait()
    tall, wide = heads * ROW_BLOCK, cache * ROW_BLOCK
    scale = math.log2(math.e) / math.sqrt(side)
    lengths = jnp.transpose(jnp.broadcast_to(length_ref[...].astype(F32), (rows, rows)))[:, :1]
    row_in = lax.broadcasted_iota(jnp.int32, (tall, wide), 0) % ROW_BLOCK
    place = (lax.broadcasted_iota(jnp.int32, (tall, wide), 1) - cache * row_in).astype(F32)
    place = jnp.where(place < 0, 1e9, place)
    for r in range(0, rows, ROW_BLOCK):
        if r % (rows // PIECES) == 0:
            for copy in pieces[2 * (r * PIECES // rows) :][:2]:
                copy.wait()
        here = slice(r, r + ROW_BLOCK)
        cached = slice(r * cache, (r + ROW_BLOCK) * cache)
        query = jnp.concatenate(
            [q_ref[here, h * side : (h + 1) * side] for h in range(heads)], axis=0
        )
        new_key = jnp.concatenate([new_key_ref[here].astype(F32)] * heads, axis=0)
        new_value = jnp.concatenate([new_value_ref[here].astype(F32)] * heads, axis=0)
        live = place < jnp.concatenate([lengths[here]] * heads, axis=0)
        scores = lax.dot_general(query, key_ref[cached], NT, preferred_element_type=F32)
        fresh = jnp.sum(query.astype(F32) * new_key, axis=1, keepdims=True)
        scores = jnp.where(live, scores, -jnp.inf)
        top = jnp.maximum(jnp.max(scores, axis=1, keepdims=True), fresh)
        raw = jnp.exp2((scores - top) * scale)
        fresh_raw = jnp.exp2((fresh - top) * scale)
        inverse = 1.0 / (jnp.sum(raw, axis=1, keepdims=True) + fresh_raw)
        attended = jnp.dot(raw.astype(BF16), value_ref[cached], preferred_element_type=F32)
        attended = ((attended + fresh_raw * new_value) * inverse).astype(BF16)
        for h in range(heads):
            out_ref[h, here, :] = attended[h * ROW_BLOCK : (h + 1) * ROW_BLOCK]


def dense_kernel(distances, count, listing, *refs):
    x_ref, weight_ref = refs[:2]
    if listing:
        variant_ref, holder_ref, owner_ref = refs[2:5]
        outs, slot_ref, table_ref = refs[5 : 5 + len(distances)], refs[-4], refs[-3]
    else:
        outs = refs[2 : 2 + len(distances)]
    buffers, sems = refs[-2:]
    heads, rows, side = x_ref.shape
    width = heads * side
    depth = buffers.shape[0]
    piece = buffers.shape[2]
    cuts = width // piece

    def fetch(i):
        start = pl.multiple_of(owner_at(distances[i // cuts], count) * width, width) + i % cuts * piece
        return pltpu.make_async_copy(
            weight_ref.at[:, pl.ds(pl.multiple_of(start, piece), piece)],
            buffers.at[i % depth],
            sems.at[i % depth],
        )

    total = len(distances) * cuts
    for i in range(min(depth, total)):
        fetch(i).start()
    if listing:
        slots = owner_ref.shape[0]
        variant = variant_ref[...]
        slot_row = jnp.zeros(variant.shape, jnp.int32)
        for v in range(holder_ref.shape[0]):
            slot_row = jnp.where(variant == v, holder_ref[v], slot_row)
        slot_row = (slot_row - lax.axis_index("tp") * slots).astype(F32)
        slot_ref[...] = jnp.transpose(jnp.broadcast_to(slot_row, (rows, rows))).astype(jnp.int32)
        for e in range(table_ref.shape[0]):
            table_ref[e] = -1
        for j in range(slots):

            def note(b, carry, j=j):
                e = (owner_ref[j, b] * slots + j) * CAP
                table_ref[e + jnp.where(table_ref[e] >= 0, 1, 0)] = b
                return carry

            lax.fori_loop(0, owner_ref.shape[1], note, 0)
    x = jnp.concatenate([x_ref[h] for h in range(heads)], axis=1)
    for i in range(total):
        fetch(i).wait()
        outs[i // cuts][:, i % cuts * piece : (i % cuts + 1) * piece] = jnp.dot(
            x, buffers[i % depth], preferred_element_type=F32
        )
        if i + depth < total:
            fetch(i + depth).start()


def held_blocks(distance, count, slots, heads, scale_ref, cell_ref, table_ref):
    tiles = count * heads
    owner = owner_at(distance, count)
    listed = []
    for j in range(slots):
        for c in range(CAP):
            b = table_ref[(owner * slots + j) * CAP + c]
            found = jnp.maximum(b, 0)
            cell = cell_ref[j, found]
            scale = jnp.where(b >= 0, scale_ref[j, found], 0.0)
            listed.append((j, found, scale, lax.div(cell, tiles), lax.rem(cell, tiles)))
    return listed


def fold_chunk(distance, count, chunk_ref, slot, factor_ref, values_ref, scale_ref, cell_ref,
               table_ref, low_ref):
    heads, rows, side = chunk_ref.shape
    width = heads * side
    features = jnp.concatenate([chunk_ref[h] for h in range(heads)], axis=1)
    start = pl.multiple_of(owner_at(distance, count) * width, width)
    low_ref[...] += lax.dot_general(
        features, factor_ref[:, pl.ds(start, width)], NT, preferred_element_type=F32
    )
    added = []
    for j, b, scale, row_block, column in held_blocks(
        distance, count, values_ref.shape[0], heads, scale_ref, cell_ref, table_ref
    ):
        mine = jnp.where(slot == j, 1.0, 0.0)
        product = jnp.dot(chunk_ref[row_block], values_ref[j, b], preferred_element_type=F32)
        added.append((column, product * (mine * scale)))
    return added


def fold_kernel(distances, count, first, *refs):
    chunks, refs = refs[: len(distances)], refs[len(distances) :]
    slot_ref, factor_ref, values_ref, scale_ref, cell_ref, table_ref = refs[:6]
    low_ref, block_ref = refs[-2:]
    if first:
        low_ref[...] = jnp.zeros_like(low_ref)
        block_ref[...] = jnp.zeros_like(block_ref)
    else:
        low_ref[...] = refs[6][...]
        block_ref[...] = refs[7][...]
    slot = slot_ref[...]
    for distance, chunk in zip(distances, chunks):
        for column, product in fold_chunk(distance, count, chunk, slot, factor_ref, values_ref,
                                          scale_ref, cell_ref, table_ref, low_ref):
            block_ref[column] += product


def part_for(distance, count, low_ref, second_ref, dense_ref, block_ref, extra_ref, columns, out_ref):
    width = dense_ref.shape[1]
    side = block_ref.shape[2]
    heads = width // side
    owner = owner_at(distance, count)
    start = pl.multiple_of(owner * width, width)
    blocks = jnp.concatenate([block_ref[owner * heads + i] for i in range(heads)], axis=1)
    out_ref[...] = (
        jnp.dot(low_ref[...], second_ref[:, pl.ds(start, width)], preferred_element_type=F32)
        + dense_ref[...]
        + blocks
    )
    for e, column in enumerate(columns):

        @pl.when(lax.div(column, heads) == owner)
        def _(e=e, column=column):
            place = pl.ds(pl.multiple_of(lax.rem(column, heads) * side, side), side)
            out_ref[:, place] += extra_ref[e]


def finish_kernel(distances, count, *refs):
    front_ref, back_ref, slot_ref, factor_ref, values_ref, scale_ref, cell_ref, table_ref = refs[:8]
    second_ref, low_in, block_ref = refs[8:11]
    dense_refs, refs = refs[11 : 11 + len(distances)], refs[11 + len(distances) :]
    low_out, extra_out, front_out, back_out = refs[:4]
    outs, (chunk, low_sum, total) = refs[4:-3], refs[-3:]
    half, rows, side = front_ref.shape
    chunk[:half] = front_ref[...]
    chunk[half:] = back_ref[...]
    low_sum[...] = low_in[...]
    slot = slot_ref[...]
    added = fold_chunk(distances[0], count, chunk, slot, factor_ref, values_ref, scale_ref, cell_ref,
                       table_ref, low_sum)
    for e, (_, product) in enumerate(added):
        extra_out[e] = product
    columns = [column for column, _ in added]
    low_width = low_sum.shape[1]
    rank = low_width // values_ref.shape[0]
    held = lax.broadcasted_iota(jnp.int32, (rows, low_width), 1) // rank
    slots_wide = jnp.concatenate([slot] * -(-low_width // side), axis=1)[:, :low_width]
    low = jnp.where(slots_wide == held, low_sum[...], 0.0).astype(BF16)
    low_out[...] = low
    for n, (distance, dense_ref) in enumerate(zip(distances, dense_refs)):
        part_for(distance, count, low_out, second_ref, dense_ref, block_ref, extra_out, columns,
                 total.at[n])
        for i in range(2 * half):
            tile = total[n, :, i * side : (i + 1) * side].astype(BF16)
            if n:
                outs[n - 1][i] = tile
            elif i < half:
                front_out[i] = tile
            else:
                back_out[i - half] = tile


def part_kernel(distances, count, slots, *refs):
    low_ref, second_ref, block_ref, extra_ref, scale_ref, cell_ref, table_ref = refs[:7]
    dense_refs, refs = refs[7 : 7 + len(distances)], refs[7 + len(distances) :]
    outs, total = refs[:-1], refs[-1]
    side = block_ref.shape[2]
    heads = dense_refs[0].shape[1] // side
    listed = held_blocks(count // 2, count, slots, heads, scale_ref, cell_ref, table_ref)
    columns = [entry[-1] for entry in listed]
    for n, (distance, dense_ref) in enumerate(zip(distances, dense_refs)):
        part_for(distance, count, low_ref, second_ref, dense_ref, block_ref, extra_ref, columns,
                 total.at[n])
        for i in range(heads):
            outs[n][i] = total[n, :, i * side : (i + 1) * side].astype(outs[n].dtype)


def sum_kernel(own_ref, *refs):
    out_ref = refs[-1]
    heads, _, side = own_ref.shape
    for i in range(heads):
        total = own_ref[i]
        for ref in refs[:-1]:
            total = total + ref[i].astype(F32)
        out_ref[:, i * side : (i + 1) * side] = total.astype(BF16)


def after(value, *others):
    return lax.optimization_barrier((value, *others))[0]


def body(
    queries, key_cache, value_cache, new_keys, new_values, lengths, request_variant, holder_slot,
    out_weight, factor_in, second_factor, block_values, block_scale, block_owner, block_cell,
):
    count = lax.axis_size("tp")
    half = count // 2
    ring = ring_order(count)
    rows, width = queries.shape
    side = key_cache.shape[3]
    cache = key_cache.shape[2]
    heads = width // side
    slots = block_values.shape[0]
    complete = out_weight.shape[1]
    low_width = slots * factor_in.shape[2]
    shape = jax.ShapeDtypeStruct

    attended = call(
        attend_kernel,
        "attend",
        shape((heads, rows, side), BF16),
        (queries, key_cache.reshape(-1, side), value_cache.reshape(-1, side), new_keys[0],
         new_values[0], lengths[None, :]),
        [ANY] * 6,
        VMEM,
        [pltpu.VMEM((rows, width), BF16), pltpu.VMEM((rows * cache, side), BF16),
         pltpu.VMEM((rows * cache, side), BF16), pltpu.VMEM((rows, side), BF16),
         pltpu.VMEM((rows, side), BF16), pltpu.VMEM((1, rows), jnp.int32),
         pltpu.SemaphoreType.DMA((4 + 2 * PIECES,))],
        limit=60,
    )

    wanted = [half]
    for distance in range(half - 1, 0, -1):
        wanted += [distance, count - distance]
    wanted += [0]
    piece = width // 2 if width >= 512 else width
    dense = {}

    def dense_for(distances, x, listing=False):
        extra_shapes = [shape((rows, rows), jnp.int32), shape((count * slots * CAP,), jnp.int32)]
        extra_ins = (request_variant[None, :], holder_slot, block_owner[:, :, 0])
        got = call(
            functools.partial(dense_kernel, distances, count, listing),
            "dense",
            [shape((rows, width), F32)] * len(distances) + extra_shapes * listing,
            (x, out_weight) + extra_ins * listing,
            [VMEM, ANY] + [VMEM, SMEM, SMEM] * listing,
            [VMEM] * len(distances) + [VMEM, SMEM] * listing,
            [pltpu.VMEM((4, width, piece), BF16), pltpu.SemaphoreType.DMA((4,))],
            limit=40,
            flops=2 * rows * width * width * len(distances),
            moved=2 * width * width * len(distances),
        )
        dense.update(zip(distances, got))
        return got[len(distances) :] if listing else got[0]

    def come(value, distance):
        return lax.ppermute(
            value, "tp", [(ring[(i + distance) % count], ring[i]) for i in range(count)]
        )

    short = count == 8
    chunks = {0: attended}
    if short:
        for distance in (2, 6, 1, 7):
            chunks[distance] = come(attended, distance if distance <= half else distance - count)
        wanted = [4, 3, 5, 1, 7, 2, 6, 0]
        cuts = [5, 7]
    else:
        chunks[1], chunks[count - 1] = come(attended, 1), come(attended, -1)
        cuts = [count // 2, count - 1]
    token = dense_for(wanted[: cuts[0]], attended)
    if short:
        right, left = after(chunks[2], token), after(chunks[6], token)
        chunks[3], chunks[5] = come(right, 1), come(left, -1)
        front, back = come(right[: heads // 2], 2), come(left[heads // 2 :], -2)
    else:
        for step in range(2, half):
            right, left = after(chunks[step - 1], token), after(chunks[count - step + 1], token)
            chunks[step], chunks[count - step] = come(right, 1), come(left, -1)
        right, left = chunks[half - 1], chunks[half + 1]
        front, back = come(right[: heads // 2], 1), come(left[heads // 2 :], -1)
    slot, table = dense_for(wanted[cuts[0] : cuts[1]], after(attended, token), True)

    factor_t = jnp.swapaxes(factor_in, 1, 2).reshape(low_width, -1)
    second = second_factor.reshape(low_width, complete)
    state = [shape((rows, low_width), F32), shape((complete // side, rows, side), F32)]
    early = [0]
    for distance in range(1, half - 1):
        early += [distance, count - distance]
    late = [half - 1, count - half + 1]
    tables = (slot, factor_t, block_values, block_scale, block_cell, table)
    table_specs = [VMEM, VMEM, VMEM, SMEM, SMEM, SMEM]
    low, blocks = call(
        functools.partial(fold_kernel, early, count, True),
        "fold_early",
        state,
        (*[chunks[d] for d in early], *tables),
        [VMEM] * len(early) + table_specs,
        [VMEM] * 2,
        flops=rows * low_width * complete,
        moved=4 * MIB,
    )
    low, blocks = call(
        functools.partial(fold_kernel, late, count, False),
        "fold_late",
        state,
        (*[chunks[d] for d in late], *tables, low, blocks),
        [VMEM] * len(late) + table_specs + [VMEM] * 2,
        [VMEM] * 2,
        flops=rows * low_width * width * 4,
        moved=MIB,
    )
    extras = shape((slots * CAP, rows, side), F32)
    first = [half, half - 1, half + 1] if half > 1 else [half]
    travelling = shape((heads, rows, side), BF16)
    low, extra, front, back, *sums = call(
        functools.partial(finish_kernel, first, count),
        "finish",
        [shape((rows, low_width), BF16), extras]
        + [shape((heads // 2, rows, side), BF16)] * 2
        + [travelling] * (len(first) - 1),
        (front, back, *tables, second, low, blocks, *[dense[d] for d in first]),
        [VMEM] * 2 + table_specs + [VMEM] * (3 + len(first)),
        [VMEM] * (3 + len(first)),
        [pltpu.VMEM((heads, rows, side), BF16), pltpu.VMEM((rows, low_width), F32),
         pltpu.VMEM((len(first), rows, width), F32)],
        flops=rows * low_width * width * 8,
        moved=2 * MIB,
    )
    parts = dict(zip(first[1:], sums))

    def parts_for(distances, low, kind):
        got = call(
            functools.partial(part_kernel, distances, count, slots),
            "part",
            [shape((heads, rows, side), kind)] * len(distances),
            (low, second, blocks, extra, block_scale, block_cell, table,
             *[dense[distance] for distance in distances]),
            [VMEM] * 4 + [SMEM] * 3 + [VMEM] * len(distances),
            [VMEM] * len(distances),
            [pltpu.VMEM((len(distances), rows, width), F32)],
            flops=rows * low_width * width * 2,
            moved=MIB,
        )
        parts.update(zip(distances, got))

    def joined(part, *came):
        total = part.astype(F32)
        for value, place in came:
            value = value.astype(F32)
            if place is not None:
                none = jnp.zeros_like(value)
                value = jnp.concatenate([none, value] if place else [value, none], axis=0)
            total = total + value
        return total.astype(BF16)

    if short:
        from_left, from_right = come(parts[3], -1), come(parts[5], 1)
        front, back = come(front, -2), come(back, 2)
        parts_for([1, 7], low, BF16)
        came = [come(parts[1], -1), come(parts[7], 1)]
        parts_for([2, 6], after(low, parts[1]), F32)
        from_left, from_right, front, back = lax.optimization_barrier(
            (from_left, from_right, front, back)
        )
        right = joined(parts[2], (from_left, None), (front, 0))
        left = joined(parts[6], (from_right, None), (back, 1))
        came += [come(right, -2), come(left, 2)]
    else:
        left, right = (front, 0), (back, 1)
        left, right = (come(front, 1), 0), (come(back, -1), 1)
        for distance in range(half - 1, 0, -1):
            left = joined(parts[count - distance], left)
            right = joined(parts[distance], right)
            if distance > 1:
                parts_for([distance - 1, count - distance + 1], after(low, right), F32)
            left, right = (come(left, 1), None), (come(right, -1), None)
        came = [left[0], right[0]]
    dense_for([0], after(attended, right if short else parts[1]))
    parts_for([0], low, F32)
    return call(
        sum_kernel,
        "sum_up",
        shape((rows, width), BF16),
        (parts[0], *came),
        [VMEM] * (1 + len(came)),
        VMEM,
        flops=1,
        moved=1,
    )


def solution(mesh):
    return jax.shard_map(
        body,
        mesh=mesh,
        in_specs=(
            P(("groups", "rep"), "tp"),
            P("tp", ("groups", "rep"), None, None),
            P("tp", ("groups", "rep"), None, None),
            P("tp", ("groups", "rep"), None),
            P("tp", ("groups", "rep"), None),
            P(("groups", "rep")),
            P(("groups", "rep")),
            P(),
            P("tp", None),
            P("tp", None, None),
            P("tp", None, None),
            P("tp", None, None, None),
            P("tp", None),
            P("tp", None, None),
            P("tp", None),
        ),
        out_specs=P(("groups", "rep"), "tp"),
        check_vma=False,
    )
```

```python
import functools
import math

import jax
import jax.numpy as jnp
from jax import lax
from jax.experimental import pallas as pl
from jax.experimental.pallas import tpu as pltpu
from jax.sharding import PartitionSpec as P

BF16 = jnp.bfloat16
F32 = jnp.float32
CAP = 2
ROW_BLOCK = 16
PIECES = 4
MIB = 1024 * 1024
NT = (((1,), (1,)), ((), ()))
VMEM = pl.BlockSpec(memory_space=pltpu.VMEM)
SMEM = pl.BlockSpec(memory_space=pltpu.SMEM)
ANY = pl.BlockSpec(memory_space=pl.ANY)


def ring_order(count):
    if count == 8:
        return [0, 2, 4, 6, 7, 5, 3, 1]
    return list(range(count))


def owner_at(distance, count):
    me = lax.axis_index("tp")
    if count != 8:
        return lax.rem(me + distance, count)
    spot = jnp.where((me & 1) == 0, me >> 1, count - 1 - (me >> 1))
    spot = lax.rem(spot + distance, count)
    return jnp.where(spot < count // 2, 2 * spot, 2 * (count - 1 - spot) + 1)


def call(kernel, name, outs, ins, specs, out_specs, scratch=(), limit=16, flops=0, moved=0):
    return pl.pallas_call(
        kernel,
        out_shape=outs,
        in_specs=specs,
        out_specs=out_specs,
        scratch_shapes=list(scratch),
        compiler_params=pltpu.CompilerParams(vmem_limit_bytes=limit * MIB),
        cost_estimate=pl.CostEstimate(flops=flops, bytes_accessed=moved, transcendentals=0),
        name=name,
    )(*ins)


def attend_kernel(
    query_hbm, key_hbm, value_hbm, new_key_hbm, new_value_hbm, length_hbm, out_ref,
    q_ref, key_ref, value_ref, new_key_ref, new_value_ref, length_ref, sems,
):
    heads, rows, side = out_ref.shape
    cache = key_ref.shape[0] // rows
    small = [
        pltpu.make_async_copy(source, target, sems.at[i])
        for i, (source, target) in enumerate(
            ((length_hbm, length_ref), (query_hbm, q_ref), (new_key_hbm, new_key_ref),
             (new_value_hbm, new_value_ref))
        )
    ]
    tall_piece = key_ref.shape[0] // PIECES
    pieces = []
    for i in range(PIECES):
        for n, (source, target) in enumerate(((key_hbm, key_ref), (value_hbm, value_ref))):
            part = pl.ds(i * tall_piece, tall_piece)
            pieces.append(
                pltpu.make_async_copy(source.at[part], target.at[part], sems.at[4 + 2 * i + n])
            )
    for copy in small + pieces:
        copy.start()
    for copy in small:
        copy.wait()
    tall, wide = heads * ROW_BLOCK, cache * ROW_BLOCK
    scale = math.log2(math.e) / math.sqrt(side)
    lengths = jnp.transpose(jnp.broadcast_to(length_ref[...].astype(F32), (rows, rows)))[:, :1]
    row_in = lax.broadcasted_iota(jnp.int32, (tall, wide), 0) % ROW_BLOCK
    place = (lax.broadcasted_iota(jnp.int32, (tall, wide), 1) - cache * row_in).astype(F32)
    place = jnp.where(place < 0, 1e9, place)
    for r in range(0, rows, ROW_BLOCK):
        if r % (rows // PIECES) == 0:
            for copy in pieces[2 * (r * PIECES // rows) :][:2]:
                copy.wait()
        here = slice(r, r + ROW_BLOCK)
        cached = slice(r * cache, (r + ROW_BLOCK) * cache)
        query = jnp.concatenate(
            [q_ref[here, h * side : (h + 1) * side] for h in range(heads)], axis=0
        )
        new_key = jnp.concatenate([new_key_ref[here].astype(F32)] * heads, axis=0)
        new_value = jnp.concatenate([new_value_ref[here].astype(F32)] * heads, axis=0)
        live = place < jnp.concatenate([lengths[here]] * heads, axis=0)
        scores = lax.dot_general(query, key_ref[cached], NT, preferred_element_type=F32)
        fresh = jnp.sum(query.astype(F32) * new_key, axis=1, keepdims=True)
        scores = jnp.where(live, scores, -jnp.inf)
        top = jnp.maximum(jnp.max(scores, axis=1, keepdims=True), fresh)
        raw = jnp.exp2((scores - top) * scale)
        fresh_raw = jnp.exp2((fresh - top) * scale)
        inverse = 1.0 / (jnp.sum(raw, axis=1, keepdims=True) + fresh_raw)
        attended = jnp.dot(raw.astype(BF16), value_ref[cached], preferred_element_type=F32)
        attended = ((attended + fresh_raw * new_value) * inverse).astype(BF16)
        for h in range(heads):
            out_ref[h, here, :] = attended[h * ROW_BLOCK : (h + 1) * ROW_BLOCK]


def dense_kernel(distances, count, listing, *refs):
    x_ref, weight_ref = refs[:2]
    if listing:
        variant_ref, holder_ref, owner_ref = refs[2:5]
        outs, slot_ref, table_ref = refs[5 : 5 + len(distances)], refs[-4], refs[-3]
    else:
        outs = refs[2 : 2 + len(distances)]
    buffers, sems = refs[-2:]
    heads, rows, side = x_ref.shape
    width = heads * side
    depth = buffers.shape[0]
    piece = buffers.shape[2]
    cuts = width // piece

    def fetch(i):
        start = pl.multiple_of(owner_at(distances[i // cuts], count) * width, width) + i % cuts * piece
        return pltpu.make_async_copy(
            weight_ref.at[:, pl.ds(pl.multiple_of(start, piece), piece)],
            buffers.at[i % depth],
            sems.at[i % depth],
        )

    total = len(distances) * cuts
    for i in range(min(depth, total)):
        fetch(i).start()
    if listing:
        slots = owner_ref.shape[0]
        variant = variant_ref[...]
        slot_row = jnp.zeros(variant.shape, jnp.int32)
        for v in range(holder_ref.shape[0]):
            slot_row = jnp.where(variant == v, holder_ref[v], slot_row)
        slot_row = (slot_row - lax.axis_index("tp") * slots).astype(F32)
        slot_ref[...] = jnp.transpose(jnp.broadcast_to(slot_row, (rows, rows))).astype(jnp.int32)
        for e in range(table_ref.shape[0]):
            table_ref[e] = -1
        for j in range(slots):

            def note(b, carry, j=j):
                e = (owner_ref[j, b] * slots + j) * CAP
                table_ref[e + jnp.where(table_ref[e] >= 0, 1, 0)] = b
                return carry

            lax.fori_loop(0, owner_ref.shape[1], note, 0)
    x = jnp.concatenate([x_ref[h] for h in range(heads)], axis=1)
    for i in range(total):
        fetch(i).wait()
        outs[i // cuts][:, i % cuts * piece : (i % cuts + 1) * piece] = jnp.dot(
            x, buffers[i % depth], preferred_element_type=F32
        )
        if i + depth < total:
            fetch(i + depth).start()


def held_blocks(distance, count, slots, heads, scale_ref, cell_ref, table_ref):
    tiles = count * heads
    owner = owner_at(distance, count)
    listed = []
    for j in range(slots):
        for c in range(CAP):
            b = table_ref[(owner * slots + j) * CAP + c]
            found = jnp.maximum(b, 0)
            cell = cell_ref[j, found]
            scale = jnp.where(b >= 0, scale_ref[j, found], 0.0)
            listed.append((j, found, scale, lax.div(cell, tiles), lax.rem(cell, tiles)))
    return listed


def fold_chunk(distance, count, chunk_ref, slot, factor_ref, values_ref, scale_ref, cell_ref,
               table_ref, low_ref):
    heads, rows, side = chunk_ref.shape
    width = heads * side
    features = jnp.concatenate([chunk_ref[h] for h in range(heads)], axis=1)
    start = pl.multiple_of(owner_at(distance, count) * width, width)
    low_ref[...] += lax.dot_general(
        features, factor_ref[:, pl.ds(start, width)], NT, preferred_element_type=F32
    )
    added = []
    for j, b, scale, row_block, column in held_blocks(
        distance, count, values_ref.shape[0], heads, scale_ref, cell_ref, table_ref
    ):
        mine = jnp.where(slot == j, 1.0, 0.0)
        product = jnp.dot(chunk_ref[row_block], values_ref[j, b], preferred_element_type=F32)
        added.append((column, product * (mine * scale)))
    return added


def fold_kernel(distances, count, first, *refs):
    chunks, refs = refs[: len(distances)], refs[len(distances) :]
    slot_ref, factor_ref, values_ref, scale_ref, cell_ref, table_ref = refs[:6]
    low_ref, block_ref = refs[-2:]
    if first:
        low_ref[...] = jnp.zeros_like(low_ref)
        block_ref[...] = jnp.zeros_like(block_ref)
    else:
        low_ref[...] = refs[6][...]
        block_ref[...] = refs[7][...]
    slot = slot_ref[...]
    for distance, chunk in zip(distances, chunks):
        for column, product in fold_chunk(distance, count, chunk, slot, factor_ref, values_ref,
                                          scale_ref, cell_ref, table_ref, low_ref):
            block_ref[column] += product


def part_for(distance, count, low_ref, second_ref, dense_ref, block_ref, extra_ref, columns, out_ref):
    width = dense_ref.shape[1]
    side = block_ref.shape[2]
    heads = width // side
    owner = owner_at(distance, count)
    start = pl.multiple_of(owner * width, width)
    blocks = jnp.concatenate([block_ref[owner * heads + i] for i in range(heads)], axis=1)
    out_ref[...] = (
        jnp.dot(low_ref[...], second_ref[:, pl.ds(start, width)], preferred_element_type=F32)
        + dense_ref[...]
        + blocks
    )
    for e, column in enumerate(columns):

        @pl.when(lax.div(column, heads) == owner)
        def _(e=e, column=column):
            place = pl.ds(pl.multiple_of(lax.rem(column, heads) * side, side), side)
            out_ref[:, place] += extra_ref[e]


def finish_kernel(distances, count, *refs):
    front_ref, back_ref, slot_ref, factor_ref, values_ref, scale_ref, cell_ref, table_ref = refs[:8]
    second_ref, low_in, block_ref = refs[8:11]
    dense_refs, refs = refs[11 : 11 + len(distances)], refs[11 + len(distances) :]
    low_out, extra_out, front_out, back_out = refs[:4]
    outs, (chunk, low_sum, total) = refs[4:-3], refs[-3:]
    half, rows, side = front_ref.shape
    chunk[:half] = front_ref[...]
    chunk[half:] = back_ref[...]
    low_sum[...] = low_in[...]
    slot = slot_ref[...]
    added = fold_chunk(distances[0], count, chunk, slot, factor_ref, values_ref, scale_ref, cell_ref,
                       table_ref, low_sum)
    for e, (_, product) in enumerate(added):
        extra_out[e] = product
    columns = [column for column, _ in added]
    low_width = low_sum.shape[1]
    rank = low_width // values_ref.shape[0]
    held = lax.broadcasted_iota(jnp.int32, (rows, low_width), 1) // rank
    slots_wide = jnp.concatenate([slot] * -(-low_width // side), axis=1)[:, :low_width]
    low = jnp.where(slots_wide == held, low_sum[...], 0.0).astype(BF16)
    low_out[...] = low
    for n, (distance, dense_ref) in enumerate(zip(distances, dense_refs)):
        part_for(distance, count, low_out, second_ref, dense_ref, block_ref, extra_out, columns,
                 total.at[n])
        for i in range(2 * half):
            tile = total[n, :, i * side : (i + 1) * side].astype(BF16)
            if n:
                outs[n - 1][i] = tile
            elif i < half:
                front_out[i] = tile
            else:
                back_out[i - half] = tile


def part_kernel(distances, count, slots, *refs):
    low_ref, second_ref, block_ref, extra_ref, scale_ref, cell_ref, table_ref = refs[:7]
    dense_refs, refs = refs[7 : 7 + len(distances)], refs[7 + len(distances) :]
    outs, total = refs[:-1], refs[-1]
    side = block_ref.shape[2]
    heads = dense_refs[0].shape[1] // side
    listed = held_blocks(count // 2, count, slots, heads, scale_ref, cell_ref, table_ref)
    columns = [entry[-1] for entry in listed]
    for n, (distance, dense_ref) in enumerate(zip(distances, dense_refs)):
        part_for(distance, count, low_ref, second_ref, dense_ref, block_ref, extra_ref, columns,
                 total.at[n])
        for i in range(heads):
            outs[n][i] = total[n, :, i * side : (i + 1) * side].astype(outs[n].dtype)


def sum_kernel(own_ref, *refs):
    out_ref = refs[-1]
    heads, _, side = own_ref.shape
    for i in range(heads):
        total = own_ref[i]
        for ref in refs[:-1]:
            total = total + ref[i].astype(F32)
        out_ref[:, i * side : (i + 1) * side] = total.astype(BF16)


def after(value, *others):
    return lax.optimization_barrier((value, *others))[0]


def body(
    queries, key_cache, value_cache, new_keys, new_values, lengths, request_variant, holder_slot,
    out_weight, factor_in, second_factor, block_values, block_scale, block_owner, block_cell,
):
    count = lax.axis_size("tp")
    half = count // 2
    ring = ring_order(count)
    rows, width = queries.shape
    side = key_cache.shape[3]
    cache = key_cache.shape[2]
    heads = width // side
    slots = block_values.shape[0]
    complete = out_weight.shape[1]
    low_width = slots * factor_in.shape[2]
    shape = jax.ShapeDtypeStruct

    attended = call(
        attend_kernel,
        "attend",
        shape((heads, rows, side), BF16),
        (queries, key_cache.reshape(-1, side), value_cache.reshape(-1, side), new_keys[0],
         new_values[0], lengths[None, :]),
        [ANY] * 6,
        VMEM,
        [pltpu.VMEM((rows, width), BF16), pltpu.VMEM((rows * cache, side), BF16),
         pltpu.VMEM((rows * cache, side), BF16), pltpu.VMEM((rows, side), BF16),
         pltpu.VMEM((rows, side), BF16), pltpu.VMEM((1, rows), jnp.int32),
         pltpu.SemaphoreType.DMA((4 + 2 * PIECES,))],
        limit=60,
    )

    wanted = [half]
    for distance in range(half - 1, 0, -1):
        wanted += [distance, count - distance]
    wanted += [0]
    piece = width // 2 if width >= 512 else width
    dense = {}

    def dense_for(distances, x, listing=False):
        extra_shapes = [shape((rows, rows), jnp.int32), shape((count * slots * CAP,), jnp.int32)]
        extra_ins = (request_variant[None, :], holder_slot, block_owner[:, :, 0])
        got = call(
            functools.partial(dense_kernel, distances, count, listing),
            "dense",
            [shape((rows, width), F32)] * len(distances) + extra_shapes * listing,
            (x, out_weight) + extra_ins * listing,
            [VMEM, ANY] + [VMEM, SMEM, SMEM] * listing,
            [VMEM] * len(distances) + [VMEM, SMEM] * listing,
            [pltpu.VMEM((4, width, piece), BF16), pltpu.SemaphoreType.DMA((4,))],
            limit=40,
            flops=2 * rows * width * width * len(distances),
            moved=2 * width * width * len(distances),
        )
        dense.update(zip(distances, got))
        return got[len(distances) :] if listing else got[0]

    def come(value, distance):
        return lax.ppermute(
            value, "tp", [(ring[(i + distance) % count], ring[i]) for i in range(count)]
        )

    chunks = {0: attended}
    chunks[1], chunks[count - 1] = come(attended, 1), come(attended, -1)
    token = dense_for(wanted[:3], attended)
    for step in range(2, half):
        right, left = after(chunks[step - 1], token), after(chunks[count - step + 1], token)
        if step == half - 1:
            front, back = come(right[: heads // 2], 2), come(left[heads // 2 :], -2)
        chunks[step], chunks[count - step] = come(right, 1), come(left, -1)
        if step == 2:
            slot, table = dense_for(wanted[3:5], after(attended, token), True)
            token = slot

    factor_t = jnp.swapaxes(factor_in, 1, 2).reshape(low_width, -1)
    second = second_factor.reshape(low_width, complete)
    state = [shape((rows, low_width), F32), shape((complete // side, rows, side), F32)]
    early = [0]
    for distance in range(1, half - 1):
        early += [distance, count - distance]
    late = [half - 1, count - half + 1]
    tables = (slot, factor_t, block_values, block_scale, block_cell, table)
    table_specs = [VMEM, VMEM, VMEM, SMEM, SMEM, SMEM]
    low, blocks = call(
        functools.partial(fold_kernel, early, count, True),
        "fold_early",
        state,
        (*[chunks[d] for d in early], *tables),
        [VMEM] * len(early) + table_specs,
        [VMEM] * 2,
        flops=rows * low_width * complete,
        moved=4 * MIB,
    )
    low, blocks = call(
        functools.partial(fold_kernel, late, count, False),
        "fold_late",
        state,
        (*[chunks[d] for d in late], *tables, low, blocks),
        [VMEM] * len(late) + table_specs + [VMEM] * 2,
        [VMEM] * 2,
        flops=rows * low_width * width * 4,
        moved=MIB,
    )
    extras = shape((slots * CAP, rows, side), F32)
    first = wanted[:3]
    travelling = shape((heads, rows, side), BF16)
    low, extra, front, back, *sums = call(
        functools.partial(finish_kernel, first, count),
        "finish",
        [shape((rows, low_width), BF16), extras]
        + [shape((heads // 2, rows, side), BF16)] * 2
        + [travelling] * (len(first) - 1),
        (front, back, *tables, second, low, blocks, *[dense[d] for d in first]),
        [VMEM] * 2 + table_specs + [VMEM] * (3 + len(first)),
        [VMEM] * (3 + len(first)),
        [pltpu.VMEM((heads, rows, side), BF16), pltpu.VMEM((rows, low_width), F32),
         pltpu.VMEM((len(first), rows, width), F32)],
        flops=rows * low_width * width * 8,
        moved=2 * MIB,
    )
    parts = dict(zip(first[1:], sums))

    def parts_for(distances, low, kind):
        got = call(
            functools.partial(part_kernel, distances, count, slots),
            "part",
            [shape((heads, rows, side), kind)] * len(distances),
            (low, second, blocks, extra, block_scale, block_cell, table,
             *[dense[distance] for distance in distances]),
            [VMEM] * 4 + [SMEM] * 3 + [VMEM] * len(distances),
            [VMEM] * len(distances),
            [pltpu.VMEM((len(distances), rows, width), F32)],
            flops=rows * low_width * width * 2,
            moved=MIB,
        )
        parts.update(zip(distances, got))

    def joined(part, *came):
        total = part.astype(F32)
        for value, place in came:
            value = value.astype(F32)
            if place is not None:
                none = jnp.zeros_like(value)
                value = jnp.concatenate([none, value] if place else [value, none], axis=0)
            total = total + value
        return total.astype(BF16)

    front, back = come(front, -2), come(back, 2)
    from_left, from_right = come(parts[half - 1], -1), come(parts[half + 1], 1)
    parts_for([half - 2, half + 2], low, F32)
    token = dense_for(wanted[5:-1], after(attended, low))
    from_left, from_right, front, back, token = lax.optimization_barrier(
        (from_left, from_right, front, back, token)
    )
    right = joined(parts[half - 2], (from_left, None), (front, 0))
    left = joined(parts[half + 2], (from_right, None), (back, 1))
    for distance in range(half - 2, 0, -1):
        nearer = distance - 1
        if distance == half - 2:
            dense_for([0], after(attended, right))
        parts_for([nearer, count - nearer] if nearer else [0], after(low, right), F32)
        from_left, from_right = come(right, -1), come(left, 1)
        if nearer:
            right = joined(parts[nearer], (from_left, None))
            left = joined(parts[count - nearer], (from_right, None))
    came = [from_left, from_right]
    return call(
        sum_kernel,
        "sum_up",
        shape((rows, width), BF16),
        (parts[0], *came),
        [VMEM] * (1 + len(came)),
        VMEM,
        flops=1,
        moved=1,
    )


def solution(mesh):
    return jax.shard_map(
        body,
        mesh=mesh,
        in_specs=(
            P(("groups", "rep"), "tp"),
            P("tp", ("groups", "rep"), None, None),
            P("tp", ("groups", "rep"), None, None),
            P("tp", ("groups", "rep"), None),
            P("tp", ("groups", "rep"), None),
            P(("groups", "rep")),
            P(("groups", "rep")),
            P(),
            P("tp", None),
            P("tp", None, None),
            P("tp", None, None),
            P("tp", None, None, None),
            P("tp", None),
            P("tp", None, None),
            P("tp", None),
        ),
        out_specs=P(("groups", "rep"), "tp"),
        check_vma=False,
    )
```

```python
import functools
import math

import jax
import jax.numpy as jnp
from jax import lax
from jax.experimental import pallas as pl
from jax.experimental.pallas import tpu as pltpu
from jax.sharding import PartitionSpec as P

BF16 = jnp.bfloat16
F32 = jnp.float32
CAP = 2
ROW_BLOCK = 16
PIECES = 4
MIB = 1024 * 1024
NT = (((1,), (1,)), ((), ()))
VMEM = pl.BlockSpec(memory_space=pltpu.VMEM)
SMEM = pl.BlockSpec(memory_space=pltpu.SMEM)
ANY = pl.BlockSpec(memory_space=pl.ANY)


def ring_order(count):
    if count == 8:
        return [0, 2, 4, 6, 7, 5, 3, 1]
    return list(range(count))


def owner_at(distance, count):
    me = lax.axis_index("tp")
    if count != 8:
        return lax.rem(me + distance, count)
    spot = jnp.where((me & 1) == 0, me >> 1, count - 1 - (me >> 1))
    spot = lax.rem(spot + distance, count)
    return jnp.where(spot < count // 2, 2 * spot, 2 * (count - 1 - spot) + 1)


def call(kernel, name, outs, ins, specs, out_specs, scratch=(), limit=16, flops=0, moved=0):
    return pl.pallas_call(
        kernel,
        out_shape=outs,
        in_specs=specs,
        out_specs=out_specs,
        scratch_shapes=list(scratch),
        compiler_params=pltpu.CompilerParams(vmem_limit_bytes=limit * MIB),
        cost_estimate=pl.CostEstimate(flops=flops, bytes_accessed=moved, transcendentals=0),
        name=name,
    )(*ins)


def attend_kernel(
    query_hbm, key_hbm, value_hbm, new_key_hbm, new_value_hbm, length_hbm, out_ref,
    q_ref, key_ref, value_ref, new_key_ref, new_value_ref, length_ref, sems,
):
    heads, rows, side = out_ref.shape
    cache = key_ref.shape[0] // rows
    small = [
        pltpu.make_async_copy(source, target, sems.at[i])
        for i, (source, target) in enumerate(
            ((length_hbm, length_ref), (query_hbm, q_ref), (new_key_hbm, new_key_ref),
             (new_value_hbm, new_value_ref))
        )
    ]
    tall_piece = key_ref.shape[0] // PIECES
    pieces = []
    for i in range(PIECES):
        for n, (source, target) in enumerate(((key_hbm, key_ref), (value_hbm, value_ref))):
            part = pl.ds(i * tall_piece, tall_piece)
            pieces.append(
                pltpu.make_async_copy(source.at[part], target.at[part], sems.at[4 + 2 * i + n])
            )
    for copy in small + pieces:
        copy.start()
    for copy in small:
        copy.wait()
    tall, wide = heads * ROW_BLOCK, cache * ROW_BLOCK
    scale = math.log2(math.e) / math.sqrt(side)
    lengths = jnp.transpose(jnp.broadcast_to(length_ref[...].astype(F32), (rows, rows)))[:, :1]
    row_in = lax.broadcasted_iota(jnp.int32, (tall, wide), 0) % ROW_BLOCK
    place = (lax.broadcasted_iota(jnp.int32, (tall, wide), 1) - cache * row_in).astype(F32)
    place = jnp.where(place < 0, 1e9, place)
    for r in range(0, rows, ROW_BLOCK):
        if r % (rows // PIECES) == 0:
            for copy in pieces[2 * (r * PIECES // rows) :][:2]:
                copy.wait()
        here = slice(r, r + ROW_BLOCK)
        cached = slice(r * cache, (r + ROW_BLOCK) * cache)
        query = jnp.concatenate(
            [q_ref[here, h * side : (h + 1) * side] for h in range(heads)], axis=0
        )
        new_key = jnp.concatenate([new_key_ref[here].astype(F32)] * heads, axis=0)
        new_value = jnp.concatenate([new_value_ref[here].astype(F32)] * heads, axis=0)
        live = place < jnp.concatenate([lengths[here]] * heads, axis=0)
        scores = lax.dot_general(query, key_ref[cached], NT, preferred_element_type=F32)
        fresh = jnp.sum(query.astype(F32) * new_key, axis=1, keepdims=True)
        scores = jnp.where(live, scores, -jnp.inf)
        top = jnp.maximum(jnp.max(scores, axis=1, keepdims=True), fresh)
        raw = jnp.exp2((scores - top) * scale)
        fresh_raw = jnp.exp2((fresh - top) * scale)
        inverse = 1.0 / (jnp.sum(raw, axis=1, keepdims=True) + fresh_raw)
        attended = jnp.dot(raw.astype(BF16), value_ref[cached], preferred_element_type=F32)
        attended = ((attended + fresh_raw * new_value) * inverse).astype(BF16)
        for h in range(heads):
            out_ref[h, here, :] = attended[h * ROW_BLOCK : (h + 1) * ROW_BLOCK]


def dense_kernel(distances, count, listing, turn, *refs):
    x_ref, weight_ref = refs[:2]
    outs = refs[-2 - 2 * listing - len(distances) : -2 - 2 * listing]
    buffers, sems = refs[-2:]
    heads, rows, side = x_ref.shape
    width = heads * side
    depth = buffers.shape[0]
    piece = buffers.shape[2]
    cuts = width // piece
    total = len(distances) * cuts

    def fetch(i):
        start = pl.multiple_of(owner_at(distances[i // cuts], count) * width, width) + i % cuts * piece
        return pltpu.make_async_copy(
            weight_ref.at[:, pl.ds(pl.multiple_of(start, piece), piece)],
            buffers.at[i % depth],
            sems.at[i % depth],
        )

    def compute():
        for i in range(min(depth, total)):
            fetch(i).start()
        if listing:
            list_blocks(refs[2], refs[3], refs[4], refs[-4], refs[-3])
        x = jnp.concatenate([x_ref[h] for h in range(heads)], axis=1)
        for i in range(total):
            fetch(i).wait()
            outs[i // cuts][:, i % cuts * piece : (i % cuts + 1) * piece] = jnp.dot(
                x, buffers[i % depth], preferred_element_type=F32
            )
            if i + depth < total:
                fetch(i + depth).start()

    if turn is None:
        compute()
        return
    here = lax.axis_index("rep") == turn
    pl.when(here)(compute)
    handed = refs[2 : -2 - len(distances)]
    if handed:

        @pl.when(jnp.logical_not(here))
        def _():
            for source, target in zip(handed, outs):
                target[...] = source[...]


def list_blocks(variant_ref, holder_ref, owner_ref, slot_ref, table_ref):
    rows = slot_ref.shape[0]
    slots = owner_ref.shape[0]
    variant = variant_ref[...]
    slot_row = jnp.zeros(variant.shape, jnp.int32)
    for v in range(holder_ref.shape[0]):
        slot_row = jnp.where(variant == v, holder_ref[v], slot_row)
    slot_row = (slot_row - lax.axis_index("tp") * slots).astype(F32)
    slot_ref[...] = jnp.transpose(jnp.broadcast_to(slot_row, (rows, rows))).astype(jnp.int32)
    for e in range(table_ref.shape[0]):
        table_ref[e] = -1
    for j in range(slots):

        def note(b, carry, j=j):
            e = (owner_ref[j, b] * slots + j) * CAP
            table_ref[e + jnp.where(table_ref[e] >= 0, 1, 0)] = b
            return carry

        lax.fori_loop(0, owner_ref.shape[1], note, 0)


def held_blocks(distance, count, slots, heads, scale_ref, cell_ref, table_ref):
    tiles = count * heads
    owner = owner_at(distance, count)
    listed = []
    for j in range(slots):
        for c in range(CAP):
            b = table_ref[(owner * slots + j) * CAP + c]
            found = jnp.maximum(b, 0)
            cell = cell_ref[j, found]
            scale = jnp.where(b >= 0, scale_ref[j, found], 0.0)
            listed.append((j, found, scale, lax.div(cell, tiles), lax.rem(cell, tiles)))
    return listed


def fold_chunk(distance, count, chunk_ref, slot, factor_ref, values_ref, scale_ref, cell_ref,
               table_ref, low_ref):
    heads, rows, side = chunk_ref.shape
    width = heads * side
    features = jnp.concatenate([chunk_ref[h] for h in range(heads)], axis=1)
    start = pl.multiple_of(owner_at(distance, count) * width, width)
    low_ref[...] += lax.dot_general(
        features, factor_ref[:, pl.ds(start, width)], NT, preferred_element_type=F32
    )
    added = []
    for j, b, scale, row_block, column in held_blocks(
        distance, count, values_ref.shape[0], heads, scale_ref, cell_ref, table_ref
    ):
        mine = jnp.where(slot == j, 1.0, 0.0)
        product = jnp.dot(chunk_ref[row_block], values_ref[j, b], preferred_element_type=F32)
        added.append((column, product * (mine * scale)))
    return added


def fold_kernel(distances, count, first, *refs):
    chunks, refs = refs[: len(distances)], refs[len(distances) :]
    slot_ref, factor_ref, values_ref, scale_ref, cell_ref, table_ref = refs[:6]
    low_ref, block_ref = refs[-2:]
    if first:
        low_ref[...] = jnp.zeros_like(low_ref)
        block_ref[...] = jnp.zeros_like(block_ref)
    else:
        low_ref[...] = refs[6][...]
        block_ref[...] = refs[7][...]
    slot = slot_ref[...]
    for distance, chunk in zip(distances, chunks):
        for column, product in fold_chunk(distance, count, chunk, slot, factor_ref, values_ref,
                                          scale_ref, cell_ref, table_ref, low_ref):
            block_ref[column] += product


def part_for(distance, count, low_ref, second_ref, dense_ref, block_ref, extra_ref, columns, out_ref):
    width = dense_ref.shape[1]
    side = block_ref.shape[2]
    heads = width // side
    owner = owner_at(distance, count)
    start = pl.multiple_of(owner * width, width)
    blocks = jnp.concatenate([block_ref[owner * heads + i] for i in range(heads)], axis=1)
    out_ref[...] = (
        jnp.dot(low_ref[...], second_ref[:, pl.ds(start, width)], preferred_element_type=F32)
        + dense_ref[...]
        + blocks
    )
    for e, column in enumerate(columns):

        @pl.when(lax.div(column, heads) == owner)
        def _(e=e, column=column):
            place = pl.ds(pl.multiple_of(lax.rem(column, heads) * side, side), side)
            out_ref[:, place] += extra_ref[e]


def finish_kernel(distances, count, *refs):
    front_ref, back_ref, slot_ref, factor_ref, values_ref, scale_ref, cell_ref, table_ref = refs[:8]
    second_ref, low_in, block_ref = refs[8:11]
    dense_refs, refs = refs[11 : 11 + len(distances)], refs[11 + len(distances) :]
    low_out, extra_out, front_out, back_out = refs[:4]
    outs, (chunk, low_sum, total) = refs[4:-3], refs[-3:]
    half, rows, side = front_ref.shape
    chunk[:half] = front_ref[...]
    chunk[half:] = back_ref[...]
    low_sum[...] = low_in[...]
    slot = slot_ref[...]
    added = fold_chunk(distances[0], count, chunk, slot, factor_ref, values_ref, scale_ref, cell_ref,
                       table_ref, low_sum)
    for e, (_, product) in enumerate(added):
        extra_out[e] = product
    columns = [column for column, _ in added]
    low_width = low_sum.shape[1]
    rank = low_width // values_ref.shape[0]
    held = lax.broadcasted_iota(jnp.int32, (rows, low_width), 1) // rank
    slots_wide = jnp.concatenate([slot] * -(-low_width // side), axis=1)[:, :low_width]
    low = jnp.where(slots_wide == held, low_sum[...], 0.0).astype(BF16)
    low_out[...] = low
    for n, (distance, dense_ref) in enumerate(zip(distances, dense_refs)):
        part_for(distance, count, low_out, second_ref, dense_ref, block_ref, extra_out, columns,
                 total.at[n])
        for i in range(2 * half):
            tile = total[n, :, i * side : (i + 1) * side].astype(BF16)
            if n:
                outs[n - 1][i] = tile
            elif i < half:
                front_out[i] = tile
            else:
                back_out[i - half] = tile


def part_kernel(distances, count, slots, *refs):
    low_ref, second_ref, block_ref, extra_ref, scale_ref, cell_ref, table_ref = refs[:7]
    dense_refs, refs = refs[7 : 7 + len(distances)], refs[7 + len(distances) :]
    outs, total = refs[:-1], refs[-1]
    side = block_ref.shape[2]
    heads = dense_refs[0].shape[1] // side
    listed = held_blocks(count // 2, count, slots, heads, scale_ref, cell_ref, table_ref)
    columns = [entry[-1] for entry in listed]
    for n, (distance, dense_ref) in enumerate(zip(distances, dense_refs)):
        part_for(distance, count, low_ref, second_ref, dense_ref, block_ref, extra_ref, columns,
                 total.at[n])
        for i in range(heads):
            outs[n][i] = total[n, :, i * side : (i + 1) * side].astype(outs[n].dtype)


def sum_kernel(own_ref, *refs):
    out_ref = refs[-1]
    heads, _, side = own_ref.shape
    for i in range(heads):
        total = own_ref[i]
        for ref in refs[:-1]:
            total = total + ref[i].astype(F32)
        out_ref[:, i * side : (i + 1) * side] = total.astype(BF16)


def after(value, *others):
    return lax.optimization_barrier((value, *others))[0]


def body(
    queries, key_cache, value_cache, new_keys, new_values, lengths, request_variant, holder_slot,
    out_weight, factor_in, second_factor, block_values, block_scale, block_owner, block_cell,
):
    count = lax.axis_size("tp")
    half = count // 2
    ring = ring_order(count)
    rows, width = queries.shape
    side = key_cache.shape[3]
    cache = key_cache.shape[2]
    heads = width // side
    slots = block_values.shape[0]
    complete = out_weight.shape[1]
    low_width = slots * factor_in.shape[2]
    shape = jax.ShapeDtypeStruct

    attended = call(
        attend_kernel,
        "attend",
        shape((heads, rows, side), BF16),
        (queries, key_cache.reshape(-1, side), value_cache.reshape(-1, side), new_keys[0],
         new_values[0], lengths[None, :]),
        [ANY] * 6,
        VMEM,
        [pltpu.VMEM((rows, width), BF16), pltpu.VMEM((rows * cache, side), BF16),
         pltpu.VMEM((rows * cache, side), BF16), pltpu.VMEM((rows, side), BF16),
         pltpu.VMEM((rows, side), BF16), pltpu.VMEM((1, rows), jnp.int32),
         pltpu.SemaphoreType.DMA((4 + 2 * PIECES,))],
        limit=60,
    )

    wanted = [half]
    for distance in range(half - 1, 0, -1):
        wanted += [distance, count - distance]
    wanted += [0]
    piece = width // 2 if width >= 512 else width
    dense = {}

    def dense_for(distances, x, listing=False, turn=None, handed=()):
        extra_shapes = [shape((rows, rows), jnp.int32), shape((count * slots * CAP,), jnp.int32)]
        extra_ins = (request_variant[None, :], holder_slot, block_owner[:, :, 0])
        got = call(
            functools.partial(dense_kernel, distances, count, listing, turn),
            "dense",
            [shape((rows, width), F32)] * len(distances) + extra_shapes * listing,
            (x, out_weight) + extra_ins * listing + tuple(handed),
            [VMEM, ANY] + [VMEM, SMEM, SMEM] * listing + [VMEM] * len(handed),
            [VMEM] * len(distances) + [VMEM, SMEM] * listing,
            [pltpu.VMEM((4, width, piece), BF16), pltpu.SemaphoreType.DMA((4,))],
            limit=40,
            flops=2 * rows * width * width * len(distances),
            moved=2 * width * width * len(distances),
        )
        dense.update(zip(distances, got))
        return got[len(distances) :] if listing else got

    def come(value, distance):
        return lax.ppermute(
            value, "tp", [(ring[(i + distance) % count], ring[i]) for i in range(count)]
        )

    begun = dense_for(wanted[:3], attended, turn=1)
    attended = after(attended, begun[0])
    chunks = {0: attended}
    chunks[1], chunks[count - 1] = come(attended, 1), come(attended, -1)
    (token, *_) = dense_for(wanted[:3], attended, turn=0, handed=begun)
    for step in range(2, half):
        right, left = after(chunks[step - 1], token), after(chunks[count - step + 1], token)
        chunks[step], chunks[count - step] = come(right, 1), come(left, -1)
        if step == 2:
            slot, table = dense_for(wanted[3:5], after(attended, token), True)
            token = slot
    right, left = chunks[half - 1], chunks[half + 1]

    factor_t = jnp.swapaxes(factor_in, 1, 2).reshape(low_width, -1)
    second = second_factor.reshape(low_width, complete)
    state = [shape((rows, low_width), F32), shape((complete // side, rows, side), F32)]
    early = [0]
    for distance in range(1, half - 1):
        early += [distance, count - distance]
    late = [half - 1, count - half + 1]
    tables = (slot, factor_t, block_values, block_scale, block_cell, table)
    table_specs = [VMEM, VMEM, VMEM, SMEM, SMEM, SMEM]
    low, blocks = call(
        functools.partial(fold_kernel, early, count, True),
        "fold_early",
        state,
        (*[chunks[d] for d in early], *tables),
        [VMEM] * len(early) + table_specs,
        [VMEM] * 2,
        flops=rows * low_width * complete,
        moved=4 * MIB,
    )
    right, left = after(right, low), after(left, low)
    front, back = come(right[: heads // 2], 1), come(left[heads // 2 :], -1)
    low, blocks = call(
        functools.partial(fold_kernel, late, count, False),
        "fold_late",
        state,
        (*[chunks[d] for d in late], *tables, low, blocks),
        [VMEM] * len(late) + table_specs + [VMEM] * 2,
        [VMEM] * 2,
        flops=rows * low_width * width * 4,
        moved=MIB,
    )
    extras = shape((slots * CAP, rows, side), F32)
    first = wanted[:1]
    travelling = shape((heads, rows, side), BF16)
    low, extra, front, back, *sums = call(
        functools.partial(finish_kernel, first, count),
        "finish",
        [shape((rows, low_width), BF16), extras]
        + [shape((heads // 2, rows, side), BF16)] * 2
        + [travelling] * (len(first) - 1),
        (front, back, *tables, second, low, blocks, *[dense[d] for d in first]),
        [VMEM] * 2 + table_specs + [VMEM] * (3 + len(first)),
        [VMEM] * (3 + len(first)),
        [pltpu.VMEM((heads, rows, side), BF16), pltpu.VMEM((rows, low_width), F32),
         pltpu.VMEM((len(first), rows, width), F32)],
        flops=rows * low_width * width * 8,
        moved=2 * MIB,
    )
    parts = dict(zip(first[1:], sums))

    def parts_for(distances, low, kind):
        got = call(
            functools.partial(part_kernel, distances, count, slots),
            "part",
            [shape((heads, rows, side), kind)] * len(distances),
            (low, second, blocks, extra, block_scale, block_cell, table,
             *[dense[distance] for distance in distances]),
            [VMEM] * 4 + [SMEM] * 3 + [VMEM] * len(distances),
            [VMEM] * len(distances),
            [pltpu.VMEM((len(distances), rows, width), F32)],
            flops=rows * low_width * width * 2,
            moved=MIB,
        )
        parts.update(zip(distances, got))

    def joined(part, *came):
        total = part.astype(F32)
        for value, place in came:
            value = value.astype(F32)
            if place is not None:
                none = jnp.zeros_like(value)
                value = jnp.concatenate([none, value] if place else [value, none], axis=0)
            total = total + value
        return total.astype(BF16)

    begun = dense_for(wanted[5:-1], after(attended, low), turn=1)
    front, back = after(front, begun[0]), after(back, begun[0])
    left, right = (come(front, 1), 0), (come(back, -1), 1)
    parts_for([half - 1, half + 1], after(low, begun[0]), F32)
    for distance in range(half - 1, 0, -1):
        left = joined(parts[count - distance], left)
        right = joined(parts[distance], right)
        nearer = distance - 1
        kept = after(low, right)
        parts_for([nearer, count - nearer] if nearer else [0], kept, F32)
        if distance == half - 1:
            dense_for(wanted[5:-1], after(attended, right), turn=0, handed=begun)
        if distance == half - 2:
            dense_for([0], after(attended, right))
        left, right = (come(left, 1), None), (come(right, -1), None)
    came = [left[0], right[0]]
    return call(
        sum_kernel,
        "sum_up",
        shape((rows, width), BF16),
        (parts[0], *came),
        [VMEM] * (1 + len(came)),
        VMEM,
        flops=1,
        moved=1,
    )


def solution(mesh):
    return jax.shard_map(
        body,
        mesh=mesh,
        in_specs=(
            P(("groups", "rep"), "tp"),
            P("tp", ("groups", "rep"), None, None),
            P("tp", ("groups", "rep"), None, None),
            P("tp", ("groups", "rep"), None),
            P("tp", ("groups", "rep"), None),
            P(("groups", "rep")),
            P(("groups", "rep")),
            P(),
            P("tp", None),
            P("tp", None, None),
            P("tp", None, None),
            P("tp", None, None, None),
            P("tp", None),
            P("tp", None, None),
            P("tp", None),
        ),
        out_specs=P(("groups", "rep"), "tp"),
        check_vma=False,
    )
```

```python
import functools
import math

import jax
import jax.numpy as jnp
from jax import lax
from jax.experimental import pallas as pl
from jax.experimental.pallas import tpu as pltpu
from jax.sharding import PartitionSpec as P

BF16 = jnp.bfloat16
F32 = jnp.float32
CAP = 2
ROW_BLOCK = 16
PIECES = 4
MIB = 1024 * 1024
NT = (((1,), (1,)), ((), ()))
VMEM = pl.BlockSpec(memory_space=pltpu.VMEM)
SMEM = pl.BlockSpec(memory_space=pltpu.SMEM)
ANY = pl.BlockSpec(memory_space=pl.ANY)


def ring_order(count):
    if count == 8:
        return [0, 2, 4, 6, 7, 5, 3, 1]
    return list(range(count))


def owner_at(distance, count):
    me = lax.axis_index("tp")
    if count != 8:
        return lax.rem(me + distance, count)
    spot = jnp.where((me & 1) == 0, me >> 1, count - 1 - (me >> 1))
    spot = lax.rem(spot + distance, count)
    return jnp.where(spot < count // 2, 2 * spot, 2 * (count - 1 - spot) + 1)


def call(kernel, name, outs, ins, specs, out_specs, scratch=(), limit=16, flops=0, moved=0):
    return pl.pallas_call(
        kernel,
        out_shape=outs,
        in_specs=specs,
        out_specs=out_specs,
        scratch_shapes=list(scratch),
        compiler_params=pltpu.CompilerParams(vmem_limit_bytes=limit * MIB),
        cost_estimate=pl.CostEstimate(flops=flops, bytes_accessed=moved, transcendentals=0),
        name=name,
    )(*ins)


def attend_kernel(
    query_hbm, key_hbm, value_hbm, new_key_hbm, new_value_hbm, length_hbm, out_ref,
    q_ref, key_ref, value_ref, new_key_ref, new_value_ref, length_ref, sems,
):
    heads, rows, side = out_ref.shape
    cache = key_ref.shape[0] // rows
    small = [
        pltpu.make_async_copy(source, target, sems.at[i])
        for i, (source, target) in enumerate(
            ((length_hbm, length_ref), (query_hbm, q_ref), (new_key_hbm, new_key_ref),
             (new_value_hbm, new_value_ref))
        )
    ]
    tall_piece = key_ref.shape[0] // PIECES
    pieces = []
    for i in range(PIECES):
        for n, (source, target) in enumerate(((key_hbm, key_ref), (value_hbm, value_ref))):
            part = pl.ds(i * tall_piece, tall_piece)
            pieces.append(
                pltpu.make_async_copy(source.at[part], target.at[part], sems.at[4 + 2 * i + n])
            )
    for copy in small + pieces:
        copy.start()
    for copy in small:
        copy.wait()
    tall, wide = heads * ROW_BLOCK, cache * ROW_BLOCK
    scale = math.log2(math.e) / math.sqrt(side)
    lengths = jnp.transpose(jnp.broadcast_to(length_ref[...].astype(F32), (rows, rows)))[:, :1]
    row_in = lax.broadcasted_iota(jnp.int32, (tall, wide), 0) % ROW_BLOCK
    place = (lax.broadcasted_iota(jnp.int32, (tall, wide), 1) - cache * row_in).astype(F32)
    place = jnp.where(place < 0, 1e9, place)
    for r in range(0, rows, ROW_BLOCK):
        if r % (rows // PIECES) == 0:
            for copy in pieces[2 * (r * PIECES // rows) :][:2]:
                copy.wait()
        here = slice(r, r + ROW_BLOCK)
        cached = slice(r * cache, (r + ROW_BLOCK) * cache)
        query = jnp.concatenate(
            [q_ref[here, h * side : (h + 1) * side] for h in range(heads)], axis=0
        )
        new_key = jnp.concatenate([new_key_ref[here].astype(F32)] * heads, axis=0)
        new_value = jnp.concatenate([new_value_ref[here].astype(F32)] * heads, axis=0)
        live = place < jnp.concatenate([lengths[here]] * heads, axis=0)
        scores = lax.dot_general(query, key_ref[cached], NT, preferred_element_type=F32)
        fresh = jnp.sum(query.astype(F32) * new_key, axis=1, keepdims=True)
        scores = jnp.where(live, scores, -jnp.inf)
        top = jnp.maximum(jnp.max(scores, axis=1, keepdims=True), fresh)
        raw = jnp.exp2((scores - top) * scale)
        fresh_raw = jnp.exp2((fresh - top) * scale)
        inverse = 1.0 / (jnp.sum(raw, axis=1, keepdims=True) + fresh_raw)
        attended = jnp.dot(raw.astype(BF16), value_ref[cached], preferred_element_type=F32)
        attended = ((attended + fresh_raw * new_value) * inverse).astype(BF16)
        for h in range(heads):
            out_ref[h, here, :] = attended[h * ROW_BLOCK : (h + 1) * ROW_BLOCK]


def dense_kernel(distances, count, listing, turn, kept, *refs):
    x_hbm, weight_ref = refs[:2]
    outs = refs[-4 - 2 * listing - len(distances) : -4 - 2 * listing]
    x_ref, buffers, sems, x_sem = refs[-4:]
    heads, rows, side = x_ref.shape
    width = heads * side
    depth = buffers.shape[0]
    piece = buffers.shape[2]
    cuts = width // piece

    def compute(first):
        total = len(distances) * cuts

        def fetch(i):
            owner = owner_at(distances[i // cuts], count)
            start = pl.multiple_of(owner * width, width) + i % cuts * piece
            return pltpu.make_async_copy(
                weight_ref.at[:, pl.ds(pl.multiple_of(start, piece), piece)],
                buffers.at[i % depth],
                sems.at[i % depth],
            )

        own = pltpu.make_async_copy(x_hbm, x_ref, x_sem)
        own.start()
        for i in range(first * cuts, min(first * cuts + depth, total)):
            fetch(i).start()
        if listing:
            list_blocks(refs[2], refs[3], refs[4], refs[-6], refs[-5])
        own.wait()
        x = jnp.concatenate([x_ref[h] for h in range(heads)], axis=1)
        for i in range(first * cuts, total):
            fetch(i).wait()
            outs[i // cuts][:, i % cuts * piece : (i % cuts + 1) * piece] = jnp.dot(
                x, buffers[i % depth], preferred_element_type=F32
            )
            if i + depth < total:
                fetch(i + depth).start()

    if turn is None:
        compute(0)
        return
    here = lax.axis_index("rep") == turn
    pl.when(here)(functools.partial(compute, 0))

    @pl.when(jnp.logical_not(here))
    def _():
        handed = refs[2 : -4 - len(distances)]
        for source, target in zip(handed, outs):
            target[...] = source[...]
        if kept < len(distances):
            compute(kept)


def list_blocks(variant_ref, holder_ref, owner_ref, slot_ref, table_ref):
    rows = slot_ref.shape[0]
    slots = owner_ref.shape[0]
    variant = variant_ref[...]
    slot_row = jnp.zeros(variant.shape, jnp.int32)
    for v in range(holder_ref.shape[0]):
        slot_row = jnp.where(variant == v, holder_ref[v], slot_row)
    slot_row = (slot_row - lax.axis_index("tp") * slots).astype(F32)
    slot_ref[...] = jnp.transpose(jnp.broadcast_to(slot_row, (rows, rows))).astype(jnp.int32)
    for e in range(table_ref.shape[0]):
        table_ref[e] = -1
    for j in range(slots):

        def note(b, carry, j=j):
            e = (owner_ref[j, b] * slots + j) * CAP
            table_ref[e + jnp.where(table_ref[e] >= 0, 1, 0)] = b
            return carry

        lax.fori_loop(0, owner_ref.shape[1], note, 0)


def held_blocks(distance, count, slots, heads, scale_ref, cell_ref, table_ref):
    tiles = count * heads
    owner = owner_at(distance, count)
    listed = []
    for j in range(slots):
        for c in range(CAP):
            b = table_ref[(owner * slots + j) * CAP + c]
            found = jnp.maximum(b, 0)
            cell = cell_ref[j, found]
            scale = jnp.where(b >= 0, scale_ref[j, found], 0.0)
            listed.append((j, found, scale, lax.div(cell, tiles), lax.rem(cell, tiles)))
    return listed


def fold_chunk(distance, count, chunk_ref, slot, factor_ref, values_ref, scale_ref, cell_ref,
               table_ref, low_ref):
    heads, rows, side = chunk_ref.shape
    width = heads * side
    features = jnp.concatenate([chunk_ref[h] for h in range(heads)], axis=1)
    start = pl.multiple_of(owner_at(distance, count) * width, width)
    low_ref[...] += lax.dot_general(
        features, factor_ref[:, pl.ds(start, width)], NT, preferred_element_type=F32
    )
    added = []
    for j, b, scale, row_block, column in held_blocks(
        distance, count, values_ref.shape[0], heads, scale_ref, cell_ref, table_ref
    ):
        mine = jnp.where(slot == j, 1.0, 0.0)
        product = jnp.dot(chunk_ref[row_block], values_ref[j, b], preferred_element_type=F32)
        added.append((column, product * (mine * scale)))
    return added


def fold_kernel(distances, count, first, *refs):
    chunks, refs = refs[: len(distances)], refs[len(distances) :]
    slot_ref, factor_ref, values_ref, scale_ref, cell_ref, table_ref = refs[:6]
    low_ref, block_ref = refs[-2:]
    if first:
        low_ref[...] = jnp.zeros_like(low_ref)
        block_ref[...] = jnp.zeros_like(block_ref)
    else:
        low_ref[...] = refs[6][...]
        block_ref[...] = refs[7][...]
    slot = slot_ref[...]
    for distance, chunk in zip(distances, chunks):
        for column, product in fold_chunk(distance, count, chunk, slot, factor_ref, values_ref,
                                          scale_ref, cell_ref, table_ref, low_ref):
            block_ref[column] += product


def part_for(distance, count, low_ref, second_ref, dense_ref, block_ref, extra_ref, columns, out_ref):
    width = dense_ref.shape[1]
    side = block_ref.shape[2]
    heads = width // side
    owner = owner_at(distance, count)
    start = pl.multiple_of(owner * width, width)
    blocks = jnp.concatenate([block_ref[owner * heads + i] for i in range(heads)], axis=1)
    out_ref[...] = (
        jnp.dot(low_ref[...], second_ref[:, pl.ds(start, width)], preferred_element_type=F32)
        + dense_ref[...]
        + blocks
    )
    for e, column in enumerate(columns):

        @pl.when(lax.div(column, heads) == owner)
        def _(e=e, column=column):
            place = pl.ds(pl.multiple_of(lax.rem(column, heads) * side, side), side)
            out_ref[:, place] += extra_ref[e]


def finish_kernel(distances, count, *refs):
    front_ref, back_ref, slot_ref, factor_ref, values_ref, scale_ref, cell_ref, table_ref = refs[:8]
    second_ref, low_in, block_ref = refs[8:11]
    dense_refs, refs = refs[11 : 11 + len(distances)], refs[11 + len(distances) :]
    low_out, extra_out, front_out, back_out = refs[:4]
    outs, (chunk, low_sum, total) = refs[4:-3], refs[-3:]
    half, rows, side = front_ref.shape
    chunk[:half] = front_ref[...]
    chunk[half:] = back_ref[...]
    low_sum[...] = low_in[...]
    slot = slot_ref[...]
    added = fold_chunk(distances[0], count, chunk, slot, factor_ref, values_ref, scale_ref, cell_ref,
                       table_ref, low_sum)
    for e, (_, product) in enumerate(added):
        extra_out[e] = product
    columns = [column for column, _ in added]
    low_width = low_sum.shape[1]
    rank = low_width // values_ref.shape[0]
    held = lax.broadcasted_iota(jnp.int32, (rows, low_width), 1) // rank
    slots_wide = jnp.concatenate([slot] * -(-low_width // side), axis=1)[:, :low_width]
    low = jnp.where(slots_wide == held, low_sum[...], 0.0).astype(BF16)
    low_out[...] = low
    for n, (distance, dense_ref) in enumerate(zip(distances, dense_refs)):
        part_for(distance, count, low_out, second_ref, dense_ref, block_ref, extra_out, columns,
                 total.at[n])
        for i in range(2 * half):
            tile = total[n, :, i * side : (i + 1) * side].astype(BF16)
            if n:
                outs[n - 1][i] = tile
            elif i < half:
                front_out[i] = tile
            else:
                back_out[i - half] = tile


def part_kernel(distances, count, slots, *refs):
    low_ref, second_ref, block_ref, extra_ref, scale_ref, cell_ref, table_ref = refs[:7]
    dense_refs, refs = refs[7 : 7 + len(distances)], refs[7 + len(distances) :]
    outs, total = refs[:-1], refs[-1]
    side = block_ref.shape[2]
    heads = dense_refs[0].shape[1] // side
    listed = held_blocks(count // 2, count, slots, heads, scale_ref, cell_ref, table_ref)
    columns = [entry[-1] for entry in listed]
    for n, (distance, dense_ref) in enumerate(zip(distances, dense_refs)):
        part_for(distance, count, low_ref, second_ref, dense_ref, block_ref, extra_ref, columns,
                 total.at[n])
        for i in range(heads):
            outs[n][i] = total[n, :, i * side : (i + 1) * side].astype(outs[n].dtype)


def sum_kernel(own_ref, *refs):
    out_ref = refs[-1]
    heads, _, side = own_ref.shape
    for i in range(heads):
        total = own_ref[i]
        for ref in refs[:-1]:
            total = total + ref[i].astype(F32)
        out_ref[:, i * side : (i + 1) * side] = total.astype(BF16)


def after(value, *others):
    return lax.optimization_barrier((value, *others))[0]


def body(
    queries, key_cache, value_cache, new_keys, new_values, lengths, request_variant, holder_slot,
    out_weight, factor_in, second_factor, block_values, block_scale, block_owner, block_cell,
):
    count = lax.axis_size("tp")
    half = count // 2
    ring = ring_order(count)
    rows, width = queries.shape
    side = key_cache.shape[3]
    cache = key_cache.shape[2]
    heads = width // side
    slots = block_values.shape[0]
    complete = out_weight.shape[1]
    low_width = slots * factor_in.shape[2]
    shape = jax.ShapeDtypeStruct

    attended = call(
        attend_kernel,
        "attend",
        shape((heads, rows, side), BF16),
        (queries, key_cache.reshape(-1, side), value_cache.reshape(-1, side), new_keys[0],
         new_values[0], lengths[None, :]),
        [ANY] * 6,
        VMEM,
        [pltpu.VMEM((rows, width), BF16), pltpu.VMEM((rows * cache, side), BF16),
         pltpu.VMEM((rows * cache, side), BF16), pltpu.VMEM((rows, side), BF16),
         pltpu.VMEM((rows, side), BF16), pltpu.VMEM((1, rows), jnp.int32),
         pltpu.SemaphoreType.DMA((4 + 2 * PIECES,))],
        limit=60,
    )

    wanted = [half]
    for distance in range(half - 1, 0, -1):
        wanted += [distance, count - distance]
    wanted += [0]
    piece = width // 2 if width >= 512 else width
    dense = {}

    def dense_for(distances, x, listing=False, turn=None, handed=(), kept=0, limit=40):
        extra_shapes = [shape((rows, rows), jnp.int32), shape((count * slots * CAP,), jnp.int32)]
        extra_ins = (request_variant[None, :], holder_slot, block_owner[:, :, 0])
        got = call(
            functools.partial(dense_kernel, distances, count, listing, turn, kept),
            "dense",
            [shape((rows, width), F32)] * len(distances) + extra_shapes * listing,
            (x, out_weight) + extra_ins * listing + tuple(handed),
            [ANY, ANY] + [VMEM, SMEM, SMEM] * listing + [VMEM] * len(handed),
            [VMEM] * len(distances) + [VMEM, SMEM] * listing,
            [pltpu.VMEM((heads, rows, side), BF16), pltpu.VMEM((4, width, piece), BF16),
             pltpu.SemaphoreType.DMA((4,)), pltpu.SemaphoreType.DMA],
            limit=limit,
            flops=2 * rows * width * width * len(distances),
            moved=2 * width * width * len(distances),
        )
        dense.update(zip(distances, got))
        return got[len(distances) :] if listing else got

    def come(value, distance):
        return lax.ppermute(
            value, "tp", [(ring[(i + distance) % count], ring[i]) for i in range(count)]
        )

    begun = dense_for(wanted[:1], attended, turn=0, kept=1, limit=60)
    attended = after(attended, begun[0])
    chunks = {0: attended}
    chunks[1], chunks[count - 1] = come(attended, 1), come(attended, -1)
    (token, *_) = dense_for(wanted[:3], attended, turn=1, handed=begun, kept=1)
    for step in range(2, half):
        right, left = after(chunks[step - 1], token), after(chunks[count - step + 1], token)
        chunks[step], chunks[count - step] = come(right, 1), come(left, -1)
        if step == 2:
            slot, table = dense_for(wanted[3:5], after(attended, token), True)
            token = slot
    right, left = chunks[half - 1], chunks[half + 1]

    factor_t = jnp.swapaxes(factor_in, 1, 2).reshape(low_width, -1)
    second = second_factor.reshape(low_width, complete)
    state = [shape((rows, low_width), F32), shape((complete // side, rows, side), F32)]
    early = [0]
    for distance in range(1, half - 1):
        early += [distance, count - distance]
    late = [half - 1, count - half + 1]
    tables = (slot, factor_t, block_values, block_scale, block_cell, table)
    table_specs = [VMEM, VMEM, VMEM, SMEM, SMEM, SMEM]
    low, blocks = call(
        functools.partial(fold_kernel, early, count, True),
        "fold_early",
        state,
        (*[chunks[d] for d in early], *tables),
        [VMEM] * len(early) + table_specs,
        [VMEM] * 2,
        flops=rows * low_width * complete,
        moved=4 * MIB,
    )
    right, left = after(right, low), after(left, low)
    front, back = come(right[: heads // 2], 1), come(left[heads // 2 :], -1)
    low, blocks = call(
        functools.partial(fold_kernel, late, count, False),
        "fold_late",
        state,
        (*[chunks[d] for d in late], *tables, low, blocks),
        [VMEM] * len(late) + table_specs + [VMEM] * 2,
        [VMEM] * 2,
        flops=rows * low_width * width * 4,
        moved=MIB,
    )
    extras = shape((slots * CAP, rows, side), F32)
    first = wanted[:1]
    travelling = shape((heads, rows, side), BF16)
    low, extra, front, back, *sums = call(
        functools.partial(finish_kernel, first, count),
        "finish",
        [shape((rows, low_width), BF16), extras]
        + [shape((heads // 2, rows, side), BF16)] * 2
        + [travelling] * (len(first) - 1),
        (front, back, *tables, second, low, blocks, *[dense[d] for d in first]),
        [VMEM] * 2 + table_specs + [VMEM] * (3 + len(first)),
        [VMEM] * (3 + len(first)),
        [pltpu.VMEM((heads, rows, side), BF16), pltpu.VMEM((rows, low_width), F32),
         pltpu.VMEM((len(first), rows, width), F32)],
        flops=rows * low_width * width * 8,
        moved=2 * MIB,
    )
    parts = dict(zip(first[1:], sums))

    def parts_for(distances, low, kind):
        got = call(
            functools.partial(part_kernel, distances, count, slots),
            "part",
            [shape((heads, rows, side), kind)] * len(distances),
            (low, second, blocks, extra, block_scale, block_cell, table,
             *[dense[distance] for distance in distances]),
            [VMEM] * 4 + [SMEM] * 3 + [VMEM] * len(distances),
            [VMEM] * len(distances),
            [pltpu.VMEM((len(distances), rows, width), F32)],
            flops=rows * low_width * width * 2,
            moved=MIB,
        )
        parts.update(zip(distances, got))

    def joined(part, *came):
        total = part.astype(F32)
        for value, place in came:
            value = value.astype(F32)
            if place is not None:
                none = jnp.zeros_like(value)
                value = jnp.concatenate([none, value] if place else [value, none], axis=0)
            total = total + value
        return total.astype(BF16)

    near = wanted[5:-1]
    begun = dense_for(near, after(attended, low), turn=1, kept=len(near))
    front, back = after(front, begun[0]), after(back, begun[0])
    left, right = (come(front, 1), 0), (come(back, -1), 1)
    parts_for([half - 1, half + 1], after(low, begun[0]), F32)
    for distance in range(half - 1, 0, -1):
        left = joined(parts[count - distance], left)
        right = joined(parts[distance], right)
        nearer = distance - 1
        kept = after(low, right)
        parts_for([nearer, count - nearer] if nearer else [0], kept, F32)
        if distance == half - 1:
            dense_for(near, after(attended, right), turn=0, handed=begun, kept=len(near))
        if distance == half - 2:
            dense_for([0], after(attended, right))
        left, right = (come(left, 1), None), (come(right, -1), None)
    came = [left[0], right[0]]
    return call(
        sum_kernel,
        "sum_up",
        shape((rows, width), BF16),
        (parts[0], *came),
        [VMEM] * (1 + len(came)),
        VMEM,
        flops=1,
        moved=1,
    )


def solution(mesh):
    return jax.shard_map(
        body,
        mesh=mesh,
        in_specs=(
            P(("groups", "rep"), "tp"),
            P("tp", ("groups", "rep"), None, None),
            P("tp", ("groups", "rep"), None, None),
            P("tp", ("groups", "rep"), None),
            P("tp", ("groups", "rep"), None),
            P(("groups", "rep")),
            P(("groups", "rep")),
            P(),
            P("tp", None),
            P("tp", None, None),
            P("tp", None, None),
            P("tp", None, None, None),
            P("tp", None),
            P("tp", None, None),
            P("tp", None),
        ),
        out_specs=P(("groups", "rep"), "tp"),
        check_vma=False,
    )
```

```python
import functools
import math

import jax
import jax.numpy as jnp
from jax import lax
from jax.experimental import pallas as pl
from jax.experimental.pallas import tpu as pltpu
from jax.sharding import PartitionSpec as P

BF16 = jnp.bfloat16
F32 = jnp.float32
CAP = 2
ROW_BLOCK = 16
PIECES = 4
MIB = 1024 * 1024
NT = (((1,), (1,)), ((), ()))
VMEM = pl.BlockSpec(memory_space=pltpu.VMEM)
SMEM = pl.BlockSpec(memory_space=pltpu.SMEM)
ANY = pl.BlockSpec(memory_space=pl.ANY)


def ring_order(count):
    if count == 8:
        return [0, 2, 4, 6, 7, 5, 3, 1]
    return list(range(count))


def owner_at(distance, count):
    me = lax.axis_index("tp")
    if count != 8:
        return lax.rem(me + distance, count)
    spot = jnp.where((me & 1) == 0, me >> 1, count - 1 - (me >> 1))
    spot = lax.rem(spot + distance, count)
    return jnp.where(spot < count // 2, 2 * spot, 2 * (count - 1 - spot) + 1)


def call(kernel, name, outs, ins, specs, out_specs, scratch=(), limit=16, flops=0, moved=0):
    return pl.pallas_call(
        kernel,
        out_shape=outs,
        in_specs=specs,
        out_specs=out_specs,
        scratch_shapes=list(scratch),
        compiler_params=pltpu.CompilerParams(vmem_limit_bytes=limit * MIB),
        cost_estimate=pl.CostEstimate(flops=flops, bytes_accessed=moved, transcendentals=0),
        name=name,
    )(*ins)


def attend_kernel(
    query_hbm, key_hbm, value_hbm, new_key_hbm, new_value_hbm, length_hbm, out_ref,
    q_ref, key_ref, value_ref, new_key_ref, new_value_ref, length_ref, sems,
):
    heads, rows, side = out_ref.shape
    cache = key_ref.shape[0] // rows
    small = [
        pltpu.make_async_copy(source, target, sems.at[i])
        for i, (source, target) in enumerate(
            ((length_hbm, length_ref), (query_hbm, q_ref), (new_key_hbm, new_key_ref),
             (new_value_hbm, new_value_ref))
        )
    ]
    tall_piece = key_ref.shape[0] // PIECES
    pieces = []
    for i in range(PIECES):
        for n, (source, target) in enumerate(((key_hbm, key_ref), (value_hbm, value_ref))):
            part = pl.ds(i * tall_piece, tall_piece)
            pieces.append(
                pltpu.make_async_copy(source.at[part], target.at[part], sems.at[4 + 2 * i + n])
            )
    for copy in small + pieces:
        copy.start()
    for copy in small:
        copy.wait()
    tall, wide = heads * ROW_BLOCK, cache * ROW_BLOCK
    scale = math.log2(math.e) / math.sqrt(side)
    lengths = jnp.transpose(jnp.broadcast_to(length_ref[...].astype(F32), (rows, rows)))[:, :1]
    row_in = lax.broadcasted_iota(jnp.int32, (tall, wide), 0) % ROW_BLOCK
    place = (lax.broadcasted_iota(jnp.int32, (tall, wide), 1) - cache * row_in).astype(F32)
    place = jnp.where(place < 0, 1e9, place)
    for r in range(0, rows, ROW_BLOCK):
        if r % (rows // PIECES) == 0:
            for copy in pieces[2 * (r * PIECES // rows) :][:2]:
                copy.wait()
        here = slice(r, r + ROW_BLOCK)
        cached = slice(r * cache, (r + ROW_BLOCK) * cache)
        query = jnp.concatenate(
            [q_ref[here, h * side : (h + 1) * side] for h in range(heads)], axis=0
        )
        new_key = jnp.concatenate([new_key_ref[here].astype(F32)] * heads, axis=0)
        new_value = jnp.concatenate([new_value_ref[here].astype(F32)] * heads, axis=0)
        live = place < jnp.concatenate([lengths[here]] * heads, axis=0)
        scores = lax.dot_general(query, key_ref[cached], NT, preferred_element_type=F32)
        fresh = jnp.sum(query.astype(F32) * new_key, axis=1, keepdims=True)
        scores = jnp.where(live, scores, -jnp.inf)
        top = jnp.maximum(jnp.max(scores, axis=1, keepdims=True), fresh)
        raw = jnp.exp2((scores - top) * scale)
        fresh_raw = jnp.exp2((fresh - top) * scale)
        inverse = 1.0 / (jnp.sum(raw, axis=1, keepdims=True) + fresh_raw)
        attended = jnp.dot(raw.astype(BF16), value_ref[cached], preferred_element_type=F32)
        attended = ((attended + fresh_raw * new_value) * inverse).astype(BF16)
        for h in range(heads):
            out_ref[h, here, :] = attended[h * ROW_BLOCK : (h + 1) * ROW_BLOCK]


def dense_kernel(distances, count, listing, *refs):
    x_ref, weight_ref = refs[:2]
    outs = refs[-2 - 2 * listing - len(distances) : -2 - 2 * listing]
    buffers, sems = refs[-2:]
    heads, rows, side = x_ref.shape
    width = heads * side
    depth = buffers.shape[0]
    piece = buffers.shape[2]
    cuts = width // piece
    total = len(distances) * cuts

    def fetch(i):
        start = pl.multiple_of(owner_at(distances[i // cuts], count) * width, width) + i % cuts * piece
        return pltpu.make_async_copy(
            weight_ref.at[:, pl.ds(pl.multiple_of(start, piece), piece)],
            buffers.at[i % depth],
            sems.at[i % depth],
        )

    for i in range(min(depth, total)):
        fetch(i).start()
    if listing:
        list_blocks(refs[2], refs[3], refs[4], refs[-4], refs[-3])
    x = jnp.concatenate([x_ref[h] for h in range(heads)], axis=1)
    for i in range(total):
        fetch(i).wait()
        outs[i // cuts][:, i % cuts * piece : (i % cuts + 1) * piece] = jnp.dot(
            x, buffers[i % depth], preferred_element_type=F32
        )
        if i + depth < total:
            fetch(i + depth).start()


def list_blocks(variant_ref, holder_ref, owner_ref, slot_ref, table_ref):
    rows = slot_ref.shape[0]
    slots = owner_ref.shape[0]
    variant = variant_ref[...]
    slot_row = jnp.zeros(variant.shape, jnp.int32)
    for v in range(holder_ref.shape[0]):
        slot_row = jnp.where(variant == v, holder_ref[v], slot_row)
    slot_row = (slot_row - lax.axis_index("tp") * slots).astype(F32)
    slot_ref[...] = jnp.transpose(jnp.broadcast_to(slot_row, (rows, rows))).astype(jnp.int32)
    for e in range(table_ref.shape[0]):
        table_ref[e] = -1
    for j in range(slots):

        def note(b, carry, j=j):
            e = (owner_ref[j, b] * slots + j) * CAP
            table_ref[e + jnp.where(table_ref[e] >= 0, 1, 0)] = b
            return carry

        lax.fori_loop(0, owner_ref.shape[1], note, 0)


def held_blocks(distance, count, slots, heads, scale_ref, cell_ref, table_ref):
    tiles = count * heads
    owner = owner_at(distance, count)
    listed = []
    for j in range(slots):
        for c in range(CAP):
            b = table_ref[(owner * slots + j) * CAP + c]
            found = jnp.maximum(b, 0)
            cell = cell_ref[j, found]
            scale = jnp.where(b >= 0, scale_ref[j, found], 0.0)
            listed.append((j, found, scale, lax.div(cell, tiles), lax.rem(cell, tiles)))
    return listed


def fold_chunk(distance, count, chunk_ref, slot, factor_ref, values_ref, scale_ref, cell_ref,
               table_ref, low_ref):
    heads, rows, side = chunk_ref.shape
    width = heads * side
    features = jnp.concatenate([chunk_ref[h] for h in range(heads)], axis=1)
    start = pl.multiple_of(owner_at(distance, count) * width, width)
    low_ref[...] += lax.dot_general(
        features, factor_ref[:, pl.ds(start, width)], NT, preferred_element_type=F32
    )
    added = []
    for j, b, scale, row_block, column in held_blocks(
        distance, count, values_ref.shape[0], heads, scale_ref, cell_ref, table_ref
    ):
        mine = jnp.where(slot == j, 1.0, 0.0)
        product = jnp.dot(chunk_ref[row_block], values_ref[j, b], preferred_element_type=F32)
        added.append((column, product * (mine * scale)))
    return added


def fold_kernel(distances, count, first, *refs):
    chunks, refs = refs[: len(distances)], refs[len(distances) :]
    slot_ref, factor_ref, values_ref, scale_ref, cell_ref, table_ref = refs[:6]
    low_ref, block_ref = refs[-2:]
    if first:
        low_ref[...] = jnp.zeros_like(low_ref)
        block_ref[...] = jnp.zeros_like(block_ref)
    else:
        low_ref[...] = refs[6][...]
        block_ref[...] = refs[7][...]
    slot = slot_ref[...]
    for distance, chunk in zip(distances, chunks):
        for column, product in fold_chunk(distance, count, chunk, slot, factor_ref, values_ref,
                                          scale_ref, cell_ref, table_ref, low_ref):
            block_ref[column] += product


def part_for(distance, count, low_ref, second_ref, dense_ref, block_ref, extra_ref, columns, out_ref):
    width = dense_ref.shape[1]
    side = block_ref.shape[2]
    heads = width // side
    owner = owner_at(distance, count)
    start = pl.multiple_of(owner * width, width)
    blocks = jnp.concatenate([block_ref[owner * heads + i] for i in range(heads)], axis=1)
    out_ref[...] = (
        jnp.dot(low_ref[...], second_ref[:, pl.ds(start, width)], preferred_element_type=F32)
        + dense_ref[...]
        + blocks
    )
    for e, column in enumerate(columns):

        @pl.when(lax.div(column, heads) == owner)
        def _(e=e, column=column):
            place = pl.ds(pl.multiple_of(lax.rem(column, heads) * side, side), side)
            out_ref[:, place] += extra_ref[e]


def finish_kernel(distances, count, *refs):
    front_ref, back_ref, slot_ref, factor_ref, values_ref, scale_ref, cell_ref, table_ref = refs[:8]
    second_ref, low_in, block_ref = refs[8:11]
    dense_refs, refs = refs[11 : 11 + len(distances)], refs[11 + len(distances) :]
    low_out, extra_out, front_out, back_out = refs[:4]
    outs, (chunk, low_sum, total) = refs[4:-3], refs[-3:]
    half, rows, side = front_ref.shape
    chunk[:half] = front_ref[...]
    chunk[half:] = back_ref[...]
    low_sum[...] = low_in[...]
    slot = slot_ref[...]
    added = fold_chunk(distances[0], count, chunk, slot, factor_ref, values_ref, scale_ref, cell_ref,
                       table_ref, low_sum)
    for e, (_, product) in enumerate(added):
        extra_out[e] = product
    columns = [column for column, _ in added]
    low_width = low_sum.shape[1]
    rank = low_width // values_ref.shape[0]
    held = lax.broadcasted_iota(jnp.int32, (rows, low_width), 1) // rank
    slots_wide = jnp.concatenate([slot] * -(-low_width // side), axis=1)[:, :low_width]
    low = jnp.where(slots_wide == held, low_sum[...], 0.0).astype(BF16)
    low_out[...] = low
    for n, (distance, dense_ref) in enumerate(zip(distances, dense_refs)):
        part_for(distance, count, low_out, second_ref, dense_ref, block_ref, extra_out, columns,
                 total.at[n])
        for i in range(2 * half):
            tile = total[n, :, i * side : (i + 1) * side]
            if n:
                outs[2 * n - 2 + i // half][i % half] = tile
            elif i < half:
                front_out[i] = tile.astype(BF16)
            else:
                back_out[i - half] = tile.astype(BF16)


def part_kernel(distances, count, slots, *refs):
    low_ref, second_ref, block_ref, extra_ref, scale_ref, cell_ref, table_ref = refs[:7]
    dense_refs, refs = refs[7 : 7 + len(distances)], refs[7 + len(distances) :]
    outs, total = refs[:-1], refs[-1]
    side = block_ref.shape[2]
    heads = dense_refs[0].shape[1] // side
    listed = held_blocks(count // 2, count, slots, heads, scale_ref, cell_ref, table_ref)
    columns = [entry[-1] for entry in listed]
    for n, (distance, dense_ref) in enumerate(zip(distances, dense_refs)):
        part_for(distance, count, low_ref, second_ref, dense_ref, block_ref, extra_ref, columns,
                 total.at[n])
        for i in range(heads):
            outs[2 * n + 2 * i // heads][i % (heads // 2)] = total[n, :, i * side : (i + 1) * side]


def sum_kernel(*refs):
    out_ref = refs[-1]
    half, _, side = refs[0].shape
    for i in range(2 * half):
        total = refs[i // half][i % half]
        for ref in refs[2 + i // half : -1 : 2]:
            total = total + ref[i % half].astype(F32)
        out_ref[:, i * side : (i + 1) * side] = total.astype(BF16)


def after(value, *others):
    return lax.optimization_barrier((value, *others))[0]


def body(
    queries, key_cache, value_cache, new_keys, new_values, lengths, request_variant, holder_slot,
    out_weight, factor_in, second_factor, block_values, block_scale, block_owner, block_cell,
):
    count = lax.axis_size("tp")
    half = count // 2
    ring = ring_order(count)
    rows, width = queries.shape
    side = key_cache.shape[3]
    cache = key_cache.shape[2]
    heads = width // side
    slots = block_values.shape[0]
    complete = out_weight.shape[1]
    low_width = slots * factor_in.shape[2]
    shape = jax.ShapeDtypeStruct

    attended = call(
        attend_kernel,
        "attend",
        shape((heads, rows, side), BF16),
        (queries, key_cache.reshape(-1, side), value_cache.reshape(-1, side), new_keys[0],
         new_values[0], lengths[None, :]),
        [ANY] * 6,
        VMEM,
        [pltpu.VMEM((rows, width), BF16), pltpu.VMEM((rows * cache, side), BF16),
         pltpu.VMEM((rows * cache, side), BF16), pltpu.VMEM((rows, side), BF16),
         pltpu.VMEM((rows, side), BF16), pltpu.VMEM((1, rows), jnp.int32),
         pltpu.SemaphoreType.DMA((4 + 2 * PIECES,))],
        limit=60,
    )

    wanted = [half]
    for distance in range(half - 1, 0, -1):
        wanted += [distance, count - distance]
    wanted += [0]
    piece = width // 2 if width >= 512 else width
    dense = {}

    def dense_for(distances, x, listing=False):
        extra_shapes = [shape((rows, rows), jnp.int32), shape((count * slots * CAP,), jnp.int32)]
        extra_ins = (request_variant[None, :], holder_slot, block_owner[:, :, 0])
        got = call(
            functools.partial(dense_kernel, distances, count, listing),
            "dense",
            [shape((rows, width), F32)] * len(distances) + extra_shapes * listing,
            (x, out_weight) + extra_ins * listing,
            [VMEM, ANY] + [VMEM, SMEM, SMEM] * listing,
            [VMEM] * len(distances) + [VMEM, SMEM] * listing,
            [pltpu.VMEM((4, width, piece), BF16), pltpu.SemaphoreType.DMA((4,))],
            limit=40,
            flops=2 * rows * width * width * len(distances),
            moved=2 * width * width * len(distances),
        )
        dense.update(zip(distances, got))
        return got[len(distances) :] if listing else got

    def come(value, distance):
        return lax.ppermute(
            value, "tp", [(ring[(i + distance) % count], ring[i]) for i in range(count)]
        )

    chunks = {0: attended}
    chunks[1], chunks[count - 1] = come(attended, 1), come(attended, -1)
    (token, *_) = dense_for(wanted[:3], attended)
    for step in range(2, half):
        right, left = after(chunks[step - 1], token), after(chunks[count - step + 1], token)
        chunks[step], chunks[count - step] = come(right, 1), come(left, -1)
        if step == 2:
            slot, table = dense_for(wanted[3:5], after(attended, token), True)
            token = slot
    right, left = chunks[half - 1], chunks[half + 1]

    factor_t = jnp.swapaxes(factor_in, 1, 2).reshape(low_width, -1)
    second = second_factor.reshape(low_width, complete)
    state = [shape((rows, low_width), F32), shape((complete // side, rows, side), F32)]
    early = [0]
    for distance in range(1, half - 1):
        early += [distance, count - distance]
    late = [half - 1, count - half + 1]
    tables = (slot, factor_t, block_values, block_scale, block_cell, table)
    table_specs = [VMEM, VMEM, VMEM, SMEM, SMEM, SMEM]
    low, blocks = call(
        functools.partial(fold_kernel, early, count, True),
        "fold_early",
        state,
        (*[chunks[d] for d in early], *tables),
        [VMEM] * len(early) + table_specs,
        [VMEM] * 2,
        flops=rows * low_width * complete,
        moved=4 * MIB,
    )
    right, left = after(right, low), after(left, low)
    front, back = come(right[: heads // 2], 1), come(left[heads // 2 :], -1)
    low, blocks = call(
        functools.partial(fold_kernel, late, count, False),
        "fold_late",
        state,
        (*[chunks[d] for d in late], *tables, low, blocks),
        [VMEM] * len(late) + table_specs + [VMEM] * 2,
        [VMEM] * 2,
        flops=rows * low_width * width * 4,
        moved=MIB,
    )
    extras = shape((slots * CAP, rows, side), F32)
    first = wanted[:3]
    part_half = shape((heads // 2, rows, side), F32)
    low, extra, front, back, *sums = call(
        functools.partial(finish_kernel, first, count),
        "finish",
        [shape((rows, low_width), BF16), extras]
        + [shape((heads // 2, rows, side), BF16)] * 2
        + [part_half] * (2 * len(first) - 2),
        (front, back, *tables, second, low, blocks, *[dense[d] for d in first]),
        [VMEM] * 2 + table_specs + [VMEM] * (3 + len(first)),
        [VMEM] * (2 + 2 * len(first)),
        [pltpu.VMEM((heads, rows, side), BF16), pltpu.VMEM((rows, low_width), F32),
         pltpu.VMEM((len(first), rows, width), F32)],
        flops=rows * low_width * width * 8,
        moved=2 * MIB,
    )
    parts = {d: sums[2 * n : 2 * n + 2] for n, d in enumerate(first[1:])}

    def parts_for(distances, low):
        got = call(
            functools.partial(part_kernel, distances, count, slots),
            "part",
            [part_half] * (2 * len(distances)),
            (low, second, blocks, extra, block_scale, block_cell, table,
             *[dense[distance] for distance in distances]),
            [VMEM] * 4 + [SMEM] * 3 + [VMEM] * len(distances),
            [VMEM] * (2 * len(distances)),
            [pltpu.VMEM((len(distances), rows, width), F32)],
            flops=rows * low_width * width * 2,
            moved=MIB,
        )
        parts.update((d, got[2 * n : 2 * n + 2]) for n, d in enumerate(distances))

    def joined(part, came):
        return (part if came is None else part + came.astype(F32)).astype(BF16)

    far, near = (front, back), (None, None)
    for distance in range(half, 0, -1):
        nearer = distance - 1
        if distance < half:
            far = lax.optimization_barrier(
                (joined(parts[count - distance][0], far[0]), joined(parts[distance][1], far[1]))
            )
        if distance == half - 1:
            dense_for(wanted[5:-1], after(attended, *far))
        if nearer and nearer < half - 1:
            parts_for([nearer, count - nearer], after(low, *far))
        if not nearer:
            dense_for([0], after(attended, *far))
            parts_for([0], after(low, *far))
        far = come(far[0], 1), come(far[1], -1)
        if nearer:
            near = lax.optimization_barrier(
                (joined(parts[count - nearer][1], near[0]), joined(parts[nearer][0], near[1]))
            )
            near = come(near[0], 1), come(near[1], -1)
    came = [far[0], near[0], near[1], far[1]] if half > 1 else [far[0], far[1]]
    return call(
        sum_kernel,
        "sum_up",
        shape((rows, width), BF16),
        (*parts[0], *came),
        [VMEM] * (2 + len(came)),
        VMEM,
        flops=1,
        moved=1,
    )


def solution(mesh):
    return jax.shard_map(
        body,
        mesh=mesh,
        in_specs=(
            P(("groups", "rep"), "tp"),
            P("tp", ("groups", "rep"), None, None),
            P("tp", ("groups", "rep"), None, None),
            P("tp", ("groups", "rep"), None),
            P("tp", ("groups", "rep"), None),
            P(("groups", "rep")),
            P(("groups", "rep")),
            P(),
            P("tp", None),
            P("tp", None, None),
            P("tp", None, None),
            P("tp", None, None, None),
            P("tp", None),
            P("tp", None, None),
            P("tp", None),
        ),
        out_specs=P(("groups", "rep"), "tp"),
        check_vma=False,
    )
```

```python
import functools
import math

import jax
import jax.numpy as jnp
from jax import lax
from jax.experimental import pallas as pl
from jax.experimental.pallas import tpu as pltpu
from jax.sharding import PartitionSpec as P

BF16 = jnp.bfloat16
F32 = jnp.float32
CAP = 2
ROW_BLOCK = 16
PIECES = 2
MIB = 1024 * 1024
NT = (((1,), (1,)), ((), ()))
VMEM = pl.BlockSpec(memory_space=pltpu.VMEM)
SMEM = pl.BlockSpec(memory_space=pltpu.SMEM)
ANY = pl.BlockSpec(memory_space=pl.ANY)


def ring_order(count):
    if count == 8:
        return [0, 2, 4, 6, 7, 5, 3, 1]
    return list(range(count))


def owner_at(distance, count):
    me = lax.axis_index("tp")
    if count != 8:
        return lax.rem(me + distance, count)
    spot = jnp.where((me & 1) == 0, me >> 1, count - 1 - (me >> 1))
    spot = lax.rem(spot + distance, count)
    return jnp.where(spot < count // 2, 2 * spot, 2 * (count - 1 - spot) + 1)


def call(kernel, name, outs, ins, specs, out_specs, scratch=(), limit=16, flops=0, moved=0):
    return pl.pallas_call(
        kernel,
        out_shape=outs,
        in_specs=specs,
        out_specs=out_specs,
        scratch_shapes=list(scratch),
        compiler_params=pltpu.CompilerParams(vmem_limit_bytes=limit * MIB),
        cost_estimate=pl.CostEstimate(flops=flops, bytes_accessed=moved, transcendentals=0),
        name=name,
    )(*ins)


def attend_kernel(
    query_hbm, key_hbm, value_hbm, new_key_hbm, new_value_hbm, length_hbm, out_ref,
    q_ref, key_ref, value_ref, new_key_ref, new_value_ref, length_ref, sems,
):
    heads, rows, side = out_ref.shape
    cache = key_ref.shape[0] // rows
    small = [
        pltpu.make_async_copy(source, target, sems.at[i])
        for i, (source, target) in enumerate(
            ((length_hbm, length_ref), (query_hbm, q_ref), (new_key_hbm, new_key_ref),
             (new_value_hbm, new_value_ref))
        )
    ]
    tall_piece = key_ref.shape[0] // PIECES
    pieces = []
    for i in range(PIECES):
        for n, (source, target) in enumerate(((key_hbm, key_ref), (value_hbm, value_ref))):
            part = pl.ds(i * tall_piece, tall_piece)
            pieces.append(
                pltpu.make_async_copy(source.at[part], target.at[part], sems.at[4 + 2 * i + n])
            )
    for copy in small + pieces:
        copy.start()
    for copy in small:
        copy.wait()
    tall, wide = heads * ROW_BLOCK, cache * ROW_BLOCK
    scale = math.log2(math.e) / math.sqrt(side)
    lengths = jnp.transpose(jnp.broadcast_to(length_ref[...].astype(F32), (rows, rows)))[:, :1]
    row_in = lax.broadcasted_iota(jnp.int32, (tall, wide), 0) % ROW_BLOCK
    place = (lax.broadcasted_iota(jnp.int32, (tall, wide), 1) - cache * row_in).astype(F32)
    place = jnp.where(place < 0, 1e9, place)
    for r in range(0, rows, ROW_BLOCK):
        if r % (rows // PIECES) == 0:
            for copy in pieces[2 * (r * PIECES // rows) :][:2]:
                copy.wait()
        here = slice(r, r + ROW_BLOCK)
        cached = slice(r * cache, (r + ROW_BLOCK) * cache)
        query = jnp.concatenate(
            [q_ref[here, h * side : (h + 1) * side] for h in range(heads)], axis=0
        )
        new_key = jnp.concatenate([new_key_ref[here].astype(F32)] * heads, axis=0)
        new_value = jnp.concatenate([new_value_ref[here].astype(F32)] * heads, axis=0)
        live = place < jnp.concatenate([lengths[here]] * heads, axis=0)
        scores = lax.dot_general(query, key_ref[cached], NT, preferred_element_type=F32)
        fresh = jnp.sum(query.astype(F32) * new_key, axis=1, keepdims=True)
        scores = jnp.where(live, scores, -jnp.inf)
        top = jnp.maximum(jnp.max(scores, axis=1, keepdims=True), fresh)
        raw = jnp.exp2((scores - top) * scale)
        fresh_raw = jnp.exp2((fresh - top) * scale)
        inverse = 1.0 / (jnp.sum(raw, axis=1, keepdims=True) + fresh_raw)
        attended = jnp.dot(raw.astype(BF16), value_ref[cached], preferred_element_type=F32)
        attended = ((attended + fresh_raw * new_value) * inverse).astype(BF16)
        for h in range(heads):
            out_ref[h, here, :] = attended[h * ROW_BLOCK : (h + 1) * ROW_BLOCK]


def dense_kernel(distances, count, listing, *refs):
    x_ref, weight_ref = refs[:2]
    outs = refs[-2 - 2 * listing - len(distances) : -2 - 2 * listing]
    buffers, sems = refs[-2:]
    heads, rows, side = x_ref.shape
    width = heads * side
    depth = buffers.shape[0]
    piece = buffers.shape[2]
    cuts = width // piece
    total = len(distances) * cuts

    def fetch(i):
        start = pl.multiple_of(owner_at(distances[i // cuts], count) * width, width) + i % cuts * piece
        return pltpu.make_async_copy(
            weight_ref.at[:, pl.ds(pl.multiple_of(start, piece), piece)],
            buffers.at[i % depth],
            sems.at[i % depth],
        )

    for i in range(min(depth, total)):
        fetch(i).start()
    if listing:
        list_blocks(refs[2], refs[3], refs[4], refs[-4], refs[-3])
    x = jnp.concatenate([x_ref[h] for h in range(heads)], axis=1)
    for i in range(total):
        fetch(i).wait()
        outs[i // cuts][:, i % cuts * piece : (i % cuts + 1) * piece] = jnp.dot(
            x, buffers[i % depth], preferred_element_type=F32
        )
        if i + depth < total:
            fetch(i + depth).start()


def list_blocks(variant_ref, holder_ref, owner_ref, slot_ref, table_ref):
    rows = slot_ref.shape[0]
    slots = owner_ref.shape[0]
    variant = variant_ref[...]
    slot_row = jnp.zeros(variant.shape, jnp.int32)
    for v in range(holder_ref.shape[0]):
        slot_row = jnp.where(variant == v, holder_ref[v], slot_row)
    slot_row = (slot_row - lax.axis_index("tp") * slots).astype(F32)
    slot_ref[...] = jnp.transpose(jnp.broadcast_to(slot_row, (rows, rows))).astype(jnp.int32)
    for e in range(table_ref.shape[0]):
        table_ref[e] = -1
    for j in range(slots):

        def note(b, carry, j=j):
            e = (owner_ref[j, b] * slots + j) * CAP
            table_ref[e + jnp.where(table_ref[e] >= 0, 1, 0)] = b
            return carry

        lax.fori_loop(0, owner_ref.shape[1], note, 0)


def held_blocks(distance, count, slots, heads, scale_ref, cell_ref, table_ref):
    tiles = count * heads
    owner = owner_at(distance, count)
    listed = []
    for j in range(slots):
        for c in range(CAP):
            b = table_ref[(owner * slots + j) * CAP + c]
            found = jnp.maximum(b, 0)
            cell = cell_ref[j, found]
            scale = jnp.where(b >= 0, scale_ref[j, found], 0.0)
            listed.append((j, found, scale, lax.div(cell, tiles), lax.rem(cell, tiles)))
    return listed


def fold_chunk(distance, count, chunk_ref, slot, factor_ref, values_ref, scale_ref, cell_ref,
               table_ref, low_ref):
    heads, rows, side = chunk_ref.shape
    width = heads * side
    features = jnp.concatenate([chunk_ref[h] for h in range(heads)], axis=1)
    start = pl.multiple_of(owner_at(distance, count) * width, width)
    low_ref[...] += lax.dot_general(
        features, factor_ref[:, pl.ds(start, width)], NT, preferred_element_type=F32
    )
    added = []
    for j, b, scale, row_block, column in held_blocks(
        distance, count, values_ref.shape[0], heads, scale_ref, cell_ref, table_ref
    ):
        mine = jnp.where(slot == j, 1.0, 0.0)
        product = jnp.dot(chunk_ref[row_block], values_ref[j, b], preferred_element_type=F32)
        added.append((column, product * (mine * scale)))
    return added


def fold_kernel(distances, count, first, *refs):
    chunks, refs = refs[: len(distances)], refs[len(distances) :]
    slot_ref, factor_ref, values_ref, scale_ref, cell_ref, table_ref = refs[:6]
    low_ref, block_ref = refs[-2:]
    if first:
        low_ref[...] = jnp.zeros_like(low_ref)
        block_ref[...] = jnp.zeros_like(block_ref)
    else:
        low_ref[...] = refs[6][...]
        block_ref[...] = refs[7][...]
    slot = slot_ref[...]
    for distance, chunk in zip(distances, chunks):
        for column, product in fold_chunk(distance, count, chunk, slot, factor_ref, values_ref,
                                          scale_ref, cell_ref, table_ref, low_ref):
            block_ref[column] += product


def part_for(distance, count, low_ref, second_ref, dense_ref, block_ref, extra_ref, columns, out_ref):
    width = dense_ref.shape[1]
    side = block_ref.shape[2]
    heads = width // side
    owner = owner_at(distance, count)
    start = pl.multiple_of(owner * width, width)
    blocks = jnp.concatenate([block_ref[owner * heads + i] for i in range(heads)], axis=1)
    out_ref[...] = (
        jnp.dot(low_ref[...], second_ref[:, pl.ds(start, width)], preferred_element_type=F32)
        + dense_ref[...]
        + blocks
    )
    for e, column in enumerate(columns):

        @pl.when(lax.div(column, heads) == owner)
        def _(e=e, column=column):
            place = pl.ds(pl.multiple_of(lax.rem(column, heads) * side, side), side)
            out_ref[:, place] += extra_ref[e]


def finish_kernel(distances, count, *refs):
    front_ref, back_ref, slot_ref, factor_ref, values_ref, scale_ref, cell_ref, table_ref = refs[:8]
    second_ref, low_in, block_ref = refs[8:11]
    dense_refs, refs = refs[11 : 11 + len(distances)], refs[11 + len(distances) :]
    low_out, extra_out, front_out, back_out = refs[:4]
    outs, (chunk, low_sum, total) = refs[4:-3], refs[-3:]
    half, rows, side = front_ref.shape
    chunk[:half] = front_ref[...]
    chunk[half:] = back_ref[...]
    low_sum[...] = low_in[...]
    slot = slot_ref[...]
    added = fold_chunk(distances[0], count, chunk, slot, factor_ref, values_ref, scale_ref, cell_ref,
                       table_ref, low_sum)
    for e, (_, product) in enumerate(added):
        extra_out[e] = product
    columns = [column for column, _ in added]
    low_width = low_sum.shape[1]
    rank = low_width // values_ref.shape[0]
    held = lax.broadcasted_iota(jnp.int32, (rows, low_width), 1) // rank
    slots_wide = jnp.concatenate([slot] * -(-low_width // side), axis=1)[:, :low_width]
    low = jnp.where(slots_wide == held, low_sum[...], 0.0).astype(BF16)
    low_out[...] = low
    for n, (distance, dense_ref) in enumerate(zip(distances, dense_refs)):
        part_for(distance, count, low_out, second_ref, dense_ref, block_ref, extra_out, columns,
                 total.at[n])
        for i in range(2 * half):
            tile = total[n, :, i * side : (i + 1) * side]
            if n:
                outs[2 * n - 2 + i // half][i % half] = tile
            elif i < half:
                front_out[i] = tile.astype(BF16)
            else:
                back_out[i - half] = tile.astype(BF16)


def part_kernel(distances, count, slots, *refs):
    low_ref, second_ref, block_ref, extra_ref, scale_ref, cell_ref, table_ref = refs[:7]
    dense_refs, refs = refs[7 : 7 + len(distances)], refs[7 + len(distances) :]
    outs, total = refs[:-1], refs[-1]
    side = block_ref.shape[2]
    heads = dense_refs[0].shape[1] // side
    listed = held_blocks(count // 2, count, slots, heads, scale_ref, cell_ref, table_ref)
    columns = [entry[-1] for entry in listed]
    for n, (distance, dense_ref) in enumerate(zip(distances, dense_refs)):
        part_for(distance, count, low_ref, second_ref, dense_ref, block_ref, extra_ref, columns,
                 total.at[n])
        for i in range(heads):
            outs[2 * n + 2 * i // heads][i % (heads // 2)] = total[n, :, i * side : (i + 1) * side]


def sum_kernel(*refs):
    out_ref = refs[-1]
    half, _, side = refs[0].shape
    for i in range(2 * half):
        total = refs[i // half][i % half]
        for ref in refs[2 + i // half : -1 : 2]:
            total = total + ref[i % half].astype(F32)
        out_ref[:, i * side : (i + 1) * side] = total.astype(BF16)


def after(value, *others):
    return lax.optimization_barrier((value, *others))[0]


def body(
    queries, key_cache, value_cache, new_keys, new_values, lengths, request_variant, holder_slot,
    out_weight, factor_in, second_factor, block_values, block_scale, block_owner, block_cell,
):
    count = lax.axis_size("tp")
    half = count // 2
    ring = ring_order(count)
    rows, width = queries.shape
    side = key_cache.shape[3]
    cache = key_cache.shape[2]
    heads = width // side
    slots = block_values.shape[0]
    complete = out_weight.shape[1]
    low_width = slots * factor_in.shape[2]
    shape = jax.ShapeDtypeStruct

    attended = call(
        attend_kernel,
        "attend",
        shape((heads, rows, side), BF16),
        (queries, key_cache.reshape(-1, side), value_cache.reshape(-1, side), new_keys[0],
         new_values[0], lengths[None, :]),
        [ANY] * 6,
        VMEM,
        [pltpu.VMEM((rows, width), BF16), pltpu.VMEM((rows * cache, side), BF16),
         pltpu.VMEM((rows * cache, side), BF16), pltpu.VMEM((rows, side), BF16),
         pltpu.VMEM((rows, side), BF16), pltpu.VMEM((1, rows), jnp.int32),
         pltpu.SemaphoreType.DMA((4 + 2 * PIECES,))],
        limit=60,
    )

    wanted = [half]
    for distance in range(half - 1, 0, -1):
        wanted += [distance, count - distance]
    wanted += [0]
    piece = width // 2 if width >= 512 else width
    dense = {}

    def dense_for(distances, x, listing=False):
        extra_shapes = [shape((rows, rows), jnp.int32), shape((count * slots * CAP,), jnp.int32)]
        extra_ins = (request_variant[None, :], holder_slot, block_owner[:, :, 0])
        got = call(
            functools.partial(dense_kernel, distances, count, listing),
            "dense",
            [shape((rows, width), F32)] * len(distances) + extra_shapes * listing,
            (x, out_weight) + extra_ins * listing,
            [VMEM, ANY] + [VMEM, SMEM, SMEM] * listing,
            [VMEM] * len(distances) + [VMEM, SMEM] * listing,
            [pltpu.VMEM((4, width, piece), BF16), pltpu.SemaphoreType.DMA((4,))],
            limit=40,
            flops=2 * rows * width * width * len(distances),
            moved=2 * width * width * len(distances),
        )
        dense.update(zip(distances, got))
        return got[len(distances) :] if listing else got

    def come(value, distance):
        return lax.ppermute(
            value, "tp", [(ring[(i + distance) % count], ring[i]) for i in range(count)]
        )

    chunks = {0: attended}
    chunks[1], chunks[count - 1] = come(attended, 1), come(attended, -1)
    (token, *_) = dense_for(wanted[:3], attended)
    for step in range(2, half):
        right, left = after(chunks[step - 1], token), after(chunks[count - step + 1], token)
        chunks[step], chunks[count - step] = come(right, 1), come(left, -1)
        if step == 2:
            slot, table = dense_for(wanted[3:5], after(attended, token), True)
            token = slot
    (token, *_) = dense_for(wanted[5:-1], after(attended, chunks[half - 2], chunks[half + 2]))
    right, left = chunks[half - 1], chunks[half + 1]

    factor_t = jnp.swapaxes(factor_in, 1, 2).reshape(low_width, -1)
    second = second_factor.reshape(low_width, complete)
    state = [shape((rows, low_width), F32), shape((complete // side, rows, side), F32)]
    early = [0]
    for distance in range(1, half - 1):
        early += [distance, count - distance]
    late = [half - 1, count - half + 1]
    tables = (slot, factor_t, block_values, block_scale, block_cell, table)
    table_specs = [VMEM, VMEM, VMEM, SMEM, SMEM, SMEM]
    low, blocks = call(
        functools.partial(fold_kernel, early, count, True),
        "fold_early",
        state,
        (*[chunks[d] for d in early], *tables),
        [VMEM] * len(early) + table_specs,
        [VMEM] * 2,
        flops=rows * low_width * complete,
        moved=4 * MIB,
    )
    right, left = after(right, low, token), after(left, low, token)
    front, back = come(right[: heads // 2], 1), come(left[heads // 2 :], -1)
    low, blocks = call(
        functools.partial(fold_kernel, late, count, False),
        "fold_late",
        state,
        (*[chunks[d] for d in late], *tables, low, blocks),
        [VMEM] * len(late) + table_specs + [VMEM] * 2,
        [VMEM] * 2,
        flops=rows * low_width * width * 4,
        moved=MIB,
    )
    extras = shape((slots * CAP, rows, side), F32)
    first = wanted[:3]
    part_half = shape((heads // 2, rows, side), F32)
    low, extra, front, back, *sums = call(
        functools.partial(finish_kernel, first, count),
        "finish",
        [shape((rows, low_width), BF16), extras]
        + [shape((heads // 2, rows, side), BF16)] * 2
        + [part_half] * (2 * len(first) - 2),
        (front, back, *tables, second, low, blocks, *[dense[d] for d in first]),
        [VMEM] * 2 + table_specs + [VMEM] * (3 + len(first)),
        [VMEM] * (2 + 2 * len(first)),
        [pltpu.VMEM((heads, rows, side), BF16), pltpu.VMEM((rows, low_width), F32),
         pltpu.VMEM((len(first), rows, width), F32)],
        flops=rows * low_width * width * 8,
        moved=2 * MIB,
    )
    parts = {d: sums[2 * n : 2 * n + 2] for n, d in enumerate(first[1:])}

    def parts_for(distances, low):
        got = call(
            functools.partial(part_kernel, distances, count, slots),
            "part",
            [part_half] * (2 * len(distances)),
            (low, second, blocks, extra, block_scale, block_cell, table,
             *[dense[distance] for distance in distances]),
            [VMEM] * 4 + [SMEM] * 3 + [VMEM] * len(distances),
            [VMEM] * (2 * len(distances)),
            [pltpu.VMEM((len(distances), rows, width), F32)],
            flops=rows * low_width * width * 2,
            moved=MIB,
        )
        parts.update((d, got[2 * n : 2 * n + 2]) for n, d in enumerate(distances))

    def joined(part, came):
        return (part if came is None else part + came.astype(F32)).astype(BF16)

    far, near = (front, back), (None, None)
    for distance in range(half, 0, -1):
        nearer = distance - 1
        if distance < half:
            far = lax.optimization_barrier(
                (joined(parts[count - distance][0], far[0]), joined(parts[distance][1], far[1]))
            )
        if nearer and nearer < half - 1:
            parts_for([nearer, count - nearer], after(low, *far))
        if not nearer:
            dense_for([0], after(attended, *far))
            parts_for([0], after(low, *far))
        far = come(far[0], 1), come(far[1], -1)
        if nearer:
            near = lax.optimization_barrier(
                (joined(parts[count - nearer][1], near[0]), joined(parts[nearer][0], near[1]))
            )
            near = come(near[0], 1), come(near[1], -1)
    came = [far[0], near[0], near[1], far[1]] if half > 1 else [far[0], far[1]]
    return call(
        sum_kernel,
        "sum_up",
        shape((rows, width), BF16),
        (*parts[0], *came),
        [VMEM] * (2 + len(came)),
        VMEM,
        flops=1,
        moved=1,
    )


def solution(mesh):
    return jax.shard_map(
        body,
        mesh=mesh,
        in_specs=(
            P(("groups", "rep"), "tp"),
            P("tp", ("groups", "rep"), None, None),
            P("tp", ("groups", "rep"), None, None),
            P("tp", ("groups", "rep"), None),
            P("tp", ("groups", "rep"), None),
            P(("groups", "rep")),
            P(("groups", "rep")),
            P(),
            P("tp", None),
            P("tp", None, None),
            P("tp", None, None),
            P("tp", None, None, None),
            P("tp", None),
            P("tp", None, None),
            P("tp", None),
        ),
        out_specs=P(("groups", "rep"), "tp"),
        check_vma=False,
    )
```

```python
import functools
import math

import jax
import jax.numpy as jnp
from jax import lax
from jax.experimental import pallas as pl
from jax.experimental.pallas import tpu as pltpu
from jax.sharding import PartitionSpec as P

BF16 = jnp.bfloat16
F32 = jnp.float32
CAP = 2
ROW_BLOCK = 16
PIECES = 2
MIB = 1024 * 1024
NT = (((1,), (1,)), ((), ()))
VMEM = pl.BlockSpec(memory_space=pltpu.VMEM)
SMEM = pl.BlockSpec(memory_space=pltpu.SMEM)
ANY = pl.BlockSpec(memory_space=pl.ANY)


def ring_order(count):
    if count == 8:
        return [0, 2, 4, 6, 7, 5, 3, 1]
    return list(range(count))


def owner_at(distance, count):
    me = lax.axis_index("tp")
    if count != 8:
        return lax.rem(me + distance, count)
    spot = jnp.where((me & 1) == 0, me >> 1, count - 1 - (me >> 1))
    spot = lax.rem(spot + distance, count)
    return jnp.where(spot < count // 2, 2 * spot, 2 * (count - 1 - spot) + 1)


def call(kernel, name, outs, ins, specs, out_specs, scratch=(), limit=16, flops=0, moved=0):
    return pl.pallas_call(
        kernel,
        out_shape=outs,
        in_specs=specs,
        out_specs=out_specs,
        scratch_shapes=list(scratch),
        compiler_params=pltpu.CompilerParams(vmem_limit_bytes=limit * MIB),
        cost_estimate=pl.CostEstimate(flops=flops, bytes_accessed=moved, transcendentals=0),
        name=name,
    )(*ins)


def attend_kernel(
    query_hbm, key_hbm, value_hbm, new_key_hbm, new_value_hbm, length_hbm, out_ref,
    q_ref, key_ref, value_ref, new_key_ref, new_value_ref, length_ref, sems,
):
    heads, rows, side = out_ref.shape
    cache = key_ref.shape[0] // rows
    small = [
        pltpu.make_async_copy(source, target, sems.at[i])
        for i, (source, target) in enumerate(
            ((length_hbm, length_ref), (query_hbm, q_ref), (new_key_hbm, new_key_ref),
             (new_value_hbm, new_value_ref))
        )
    ]
    tall_piece = key_ref.shape[0] // PIECES
    pieces = []
    for i in range(PIECES):
        for n, (source, target) in enumerate(((key_hbm, key_ref), (value_hbm, value_ref))):
            part = pl.ds(i * tall_piece, tall_piece)
            pieces.append(
                pltpu.make_async_copy(source.at[part], target.at[part], sems.at[4 + 2 * i + n])
            )
    for copy in small + pieces:
        copy.start()
    for copy in small:
        copy.wait()
    tall, wide = heads * ROW_BLOCK, cache * ROW_BLOCK
    scale = math.log2(math.e) / math.sqrt(side)
    lengths = jnp.transpose(jnp.broadcast_to(length_ref[...].astype(F32), (rows, rows)))[:, :1]
    row_in = lax.broadcasted_iota(jnp.int32, (tall, wide), 0) % ROW_BLOCK
    place = (lax.broadcasted_iota(jnp.int32, (tall, wide), 1) - cache * row_in).astype(F32)
    place = jnp.where(place < 0, 1e9, place)
    for r in range(0, rows, ROW_BLOCK):
        if r % (rows // PIECES) == 0:
            for copy in pieces[2 * (r * PIECES // rows) :][:2]:
                copy.wait()
        here = slice(r, r + ROW_BLOCK)
        cached = slice(r * cache, (r + ROW_BLOCK) * cache)
        query = jnp.concatenate(
            [q_ref[here, h * side : (h + 1) * side] for h in range(heads)], axis=0
        )
        new_key = jnp.concatenate([new_key_ref[here].astype(F32)] * heads, axis=0)
        new_value = jnp.concatenate([new_value_ref[here].astype(F32)] * heads, axis=0)
        live = place < jnp.concatenate([lengths[here]] * heads, axis=0)
        scores = lax.dot_general(query, key_ref[cached], NT, preferred_element_type=F32)
        fresh = jnp.sum(query.astype(F32) * new_key, axis=1, keepdims=True)
        scores = jnp.where(live, scores, -jnp.inf)
        top = jnp.maximum(jnp.max(scores, axis=1, keepdims=True), fresh)
        raw = jnp.exp2((scores - top) * scale)
        fresh_raw = jnp.exp2((fresh - top) * scale)
        inverse = 1.0 / (jnp.sum(raw, axis=1, keepdims=True) + fresh_raw)
        attended = jnp.dot(raw.astype(BF16), value_ref[cached], preferred_element_type=F32)
        attended = ((attended + fresh_raw * new_value) * inverse).astype(BF16)
        for h in range(heads):
            out_ref[h, here, :] = attended[h * ROW_BLOCK : (h + 1) * ROW_BLOCK]


def dense_kernel(distances, count, listing, *refs):
    x_ref, weight_ref = refs[:2]
    outs = refs[-2 - 2 * listing - len(distances) : -2 - 2 * listing]
    buffers, sems = refs[-2:]
    heads, rows, side = x_ref.shape
    width = heads * side
    depth = buffers.shape[0]
    piece = buffers.shape[2]
    cuts = width // piece
    total = len(distances) * cuts

    def fetch(i):
        start = pl.multiple_of(owner_at(distances[i // cuts], count) * width, width) + i % cuts * piece
        return pltpu.make_async_copy(
            weight_ref.at[:, pl.ds(pl.multiple_of(start, piece), piece)],
            buffers.at[i % depth],
            sems.at[i % depth],
        )

    for i in range(min(depth, total)):
        fetch(i).start()
    if listing:
        list_blocks(refs[2], refs[3], refs[4], refs[-4], refs[-3])
    x = jnp.concatenate([x_ref[h] for h in range(heads)], axis=1)
    for i in range(total):
        fetch(i).wait()
        outs[i // cuts][:, i % cuts * piece : (i % cuts + 1) * piece] = jnp.dot(
            x, buffers[i % depth], preferred_element_type=F32
        )
        if i + depth < total:
            fetch(i + depth).start()


def list_blocks(variant_ref, holder_ref, owner_ref, slot_ref, table_ref):
    rows = slot_ref.shape[0]
    slots = owner_ref.shape[0]
    variant = variant_ref[...]
    slot_row = jnp.zeros(variant.shape, jnp.int32)
    for v in range(holder_ref.shape[0]):
        slot_row = jnp.where(variant == v, holder_ref[v], slot_row)
    slot_row = (slot_row - lax.axis_index("tp") * slots).astype(F32)
    slot_ref[...] = jnp.transpose(jnp.broadcast_to(slot_row, (rows, rows))).astype(jnp.int32)
    for e in range(table_ref.shape[0]):
        table_ref[e] = -1
    for j in range(slots):

        def note(b, carry, j=j):
            e = (owner_ref[j, b] * slots + j) * CAP
            table_ref[e + jnp.where(table_ref[e] >= 0, 1, 0)] = b
            return carry

        lax.fori_loop(0, owner_ref.shape[1], note, 0)


def held_blocks(distance, count, slots, heads, scale_ref, cell_ref, table_ref):
    tiles = count * heads
    owner = owner_at(distance, count)
    listed = []
    for j in range(slots):
        for c in range(CAP):
            b = table_ref[(owner * slots + j) * CAP + c]
            found = jnp.maximum(b, 0)
            cell = cell_ref[j, found]
            scale = jnp.where(b >= 0, scale_ref[j, found], 0.0)
            listed.append((j, found, scale, lax.div(cell, tiles), lax.rem(cell, tiles)))
    return listed


def fold_chunk(distance, count, chunk_ref, slot, factor_ref, values_ref, scale_ref, cell_ref,
               table_ref, low_ref):
    heads, rows, side = chunk_ref.shape
    width = heads * side
    features = jnp.concatenate([chunk_ref[h] for h in range(heads)], axis=1)
    start = pl.multiple_of(owner_at(distance, count) * width, width)
    low_ref[...] += lax.dot_general(
        features, factor_ref[:, pl.ds(start, width)], NT, preferred_element_type=F32
    )
    added = []
    for j, b, scale, row_block, column in held_blocks(
        distance, count, values_ref.shape[0], heads, scale_ref, cell_ref, table_ref
    ):
        mine = jnp.where(slot == j, 1.0, 0.0)
        product = jnp.dot(chunk_ref[row_block], values_ref[j, b], preferred_element_type=F32)
        added.append((column, product * (mine * scale)))
    return added


def fold_kernel(distances, count, first, *refs):
    chunks, refs = refs[: len(distances)], refs[len(distances) :]
    slot_ref, factor_ref, values_ref, scale_ref, cell_ref, table_ref = refs[:6]
    low_ref, block_ref = refs[-2:]
    if first:
        low_ref[...] = jnp.zeros_like(low_ref)
        block_ref[...] = jnp.zeros_like(block_ref)
    else:
        low_ref[...] = refs[6][...]
        block_ref[...] = refs[7][...]
    slot = slot_ref[...]
    for distance, chunk in zip(distances, chunks):
        for column, product in fold_chunk(distance, count, chunk, slot, factor_ref, values_ref,
                                          scale_ref, cell_ref, table_ref, low_ref):
            block_ref[column] += product


def part_for(distance, count, low_ref, second_ref, dense_ref, block_ref, extra_ref, columns, out_ref):
    width = dense_ref.shape[1]
    side = block_ref.shape[2]
    heads = width // side
    owner = owner_at(distance, count)
    start = pl.multiple_of(owner * width, width)
    blocks = jnp.concatenate([block_ref[owner * heads + i] for i in range(heads)], axis=1)
    out_ref[...] = (
        jnp.dot(low_ref[...], second_ref[:, pl.ds(start, width)], preferred_element_type=F32)
        + dense_ref[...]
        + blocks
    )
    for e, column in enumerate(columns):

        @pl.when(lax.div(column, heads) == owner)
        def _(e=e, column=column):
            place = pl.ds(pl.multiple_of(lax.rem(column, heads) * side, side), side)
            out_ref[:, place] += extra_ref[e]


def finish_kernel(distances, count, *refs):
    front_ref, back_ref, slot_ref, factor_ref, values_ref, scale_ref, cell_ref, table_ref = refs[:8]
    second_ref, low_in, block_ref = refs[8:11]
    dense_refs, refs = refs[11 : 11 + len(distances)], refs[11 + len(distances) :]
    low_out, extra_out, front_out, back_out = refs[:4]
    outs, (chunk, low_sum, total) = refs[4:-3], refs[-3:]
    half, rows, side = front_ref.shape
    chunk[:half] = front_ref[...]
    chunk[half:] = back_ref[...]
    low_sum[...] = low_in[...]
    slot = slot_ref[...]
    added = fold_chunk(distances[0], count, chunk, slot, factor_ref, values_ref, scale_ref, cell_ref,
                       table_ref, low_sum)
    for e, (_, product) in enumerate(added):
        extra_out[e] = product
    columns = [column for column, _ in added]
    low_width = low_sum.shape[1]
    rank = low_width // values_ref.shape[0]
    held = lax.broadcasted_iota(jnp.int32, (rows, low_width), 1) // rank
    slots_wide = jnp.concatenate([slot] * -(-low_width // side), axis=1)[:, :low_width]
    low = jnp.where(slots_wide == held, low_sum[...], 0.0).astype(BF16)
    low_out[...] = low
    for n, (distance, dense_ref) in enumerate(zip(distances, dense_refs)):
        part_for(distance, count, low_out, second_ref, dense_ref, block_ref, extra_out, columns,
                 total.at[n])
        for i in range(2 * half):
            tile = total[n, :, i * side : (i + 1) * side]
            if n:
                outs[2 * n - 2 + i // half][i % half] = tile
            elif i < half:
                front_out[i] = tile.astype(BF16)
            else:
                back_out[i - half] = tile.astype(BF16)


def part_kernel(distances, count, slots, *refs):
    low_ref, second_ref, block_ref, extra_ref, scale_ref, cell_ref, table_ref = refs[:7]
    dense_refs, refs = refs[7 : 7 + len(distances)], refs[7 + len(distances) :]
    outs, total = refs[:-1], refs[-1]
    side = block_ref.shape[2]
    heads = dense_refs[0].shape[1] // side
    listed = held_blocks(count // 2, count, slots, heads, scale_ref, cell_ref, table_ref)
    columns = [entry[-1] for entry in listed]
    for n, (distance, dense_ref) in enumerate(zip(distances, dense_refs)):
        part_for(distance, count, low_ref, second_ref, dense_ref, block_ref, extra_ref, columns,
                 total.at[n])
        for i in range(heads):
            outs[2 * n + 2 * i // heads][i % (heads // 2)] = total[n, :, i * side : (i + 1) * side]


def sum_kernel(*refs):
    out_ref = refs[-1]
    half, _, side = refs[0].shape
    for i in range(2 * half):
        total = refs[i // half][i % half]
        for ref in refs[2 + i // half : -1 : 2]:
            total = total + ref[i % half].astype(F32)
        out_ref[:, i * side : (i + 1) * side] = total.astype(BF16)


def after(value, *others):
    return lax.optimization_barrier((value, *others))[0]


def body(
    queries, key_cache, value_cache, new_keys, new_values, lengths, request_variant, holder_slot,
    out_weight, factor_in, second_factor, block_values, block_scale, block_owner, block_cell,
):
    count = lax.axis_size("tp")
    half = count // 2
    ring = ring_order(count)
    rows, width = queries.shape
    side = key_cache.shape[3]
    cache = key_cache.shape[2]
    heads = width // side
    slots = block_values.shape[0]
    complete = out_weight.shape[1]
    low_width = slots * factor_in.shape[2]
    shape = jax.ShapeDtypeStruct

    attended = call(
        attend_kernel,
        "attend",
        shape((heads, rows, side), BF16),
        (queries, key_cache.reshape(-1, side), value_cache.reshape(-1, side), new_keys[0],
         new_values[0], lengths[None, :]),
        [ANY] * 6,
        VMEM,
        [pltpu.VMEM((rows, width), BF16), pltpu.VMEM((rows * cache, side), BF16),
         pltpu.VMEM((rows * cache, side), BF16), pltpu.VMEM((rows, side), BF16),
         pltpu.VMEM((rows, side), BF16), pltpu.VMEM((1, rows), jnp.int32),
         pltpu.SemaphoreType.DMA((4 + 2 * PIECES,))],
        limit=60,
    )

    wanted = [half]
    for distance in range(half - 1, 0, -1):
        wanted += [distance, count - distance]
    wanted += [0]
    piece = width // 2 if width >= 512 else width
    dense = {}

    def dense_for(distances, x, listing=False):
        extra_shapes = [shape((rows, rows), jnp.int32), shape((count * slots * CAP,), jnp.int32)]
        extra_ins = (request_variant[None, :], holder_slot, block_owner[:, :, 0])
        got = call(
            functools.partial(dense_kernel, distances, count, listing),
            "dense",
            [shape((rows, width), F32)] * len(distances) + extra_shapes * listing,
            (x, out_weight) + extra_ins * listing,
            [VMEM, ANY] + [VMEM, SMEM, SMEM] * listing,
            [VMEM] * len(distances) + [VMEM, SMEM] * listing,
            [pltpu.VMEM((4, width, piece), BF16), pltpu.SemaphoreType.DMA((4,))],
            limit=40,
            flops=2 * rows * width * width * len(distances),
            moved=2 * width * width * len(distances),
        )
        dense.update(zip(distances, got))
        return got[len(distances) :] if listing else got

    def come(value, distance):
        return lax.ppermute(
            value, "tp", [(ring[(i + distance) % count], ring[i]) for i in range(count)]
        )

    chunks = {0: attended}
    chunks[1], chunks[count - 1] = come(attended, 1), come(attended, -1)
    (token, *_) = dense_for(wanted[:3], attended)
    for step in range(2, half):
        right, left = after(chunks[step - 1], token), after(chunks[count - step + 1], token)
        chunks[step], chunks[count - step] = come(right, 1), come(left, -1)
        if step == 2:
            slot, table = dense_for(wanted[3:5], after(attended, token), True)
            token = slot
    (token, *_) = dense_for(wanted[5:-1], after(attended, chunks[half - 2], chunks[half + 2]))
    right, left = chunks[half - 1], chunks[half + 1]

    factor_t = jnp.swapaxes(factor_in, 1, 2).reshape(low_width, -1)
    second = second_factor.reshape(low_width, complete)
    state = [shape((rows, low_width), F32), shape((complete // side, rows, side), F32)]
    early = [0]
    for distance in range(1, half - 1):
        early += [distance, count - distance]
    late = [half - 1, count - half + 1]
    tables = (slot, factor_t, block_values, block_scale, block_cell, table)
    table_specs = [VMEM, VMEM, VMEM, SMEM, SMEM, SMEM]
    low, blocks = call(
        functools.partial(fold_kernel, early, count, True),
        "fold_early",
        state,
        (*[chunks[d] for d in early], *tables),
        [VMEM] * len(early) + table_specs,
        [VMEM] * 2,
        flops=rows * low_width * complete,
        moved=4 * MIB,
    )
    right, left = after(right, low, token), after(left, low, token)
    front, back = come(right[: heads // 2], 1), come(left[heads // 2 :], -1)
    low, blocks = call(
        functools.partial(fold_kernel, late, count, False),
        "fold_late",
        state,
        (*[chunks[d] for d in late], *tables, low, blocks),
        [VMEM] * len(late) + table_specs + [VMEM] * 2,
        [VMEM] * 2,
        flops=rows * low_width * width * 4,
        moved=MIB,
    )
    extras = shape((slots * CAP, rows, side), F32)
    first = wanted[:1]
    part_half = shape((heads // 2, rows, side), F32)
    low, extra, front, back, *sums = call(
        functools.partial(finish_kernel, first, count),
        "finish",
        [shape((rows, low_width), BF16), extras]
        + [shape((heads // 2, rows, side), BF16)] * 2
        + [part_half] * (2 * len(first) - 2),
        (front, back, *tables, second, low, blocks, *[dense[d] for d in first]),
        [VMEM] * 2 + table_specs + [VMEM] * (3 + len(first)),
        [VMEM] * (2 + 2 * len(first)),
        [pltpu.VMEM((heads, rows, side), BF16), pltpu.VMEM((rows, low_width), F32),
         pltpu.VMEM((len(first), rows, width), F32)],
        flops=rows * low_width * width * 8,
        moved=2 * MIB,
    )
    parts = {d: sums[2 * n : 2 * n + 2] for n, d in enumerate(first[1:])}

    def parts_for(distances, low):
        got = call(
            functools.partial(part_kernel, distances, count, slots),
            "part",
            [part_half] * (2 * len(distances)),
            (low, second, blocks, extra, block_scale, block_cell, table,
             *[dense[distance] for distance in distances]),
            [VMEM] * 4 + [SMEM] * 3 + [VMEM] * len(distances),
            [VMEM] * (2 * len(distances)),
            [pltpu.VMEM((len(distances), rows, width), F32)],
            flops=rows * low_width * width * 2,
            moved=MIB,
        )
        parts.update((d, got[2 * n : 2 * n + 2]) for n, d in enumerate(distances))

    def joined(part, came):
        return (part if came is None else part + came.astype(F32)).astype(BF16)

    far, near = (front, back), (None, None)
    for distance in range(half, 0, -1):
        nearer = distance - 1
        if distance < half:
            far = lax.optimization_barrier(
                (joined(parts[count - distance][0], far[0]), joined(parts[distance][1], far[1]))
            )
        if nearer:
            parts_for([nearer, count - nearer], after(low, *far))
        if not nearer:
            dense_for([0], after(attended, *far))
            parts_for([0], after(low, *far))
        far = come(far[0], 1), come(far[1], -1)
        if nearer:
            near = lax.optimization_barrier(
                (joined(parts[count - nearer][1], near[0]), joined(parts[nearer][0], near[1]))
            )
            near = come(near[0], 1), come(near[1], -1)
    came = [far[0], near[0], near[1], far[1]] if half > 1 else [far[0], far[1]]
    return call(
        sum_kernel,
        "sum_up",
        shape((rows, width), BF16),
        (*parts[0], *came),
        [VMEM] * (2 + len(came)),
        VMEM,
        flops=1,
        moved=1,
    )


def solution(mesh):
    return jax.shard_map(
        body,
        mesh=mesh,
        in_specs=(
            P(("groups", "rep"), "tp"),
            P("tp", ("groups", "rep"), None, None),
            P("tp", ("groups", "rep"), None, None),
            P("tp", ("groups", "rep"), None),
            P("tp", ("groups", "rep"), None),
            P(("groups", "rep")),
            P(("groups", "rep")),
            P(),
            P("tp", None),
            P("tp", None, None),
            P("tp", None, None),
            P("tp", None, None, None),
            P("tp", None),
            P("tp", None, None),
            P("tp", None),
        ),
        out_specs=P(("groups", "rep"), "tp"),
        check_vma=False,
    )
```

```python
import functools
import math

import jax
import jax.numpy as jnp
from jax import lax
from jax.experimental import pallas as pl
from jax.experimental.pallas import tpu as pltpu
from jax.sharding import PartitionSpec as P

BF16 = jnp.bfloat16
F32 = jnp.float32
CAP = 2
ROW_BLOCK = 16
PIECES = 2
MIB = 1024 * 1024
NT = (((1,), (1,)), ((), ()))
VMEM = pl.BlockSpec(memory_space=pltpu.VMEM)
SMEM = pl.BlockSpec(memory_space=pltpu.SMEM)
ANY = pl.BlockSpec(memory_space=pl.ANY)


def ring_order(count):
    if count == 8:
        return [0, 2, 4, 6, 7, 5, 3, 1]
    return list(range(count))


def owner_at(distance, count):
    me = lax.axis_index("tp")
    if count != 8:
        return lax.rem(me + distance, count)
    spot = jnp.where((me & 1) == 0, me >> 1, count - 1 - (me >> 1))
    spot = lax.rem(spot + distance, count)
    return jnp.where(spot < count // 2, 2 * spot, 2 * (count - 1 - spot) + 1)


def call(kernel, name, outs, ins, specs, out_specs, scratch=(), limit=16, flops=0, moved=0):
    return pl.pallas_call(
        kernel,
        out_shape=outs,
        in_specs=specs,
        out_specs=out_specs,
        scratch_shapes=list(scratch),
        compiler_params=pltpu.CompilerParams(vmem_limit_bytes=limit * MIB),
        cost_estimate=pl.CostEstimate(flops=flops, bytes_accessed=moved, transcendentals=0),
        name=name,
    )(*ins)


def attend_kernel(
    query_hbm, key_hbm, value_hbm, new_key_hbm, new_value_hbm, length_hbm, out_ref,
    q_ref, key_ref, value_ref, new_key_ref, new_value_ref, length_ref, sems,
):
    heads, rows, side = out_ref.shape
    cache = key_ref.shape[0] // rows
    small = [
        pltpu.make_async_copy(source, target, sems.at[i])
        for i, (source, target) in enumerate(
            ((length_hbm, length_ref), (query_hbm, q_ref), (new_key_hbm, new_key_ref),
             (new_value_hbm, new_value_ref))
        )
    ]
    tall_piece = key_ref.shape[0] // PIECES
    pieces = []
    for i in range(PIECES):
        for n, (source, target) in enumerate(((key_hbm, key_ref), (value_hbm, value_ref))):
            part = pl.ds(i * tall_piece, tall_piece)
            pieces.append(
                pltpu.make_async_copy(source.at[part], target.at[part], sems.at[4 + 2 * i + n])
            )
    for copy in small + pieces:
        copy.start()
    for copy in small:
        copy.wait()
    tall, wide = heads * ROW_BLOCK, cache * ROW_BLOCK
    scale = math.log2(math.e) / math.sqrt(side)
    lengths = jnp.transpose(jnp.broadcast_to(length_ref[...].astype(F32), (rows, rows)))[:, :1]
    row_in = lax.broadcasted_iota(jnp.int32, (tall, wide), 0) % ROW_BLOCK
    place = (lax.broadcasted_iota(jnp.int32, (tall, wide), 1) - cache * row_in).astype(F32)
    place = jnp.where(place < 0, 1e9, place)
    for r in range(0, rows, ROW_BLOCK):
        if r % (rows // PIECES) == 0:
            for copy in pieces[2 * (r * PIECES // rows) :][:2]:
                copy.wait()
        here = slice(r, r + ROW_BLOCK)
        cached = slice(r * cache, (r + ROW_BLOCK) * cache)
        query = jnp.concatenate(
            [q_ref[here, h * side : (h + 1) * side] for h in range(heads)], axis=0
        )
        new_key = jnp.concatenate([new_key_ref[here].astype(F32)] * heads, axis=0)
        new_value = jnp.concatenate([new_value_ref[here].astype(F32)] * heads, axis=0)
        live = place < jnp.concatenate([lengths[here]] * heads, axis=0)
        scores = lax.dot_general(query, key_ref[cached], NT, preferred_element_type=F32)
        fresh = jnp.sum(query.astype(F32) * new_key, axis=1, keepdims=True)
        scores = jnp.where(live, scores, -jnp.inf)
        top = jnp.maximum(jnp.max(scores, axis=1, keepdims=True), fresh)
        raw = jnp.exp2((scores - top) * scale)
        fresh_raw = jnp.exp2((fresh - top) * scale)
        inverse = 1.0 / (jnp.sum(raw, axis=1, keepdims=True) + fresh_raw)
        attended = jnp.dot(raw.astype(BF16), value_ref[cached], preferred_element_type=F32)
        attended = ((attended + fresh_raw * new_value) * inverse).astype(BF16)
        for h in range(heads):
            out_ref[h, here, :] = attended[h * ROW_BLOCK : (h + 1) * ROW_BLOCK]


def dense_kernel(distances, count, listing, *refs):
    x_ref, weight_ref = refs[:2]
    outs = refs[-2 - 2 * listing - len(distances) : -2 - 2 * listing]
    buffers, sems = refs[-2:]
    heads, rows, side = x_ref.shape
    width = heads * side
    depth = buffers.shape[0]
    piece = buffers.shape[2]
    cuts = width // piece
    total = len(distances) * cuts

    def fetch(i):
        start = pl.multiple_of(owner_at(distances[i // cuts], count) * width, width) + i % cuts * piece
        return pltpu.make_async_copy(
            weight_ref.at[:, pl.ds(pl.multiple_of(start, piece), piece)],
            buffers.at[i % depth],
            sems.at[i % depth],
        )

    for i in range(min(depth, total)):
        fetch(i).start()
    if listing:
        list_blocks(refs[2], refs[3], refs[4], refs[-4], refs[-3])
    x = jnp.concatenate([x_ref[h] for h in range(heads)], axis=1)
    for i in range(total):
        fetch(i).wait()
        outs[i // cuts][:, i % cuts * piece : (i % cuts + 1) * piece] = jnp.dot(
            x, buffers[i % depth], preferred_element_type=F32
        )
        if i + depth < total:
            fetch(i + depth).start()


def list_blocks(variant_ref, holder_ref, owner_ref, slot_ref, table_ref):
    rows = slot_ref.shape[0]
    slots = owner_ref.shape[0]
    variant = variant_ref[...]
    slot_row = jnp.zeros(variant.shape, jnp.int32)
    for v in range(holder_ref.shape[0]):
        slot_row = jnp.where(variant == v, holder_ref[v], slot_row)
    slot_row = (slot_row - lax.axis_index("tp") * slots).astype(F32)
    slot_ref[...] = jnp.transpose(jnp.broadcast_to(slot_row, (rows, rows))).astype(jnp.int32)
    for e in range(table_ref.shape[0]):
        table_ref[e] = -1
    for j in range(slots):

        def note(b, carry, j=j):
            e = (owner_ref[j, b] * slots + j) * CAP
            table_ref[e + jnp.where(table_ref[e] >= 0, 1, 0)] = b
            return carry

        lax.fori_loop(0, owner_ref.shape[1], note, 0)


def held_blocks(distance, count, slots, heads, scale_ref, cell_ref, table_ref):
    tiles = count * heads
    owner = owner_at(distance, count)
    listed = []
    for j in range(slots):
        for c in range(CAP):
            b = table_ref[(owner * slots + j) * CAP + c]
            found = jnp.maximum(b, 0)
            cell = cell_ref[j, found]
            scale = jnp.where(b >= 0, scale_ref[j, found], 0.0)
            listed.append((j, found, scale, lax.div(cell, tiles), lax.rem(cell, tiles)))
    return listed


def fold_chunk(distance, count, chunk_ref, slot, factor_ref, values_ref, scale_ref, cell_ref,
               table_ref, low_ref):
    heads, rows, side = chunk_ref.shape
    width = heads * side
    features = jnp.concatenate([chunk_ref[h] for h in range(heads)], axis=1)
    start = pl.multiple_of(owner_at(distance, count) * width, width)
    low_ref[...] += lax.dot_general(
        features, factor_ref[:, pl.ds(start, width)], NT, preferred_element_type=F32
    )
    added = []
    for j, b, scale, row_block, column in held_blocks(
        distance, count, values_ref.shape[0], heads, scale_ref, cell_ref, table_ref
    ):
        mine = jnp.where(slot == j, 1.0, 0.0)
        product = jnp.dot(chunk_ref[row_block], values_ref[j, b], preferred_element_type=F32)
        added.append((column, product * (mine * scale)))
    return added


def fold_kernel(distances, count, first, *refs):
    chunks, refs = refs[: len(distances)], refs[len(distances) :]
    slot_ref, factor_ref, values_ref, scale_ref, cell_ref, table_ref = refs[:6]
    low_ref, block_ref = refs[-2:]
    if first:
        low_ref[...] = jnp.zeros_like(low_ref)
        block_ref[...] = jnp.zeros_like(block_ref)
    else:
        low_ref[...] = refs[6][...]
        block_ref[...] = refs[7][...]
    slot = slot_ref[...]
    for distance, chunk in zip(distances, chunks):
        for column, product in fold_chunk(distance, count, chunk, slot, factor_ref, values_ref,
                                          scale_ref, cell_ref, table_ref, low_ref):
            block_ref[column] += product


def part_for(distance, count, low_ref, second_ref, dense_ref, block_ref, extra_ref, columns, out_ref):
    width = dense_ref.shape[1]
    side = block_ref.shape[2]
    heads = width // side
    owner = owner_at(distance, count)
    start = pl.multiple_of(owner * width, width)
    blocks = jnp.concatenate([block_ref[owner * heads + i] for i in range(heads)], axis=1)
    out_ref[...] = (
        jnp.dot(low_ref[...], second_ref[:, pl.ds(start, width)], preferred_element_type=F32)
        + dense_ref[...]
        + blocks
    )
    for e, column in enumerate(columns):

        @pl.when(lax.div(column, heads) == owner)
        def _(e=e, column=column):
            place = pl.ds(pl.multiple_of(lax.rem(column, heads) * side, side), side)
            out_ref[:, place] += extra_ref[e]


def finish_kernel(distances, count, *refs):
    front_ref, back_ref, slot_ref, factor_ref, values_ref, scale_ref, cell_ref, table_ref = refs[:8]
    second_ref, low_in, block_ref = refs[8:11]
    dense_refs, refs = refs[11 : 11 + len(distances)], refs[11 + len(distances) :]
    low_out, extra_out, front_out, back_out = refs[:4]
    outs, (chunk, low_sum, total) = refs[4:-3], refs[-3:]
    half, rows, side = front_ref.shape
    chunk[:half] = front_ref[...]
    chunk[half:] = back_ref[...]
    low_sum[...] = low_in[...]
    slot = slot_ref[...]
    added = fold_chunk(distances[0], count, chunk, slot, factor_ref, values_ref, scale_ref, cell_ref,
                       table_ref, low_sum)
    for e, (_, product) in enumerate(added):
        extra_out[e] = product
    columns = [column for column, _ in added]
    low_width = low_sum.shape[1]
    rank = low_width // values_ref.shape[0]
    held = lax.broadcasted_iota(jnp.int32, (rows, low_width), 1) // rank
    slots_wide = jnp.concatenate([slot] * -(-low_width // side), axis=1)[:, :low_width]
    low = jnp.where(slots_wide == held, low_sum[...], 0.0).astype(BF16)
    low_out[...] = low
    for n, (distance, dense_ref) in enumerate(zip(distances, dense_refs)):
        part_for(distance, count, low_out, second_ref, dense_ref, block_ref, extra_out, columns,
                 total.at[n])
        for i in range(2 * half):
            tile = total[n, :, i * side : (i + 1) * side]
            if n:
                outs[2 * n - 2 + i // half][i % half] = tile
            elif i < half:
                front_out[i] = tile.astype(BF16)
            else:
                back_out[i - half] = tile.astype(BF16)


def part_kernel(distances, count, slots, *refs):
    low_ref, second_ref, block_ref, extra_ref, scale_ref, cell_ref, table_ref = refs[:7]
    dense_refs, refs = refs[7 : 7 + len(distances)], refs[7 + len(distances) :]
    outs, total = refs[:-1], refs[-1]
    side = block_ref.shape[2]
    heads = dense_refs[0].shape[1] // side
    listed = held_blocks(count // 2, count, slots, heads, scale_ref, cell_ref, table_ref)
    columns = [entry[-1] for entry in listed]
    for n, (distance, dense_ref) in enumerate(zip(distances, dense_refs)):
        part_for(distance, count, low_ref, second_ref, dense_ref, block_ref, extra_ref, columns,
                 total.at[n])
        for i in range(heads):
            outs[2 * n + 2 * i // heads][i % (heads // 2)] = total[n, :, i * side : (i + 1) * side]


def sum_kernel(*refs):
    out_ref = refs[-1]
    half, _, side = refs[0].shape
    for i in range(2 * half):
        total = refs[i // half][i % half]
        for ref in refs[2 + i // half : -1 : 2]:
            total = total + ref[i % half].astype(F32)
        out_ref[:, i * side : (i + 1) * side] = total.astype(BF16)


def after(value, *others):
    return lax.optimization_barrier((value, *others))[0]


def body(
    queries, key_cache, value_cache, new_keys, new_values, lengths, request_variant, holder_slot,
    out_weight, factor_in, second_factor, block_values, block_scale, block_owner, block_cell,
):
    count = lax.axis_size("tp")
    half = count // 2
    ring = ring_order(count)
    rows, width = queries.shape
    side = key_cache.shape[3]
    cache = key_cache.shape[2]
    heads = width // side
    slots = block_values.shape[0]
    complete = out_weight.shape[1]
    low_width = slots * factor_in.shape[2]
    shape = jax.ShapeDtypeStruct

    attended = call(
        attend_kernel,
        "attend",
        shape((heads, rows, side), BF16),
        (queries, key_cache.reshape(-1, side), value_cache.reshape(-1, side), new_keys[0],
         new_values[0], lengths[None, :]),
        [ANY] * 6,
        VMEM,
        [pltpu.VMEM((rows, width), BF16), pltpu.VMEM((rows * cache, side), BF16),
         pltpu.VMEM((rows * cache, side), BF16), pltpu.VMEM((rows, side), BF16),
         pltpu.VMEM((rows, side), BF16), pltpu.VMEM((1, rows), jnp.int32),
         pltpu.SemaphoreType.DMA((4 + 2 * PIECES,))],
        limit=60,
    )

    wanted = [half]
    for distance in range(half - 1, 0, -1):
        wanted += [distance, count - distance]
    wanted += [0]
    piece = width // 2 if width >= 512 else width
    dense = {}

    def dense_for(distances, x, listing=False):
        extra_shapes = [shape((rows, rows), jnp.int32), shape((count * slots * CAP,), jnp.int32)]
        extra_ins = (request_variant[None, :], holder_slot, block_owner[:, :, 0])
        got = call(
            functools.partial(dense_kernel, distances, count, listing),
            "dense",
            [shape((rows, width), F32)] * len(distances) + extra_shapes * listing,
            (x, out_weight) + extra_ins * listing,
            [VMEM, ANY] + [VMEM, SMEM, SMEM] * listing,
            [VMEM] * len(distances) + [VMEM, SMEM] * listing,
            [pltpu.VMEM((4, width, piece), BF16), pltpu.SemaphoreType.DMA((4,))],
            limit=40,
            flops=2 * rows * width * width * len(distances),
            moved=2 * width * width * len(distances),
        )
        dense.update(zip(distances, got))
        return got[len(distances) :] if listing else got

    def come(value, distance):
        return lax.ppermute(
            value, "tp", [(ring[(i + distance) % count], ring[i]) for i in range(count)]
        )

    chunks = {0: attended}
    chunks[1], chunks[count - 1] = come(attended, 1), come(attended, -1)
    (token, *_) = dense_for(wanted[:3], attended)
    for step in range(2, half):
        right, left = after(chunks[step - 1], token), after(chunks[count - step + 1], token)
        chunks[step], chunks[count - step] = come(right, 1), come(left, -1)
        if step == half - 1:
            front, back = come(right[: heads // 2], 2), come(left[heads // 2 :], -2)
        if step == 2:
            slot, table = dense_for(wanted[3:5], after(attended, token), True)
            token = slot
    (token, *_) = dense_for(wanted[5:-1], after(attended, chunks[half - 2], chunks[half + 2]))

    factor_t = jnp.swapaxes(factor_in, 1, 2).reshape(low_width, -1)
    second = second_factor.reshape(low_width, complete)
    state = [shape((rows, low_width), F32), shape((complete // side, rows, side), F32)]
    early = [0]
    for distance in range(1, half - 1):
        early += [distance, count - distance]
    late = [half - 1, count - half + 1]
    tables = (slot, factor_t, block_values, block_scale, block_cell, table)
    table_specs = [VMEM, VMEM, VMEM, SMEM, SMEM, SMEM]
    low, blocks = call(
        functools.partial(fold_kernel, early, count, True),
        "fold_early",
        state,
        (*[chunks[d] for d in early], *tables),
        [VMEM] * len(early) + table_specs,
        [VMEM] * 2,
        flops=rows * low_width * complete,
        moved=4 * MIB,
    )
    low, blocks = call(
        functools.partial(fold_kernel, late, count, False),
        "fold_late",
        state,
        (*[chunks[d] for d in late], *tables, low, blocks),
        [VMEM] * len(late) + table_specs + [VMEM] * 2,
        [VMEM] * 2,
        flops=rows * low_width * width * 4,
        moved=MIB,
    )
    low = after(low, token)
    extras = shape((slots * CAP, rows, side), F32)
    first = wanted[:1]
    part_half = shape((heads // 2, rows, side), F32)
    low, extra, front, back, *sums = call(
        functools.partial(finish_kernel, first, count),
        "finish",
        [shape((rows, low_width), BF16), extras]
        + [shape((heads // 2, rows, side), BF16)] * 2
        + [part_half] * (2 * len(first) - 2),
        (front, back, *tables, second, low, blocks, *[dense[d] for d in first]),
        [VMEM] * 2 + table_specs + [VMEM] * (3 + len(first)),
        [VMEM] * (2 + 2 * len(first)),
        [pltpu.VMEM((heads, rows, side), BF16), pltpu.VMEM((rows, low_width), F32),
         pltpu.VMEM((len(first), rows, width), F32)],
        flops=rows * low_width * width * 8,
        moved=2 * MIB,
    )
    parts = {d: sums[2 * n : 2 * n + 2] for n, d in enumerate(first[1:])}

    def parts_for(distances, low):
        got = call(
            functools.partial(part_kernel, distances, count, slots),
            "part",
            [part_half] * (2 * len(distances)),
            (low, second, blocks, extra, block_scale, block_cell, table,
             *[dense[distance] for distance in distances]),
            [VMEM] * 4 + [SMEM] * 3 + [VMEM] * len(distances),
            [VMEM] * (2 * len(distances)),
            [pltpu.VMEM((len(distances), rows, width), F32)],
            flops=rows * low_width * width * 2,
            moved=MIB,
        )
        parts.update((d, got[2 * n : 2 * n + 2]) for n, d in enumerate(distances))

    def joined(part, came):
        return (part if came is None else part + came.astype(F32)).astype(BF16)

    far, near = (front, back), (None, None)
    for distance in range(half, 0, -1):
        nearer = distance - 1
        if distance < half:
            far = lax.optimization_barrier(
                (joined(parts[count - distance][0], far[0]), joined(parts[distance][1], far[1]))
            )
        if nearer:
            parts_for([nearer, count - nearer], after(low, *far))
        if not nearer:
            dense_for([0], after(attended, *far))
            parts_for([0], after(low, *far))
        far = come(far[0], 1), come(far[1], -1)
        if nearer:
            near = lax.optimization_barrier(
                (joined(parts[count - nearer][1], near[0]), joined(parts[nearer][0], near[1]))
            )
            near = come(near[0], 1), come(near[1], -1)
    came = [far[0], near[0], near[1], far[1]] if half > 1 else [far[0], far[1]]
    return call(
        sum_kernel,
        "sum_up",
        shape((rows, width), BF16),
        (*parts[0], *came),
        [VMEM] * (2 + len(came)),
        VMEM,
        flops=1,
        moved=1,
    )


def solution(mesh):
    return jax.shard_map(
        body,
        mesh=mesh,
        in_specs=(
            P(("groups", "rep"), "tp"),
            P("tp", ("groups", "rep"), None, None),
            P("tp", ("groups", "rep"), None, None),
            P("tp", ("groups", "rep"), None),
            P("tp", ("groups", "rep"), None),
            P(("groups", "rep")),
            P(("groups", "rep")),
            P(),
            P("tp", None),
            P("tp", None, None),
            P("tp", None, None),
            P("tp", None, None, None),
            P("tp", None),
            P("tp", None, None),
            P("tp", None),
        ),
        out_specs=P(("groups", "rep"), "tp"),
        check_vma=False,
    )
```

```python
import functools
import math

import jax
import jax.numpy as jnp
from jax import lax
from jax.experimental import pallas as pl
from jax.experimental.pallas import tpu as pltpu
from jax.sharding import PartitionSpec as P

BF16 = jnp.bfloat16
F32 = jnp.float32
CAP = 2
ROW_BLOCK = 16
PIECES = 2
MIB = 1024 * 1024
NT = (((1,), (1,)), ((), ()))
VMEM = pl.BlockSpec(memory_space=pltpu.VMEM)
SMEM = pl.BlockSpec(memory_space=pltpu.SMEM)
ANY = pl.BlockSpec(memory_space=pl.ANY)


def ring_order(count):
    if count == 8:
        return [0, 2, 4, 6, 7, 5, 3, 1]
    return list(range(count))


def owner_at(distance, count):
    me = lax.axis_index("tp")
    if count != 8:
        return lax.rem(me + distance, count)
    spot = jnp.where((me & 1) == 0, me >> 1, count - 1 - (me >> 1))
    spot = lax.rem(spot + distance, count)
    return jnp.where(spot < count // 2, 2 * spot, 2 * (count - 1 - spot) + 1)


def call(kernel, name, outs, ins, specs, out_specs, scratch=(), limit=16, flops=0, moved=0):
    return pl.pallas_call(
        kernel,
        out_shape=outs,
        in_specs=specs,
        out_specs=out_specs,
        scratch_shapes=list(scratch),
        compiler_params=pltpu.CompilerParams(vmem_limit_bytes=limit * MIB),
        cost_estimate=pl.CostEstimate(flops=flops, bytes_accessed=moved, transcendentals=0),
        name=name,
    )(*ins)


def attend_kernel(
    query_hbm, key_hbm, value_hbm, new_key_hbm, new_value_hbm, length_hbm, out_ref,
    q_ref, key_ref, value_ref, new_key_ref, new_value_ref, length_ref, sems,
):
    heads, rows, side = out_ref.shape
    cache = key_ref.shape[0] // rows
    small = [
        pltpu.make_async_copy(source, target, sems.at[i])
        for i, (source, target) in enumerate(
            ((length_hbm, length_ref), (query_hbm, q_ref), (new_key_hbm, new_key_ref),
             (new_value_hbm, new_value_ref))
        )
    ]
    tall_piece = key_ref.shape[0] // PIECES
    pieces = []
    for i in range(PIECES):
        for n, (source, target) in enumerate(((key_hbm, key_ref), (value_hbm, value_ref))):
            part = pl.ds(i * tall_piece, tall_piece)
            pieces.append(
                pltpu.make_async_copy(source.at[part], target.at[part], sems.at[4 + 2 * i + n])
            )
    for copy in small + pieces:
        copy.start()
    for copy in small:
        copy.wait()
    tall, wide = heads * ROW_BLOCK, cache * ROW_BLOCK
    scale = math.log2(math.e) / math.sqrt(side)
    lengths = jnp.transpose(jnp.broadcast_to(length_ref[...].astype(F32), (rows, rows)))[:, :1]
    row_in = lax.broadcasted_iota(jnp.int32, (tall, wide), 0) % ROW_BLOCK
    place = (lax.broadcasted_iota(jnp.int32, (tall, wide), 1) - cache * row_in).astype(F32)
    place = jnp.where(place < 0, 1e9, place)
    for r in range(0, rows, ROW_BLOCK):
        if r % (rows // PIECES) == 0:
            for copy in pieces[2 * (r * PIECES // rows) :][:2]:
                copy.wait()
        here = slice(r, r + ROW_BLOCK)
        cached = slice(r * cache, (r + ROW_BLOCK) * cache)
        query = jnp.concatenate(
            [q_ref[here, h * side : (h + 1) * side] for h in range(heads)], axis=0
        )
        new_key = jnp.concatenate([new_key_ref[here].astype(F32)] * heads, axis=0)
        new_value = jnp.concatenate([new_value_ref[here].astype(F32)] * heads, axis=0)
        live = place < jnp.concatenate([lengths[here]] * heads, axis=0)
        scores = lax.dot_general(query, key_ref[cached], NT, preferred_element_type=F32)
        fresh = jnp.sum(query.astype(F32) * new_key, axis=1, keepdims=True)
        scores = jnp.where(live, scores, -jnp.inf)
        top = jnp.maximum(jnp.max(scores, axis=1, keepdims=True), fresh)
        raw = jnp.exp2((scores - top) * scale)
        fresh_raw = jnp.exp2((fresh - top) * scale)
        inverse = 1.0 / (jnp.sum(raw, axis=1, keepdims=True) + fresh_raw)
        attended = jnp.dot(raw.astype(BF16), value_ref[cached], preferred_element_type=F32)
        attended = ((attended + fresh_raw * new_value) * inverse).astype(BF16)
        for h in range(heads):
            out_ref[h, here, :] = attended[h * ROW_BLOCK : (h + 1) * ROW_BLOCK]


def dense_kernel(distances, count, listing, *refs):
    x_ref, weight_ref = refs[:2]
    outs = refs[-2 - 2 * listing - len(distances) : -2 - 2 * listing]
    buffers, sems = refs[-2:]
    heads, rows, side = x_ref.shape
    width = heads * side
    depth = buffers.shape[0]
    piece = buffers.shape[2]
    cuts = width // piece
    total = len(distances) * cuts

    def fetch(i):
        start = pl.multiple_of(owner_at(distances[i // cuts], count) * width, width) + i % cuts * piece
        return pltpu.make_async_copy(
            weight_ref.at[:, pl.ds(pl.multiple_of(start, piece), piece)],
            buffers.at[i % depth],
            sems.at[i % depth],
        )

    for i in range(min(depth, total)):
        fetch(i).start()
    if listing:
        list_blocks(refs[2], refs[3], refs[4], refs[-4], refs[-3])
    x = jnp.concatenate([x_ref[h] for h in range(heads)], axis=1)
    for i in range(total):
        fetch(i).wait()
        outs[i // cuts][:, i % cuts * piece : (i % cuts + 1) * piece] = jnp.dot(
            x, buffers[i % depth], preferred_element_type=F32
        )
        if i + depth < total:
            fetch(i + depth).start()


def list_blocks(variant_ref, holder_ref, owner_ref, slot_ref, table_ref):
    rows = slot_ref.shape[0]
    slots = owner_ref.shape[0]
    variant = variant_ref[...]
    slot_row = jnp.zeros(variant.shape, jnp.int32)
    for v in range(holder_ref.shape[0]):
        slot_row = jnp.where(variant == v, holder_ref[v], slot_row)
    slot_row = (slot_row - lax.axis_index("tp") * slots).astype(F32)
    slot_ref[...] = jnp.transpose(jnp.broadcast_to(slot_row, (rows, rows))).astype(jnp.int32)
    for e in range(table_ref.shape[0]):
        table_ref[e] = -1
    for j in range(slots):

        def note(b, carry, j=j):
            e = (owner_ref[j, b] * slots + j) * CAP
            table_ref[e + jnp.where(table_ref[e] >= 0, 1, 0)] = b
            return carry

        lax.fori_loop(0, owner_ref.shape[1], note, 0)


def held_blocks(distance, count, slots, heads, scale_ref, cell_ref, table_ref):
    tiles = count * heads
    owner = owner_at(distance, count)
    listed = []
    for j in range(slots):
        for c in range(CAP):
            b = table_ref[(owner * slots + j) * CAP + c]
            found = jnp.maximum(b, 0)
            cell = cell_ref[j, found]
            scale = jnp.where(b >= 0, scale_ref[j, found], 0.0)
            listed.append((j, found, scale, lax.div(cell, tiles), lax.rem(cell, tiles)))
    return listed


def fold_chunk(distance, count, chunk_ref, slot, factor_ref, values_ref, scale_ref, cell_ref,
               table_ref, low_ref):
    heads, rows, side = chunk_ref.shape
    width = heads * side
    features = jnp.concatenate([chunk_ref[h] for h in range(heads)], axis=1)
    start = pl.multiple_of(owner_at(distance, count) * width, width)
    low_ref[...] += lax.dot_general(
        features, factor_ref[:, pl.ds(start, width)], NT, preferred_element_type=F32
    )
    added = []
    for j, b, scale, row_block, column in held_blocks(
        distance, count, values_ref.shape[0], heads, scale_ref, cell_ref, table_ref
    ):
        mine = jnp.where(slot == j, 1.0, 0.0)
        product = jnp.dot(chunk_ref[row_block], values_ref[j, b], preferred_element_type=F32)
        added.append((column, product * (mine * scale)))
    return added


def fold_kernel(distances, count, first, *refs):
    chunks, refs = refs[: len(distances)], refs[len(distances) :]
    slot_ref, factor_ref, values_ref, scale_ref, cell_ref, table_ref = refs[:6]
    low_ref, block_ref = refs[-2:]
    if first:
        low_ref[...] = jnp.zeros_like(low_ref)
        block_ref[...] = jnp.zeros_like(block_ref)
    else:
        low_ref[...] = refs[6][...]
        block_ref[...] = refs[7][...]
    slot = slot_ref[...]
    for distance, chunk in zip(distances, chunks):
        for column, product in fold_chunk(distance, count, chunk, slot, factor_ref, values_ref,
                                          scale_ref, cell_ref, table_ref, low_ref):
            block_ref[column] += product


def part_for(distance, count, low_ref, second_ref, dense_ref, block_ref, extra_ref, columns, halves):
    width = dense_ref.shape[1]
    side = block_ref.shape[2]
    heads = width // side
    half = heads // 2
    owner = owner_at(distance, count)
    start = pl.multiple_of(owner * width, width)
    delta = jnp.dot(low_ref[...], second_ref[:, pl.ds(start, width)], preferred_element_type=F32)
    for i in range(heads):
        tile = slice(i * side, (i + 1) * side)
        halves[i // half][i % half] = (
            delta[:, tile] + dense_ref[:, tile] + block_ref[owner * heads + i]
        )
    for e, column in enumerate(columns):
        here = lax.div(column, heads) == owner
        place = lax.rem(column, heads)

        @pl.when(here & (place < half))
        def _(e=e, place=place):
            halves[0][place] += extra_ref[e]

        @pl.when(here & (place >= half))
        def _(e=e, place=place):
            halves[1][place - half] += extra_ref[e]


def finish_kernel(distances, count, *refs):
    front_ref, back_ref, slot_ref, factor_ref, values_ref, scale_ref, cell_ref, table_ref = refs[:8]
    second_ref, low_in, block_ref = refs[8:11]
    dense_refs, refs = refs[11 : 11 + len(distances)], refs[11 + len(distances) :]
    low_out, extra_out, front_out, back_out = refs[:4]
    chunk, low_sum, total = refs[-3:]
    half, rows, side = front_ref.shape
    chunk[:half] = front_ref[...]
    chunk[half:] = back_ref[...]
    low_sum[...] = low_in[...]
    slot = slot_ref[...]
    added = fold_chunk(distances[0], count, chunk, slot, factor_ref, values_ref, scale_ref, cell_ref,
                       table_ref, low_sum)
    for e, (_, product) in enumerate(added):
        extra_out[e] = product
    columns = [column for column, _ in added]
    low_width = low_sum.shape[1]
    rank = low_width // values_ref.shape[0]
    held = lax.broadcasted_iota(jnp.int32, (rows, low_width), 1) // rank
    slots_wide = jnp.concatenate([slot] * -(-low_width // side), axis=1)[:, :low_width]
    low = jnp.where(slots_wide == held, low_sum[...], 0.0).astype(BF16)
    low_out[...] = low
    part_for(distances[0], count, low_out, second_ref, dense_refs[0], block_ref, extra_out, columns,
             (total.at[0], total.at[1]))
    front_out[...] = total[0].astype(BF16)
    back_out[...] = total[1].astype(BF16)


def part_kernel(distances, count, slots, *refs):
    low_ref, second_ref, block_ref, extra_ref, scale_ref, cell_ref, table_ref = refs[:7]
    dense_refs, refs = refs[7 : 7 + len(distances)], refs[7 + len(distances) :]
    heads = dense_refs[0].shape[1] // block_ref.shape[2]
    listed = held_blocks(count // 2, count, slots, heads, scale_ref, cell_ref, table_ref)
    columns = [entry[-1] for entry in listed]
    for n, (distance, dense_ref) in enumerate(zip(distances, dense_refs)):
        part_for(distance, count, low_ref, second_ref, dense_ref, block_ref, extra_ref, columns,
                 refs[2 * n : 2 * n + 2])


def sum_kernel(*refs):
    out_ref = refs[-1]
    half, _, side = refs[0].shape
    for i in range(2 * half):
        total = refs[i // half][i % half]
        for ref in refs[2 + i // half : -1 : 2]:
            total = total + ref[i % half].astype(F32)
        out_ref[:, i * side : (i + 1) * side] = total.astype(BF16)


def after(value, *others):
    return lax.optimization_barrier((value, *others))[0]


def body(
    queries, key_cache, value_cache, new_keys, new_values, lengths, request_variant, holder_slot,
    out_weight, factor_in, second_factor, block_values, block_scale, block_owner, block_cell,
):
    count = lax.axis_size("tp")
    half = count // 2
    ring = ring_order(count)
    rows, width = queries.shape
    side = key_cache.shape[3]
    cache = key_cache.shape[2]
    heads = width // side
    slots = block_values.shape[0]
    complete = out_weight.shape[1]
    low_width = slots * factor_in.shape[2]
    shape = jax.ShapeDtypeStruct

    attended = call(
        attend_kernel,
        "attend",
        shape((heads, rows, side), BF16),
        (queries, key_cache.reshape(-1, side), value_cache.reshape(-1, side), new_keys[0],
         new_values[0], lengths[None, :]),
        [ANY] * 6,
        VMEM,
        [pltpu.VMEM((rows, width), BF16), pltpu.VMEM((rows * cache, side), BF16),
         pltpu.VMEM((rows * cache, side), BF16), pltpu.VMEM((rows, side), BF16),
         pltpu.VMEM((rows, side), BF16), pltpu.VMEM((1, rows), jnp.int32),
         pltpu.SemaphoreType.DMA((4 + 2 * PIECES,))],
        limit=60,
    )

    wanted = [half]
    for distance in range(half - 1, 0, -1):
        wanted += [distance, count - distance]
    wanted += [0]
    piece = width // 2 if width >= 512 else width
    dense = {}

    def dense_for(distances, x, listing=False):
        extra_shapes = [shape((rows, rows), jnp.int32), shape((count * slots * CAP,), jnp.int32)]
        extra_ins = (request_variant[None, :], holder_slot, block_owner[:, :, 0])
        got = call(
            functools.partial(dense_kernel, distances, count, listing),
            "dense",
            [shape((rows, width), F32)] * len(distances) + extra_shapes * listing,
            (x, out_weight) + extra_ins * listing,
            [VMEM, ANY] + [VMEM, SMEM, SMEM] * listing,
            [VMEM] * len(distances) + [VMEM, SMEM] * listing,
            [pltpu.VMEM((4, width, piece), BF16), pltpu.SemaphoreType.DMA((4,))],
            limit=40,
            flops=2 * rows * width * width * len(distances),
            moved=2 * width * width * len(distances),
        )
        dense.update(zip(distances, got))
        return got[len(distances) :] if listing else got

    def come(value, distance):
        return lax.ppermute(
            value, "tp", [(ring[(i + distance) % count], ring[i]) for i in range(count)]
        )

    chunks = {0: attended}
    chunks[1], chunks[count - 1] = come(attended, 1), come(attended, -1)
    (token, *_) = dense_for(wanted[:3], attended)
    for step in range(2, half):
        right, left = after(chunks[step - 1], token), after(chunks[count - step + 1], token)
        chunks[step], chunks[count - step] = come(right, 1), come(left, -1)
        if step == half - 1:
            front, back = come(right[: heads // 2], 2), come(left[heads // 2 :], -2)
        if step == 2:
            slot, table = dense_for(wanted[3:5], after(attended, token), True)
            token = slot
    (token, *_) = dense_for(wanted[5:-1], after(attended, chunks[half - 2], chunks[half + 2]))

    factor_t = jnp.swapaxes(factor_in, 1, 2).reshape(low_width, -1)
    second = second_factor.reshape(low_width, complete)
    state = [shape((rows, low_width), F32), shape((complete // side, rows, side), F32)]
    early = [0]
    for distance in range(1, half - 1):
        early += [distance, count - distance]
    late = [half - 1, count - half + 1]
    tables = (slot, factor_t, block_values, block_scale, block_cell, table)
    table_specs = [VMEM, VMEM, VMEM, SMEM, SMEM, SMEM]
    low, blocks = call(
        functools.partial(fold_kernel, early, count, True),
        "fold_early",
        state,
        (*[chunks[d] for d in early], *tables),
        [VMEM] * len(early) + table_specs,
        [VMEM] * 2,
        flops=rows * low_width * complete,
        moved=4 * MIB,
    )
    low, blocks = call(
        functools.partial(fold_kernel, late, count, False),
        "fold_late",
        state,
        (*[chunks[d] for d in late], *tables, low, blocks),
        [VMEM] * len(late) + table_specs + [VMEM] * 2,
        [VMEM] * 2,
        flops=rows * low_width * width * 4,
        moved=MIB,
    )
    low = after(low, token)
    extras = shape((slots * CAP, rows, side), F32)
    first = wanted[:1]
    part_half = shape((heads // 2, rows, side), F32)
    low, extra, front, back, *sums = call(
        functools.partial(finish_kernel, first, count),
        "finish",
        [shape((rows, low_width), BF16), extras]
        + [shape((heads // 2, rows, side), BF16)] * 2
        + [part_half] * (2 * len(first) - 2),
        (front, back, *tables, second, low, blocks, *[dense[d] for d in first]),
        [VMEM] * 2 + table_specs + [VMEM] * (3 + len(first)),
        [VMEM] * (2 + 2 * len(first)),
        [pltpu.VMEM((heads, rows, side), BF16), pltpu.VMEM((rows, low_width), F32),
         pltpu.VMEM((2, heads // 2, rows, side), F32)],
        flops=rows * low_width * width * 8,
        moved=2 * MIB,
    )
    parts = {d: sums[2 * n : 2 * n + 2] for n, d in enumerate(first[1:])}

    def parts_for(distances, low):
        got = call(
            functools.partial(part_kernel, distances, count, slots),
            "part",
            [part_half] * (2 * len(distances)),
            (low, second, blocks, extra, block_scale, block_cell, table,
             *[dense[distance] for distance in distances]),
            [VMEM] * 4 + [SMEM] * 3 + [VMEM] * len(distances),
            [VMEM] * (2 * len(distances)),
            flops=rows * low_width * width * 2,
            moved=MIB,
        )
        parts.update((d, got[2 * n : 2 * n + 2]) for n, d in enumerate(distances))

    def joined(part, came):
        return (part if came is None else part + came.astype(F32)).astype(BF16)

    far, near = (front, back), (None, None)
    for distance in range(half, 0, -1):
        nearer = distance - 1
        if distance < half:
            far = lax.optimization_barrier(
                (joined(parts[count - distance][0], far[0]), joined(parts[distance][1], far[1]))
            )
        if nearer:
            parts_for([nearer, count - nearer], after(low, *far))
        if not nearer:
            dense_for([0], after(attended, *far))
            parts_for([0], after(low, *far))
        far = come(far[0], 1), come(far[1], -1)
        if nearer:
            near = lax.optimization_barrier(
                (joined(parts[count - nearer][1], near[0]), joined(parts[nearer][0], near[1]))
            )
            near = come(near[0], 1), come(near[1], -1)
    came = [far[0], near[0], near[1], far[1]] if half > 1 else [far[0], far[1]]
    return call(
        sum_kernel,
        "sum_up",
        shape((rows, width), BF16),
        (*parts[0], *came),
        [VMEM] * (2 + len(came)),
        VMEM,
        flops=1,
        moved=1,
    )


def solution(mesh):
    return jax.shard_map(
        body,
        mesh=mesh,
        in_specs=(
            P(("groups", "rep"), "tp"),
            P("tp", ("groups", "rep"), None, None),
            P("tp", ("groups", "rep"), None, None),
            P("tp", ("groups", "rep"), None),
            P("tp", ("groups", "rep"), None),
            P(("groups", "rep")),
            P(("groups", "rep")),
            P(),
            P("tp", None),
            P("tp", None, None),
            P("tp", None, None),
            P("tp", None, None, None),
            P("tp", None),
            P("tp", None, None),
            P("tp", None),
        ),
        out_specs=P(("groups", "rep"), "tp"),
        check_vma=False,
    )
```
